32 devices in a mesh: dp: 8 (over z, y), vocab: 4 (over x, core).
Axes of the slice: x: 2, y: 2, z: 4, core: 2. Of those that a mesh axis runs over, the one named last changes fastest.
Arguments:
- source_ids: int32 [64, 128], P('dp'), may hold values from 0 to 25599
- target_in: int32 [64, 128], P('dp'), may hold values from 0 to 25599
- target_ids: int32 [64, 128], P('dp'), may hold values from 0 to 25599
- source_length: int32 [64], P('dp'), may hold values from 16 to 128, as said below
- target_length: int32 [64], P('dp'), may hold values from 16 to 128, as said below
- task_ids: int32 [64], P('dp'), may hold values from 0 to 3, as said below
- vocab_table: bfloat16 [25600, 1024], P('vocab')
- positions: bfloat16 [2, 128, 1024], replicated, may hold values from -0.29882812 to 0.29882812
- attention_in: bfloat16 [3, 1024, 3072], P(None, ('dp', 'vocab')), may hold values from -0.1875 to 0.1875
- attention_out: bfloat16 [3, 1024, 1024], P(None, ('dp', 'vocab')), may hold values from -0.375 to 0.375
- widen_weight: bfloat16 [2, 1024, 4096], P(None, ('dp', 'vocab')), may hold values from -0.1875 to 0.1875
- narrow_weight: bfloat16 [2, 4096, 1024], P(None, ('dp', 'vocab')), may hold values from -0.09375 to 0.09375
- adapt_down: float32 [2, 1024, 512], P(None, ('dp', 'vocab')), may hold values from -0.1875 to 0.1875
- adapt_up: float32 [2, 512, 1024], P(None, ('dp', 'vocab')), may hold values from -0.0625 to 0.0625
- norm_params: float32 [14, 1024], P(None, ('dp', 'vocab'))
- down_first: float32 [2, 1024, 512], P(None, ('dp', 'vocab')), may hold values from -2.3841858e-06 to 2.3841858e-06
- down_second: float32 [2, 1024, 512], P(None, ('dp', 'vocab')), may hold values from 1.8943987e-15 to 7.577595e-15
- up_first: float32 [2, 512, 1024], P(None, ('dp', 'vocab')), may hold values from -2.3841858e-06 to 2.3841858e-06
- up_second: float32 [2, 512, 1024], P(None, ('dp', 'vocab')), may hold values from 1.8943987e-15 to 7.577595e-15
- norm_first: float32 [14, 1024], P(None, ('dp', 'vocab')), may hold values from -4.7683716e-06 to 4.7683716e-06
- norm_second: float32 [14, 1024], P(None, ('dp', 'vocab')), may hold values from 7.577595e-15 to 3.031038e-14
Outputs:
- new_down_first: float32 [2, 1024, 512], P(None, ('dp', 'vocab'))
- new_down_second: float32 [2, 1024, 512], P(None, ('dp', 'vocab'))
- new_adapt_down: float32 [2, 1024, 512], P(None, ('dp', 'vocab'))
- new_up_first: float32 [2, 512, 1024], P(None, ('dp', 'vocab'))
- new_up_second: float32 [2, 512, 1024], P(None, ('dp', 'vocab'))
- new_adapt_up: float32 [2, 512, 1024], P(None, ('dp', 'vocab'))
- new_norm_first: float32 [14, 1024], P(None, ('dp', 'vocab'))
- new_norm_second: float32 [14, 1024], P(None, ('dp', 'vocab'))
- new_norm_params: float32 [14, 1024], P(None, ('dp', 'vocab'))
- clip_norm: float32 [], replicated
- task_sums: float32 [4], replicated
- task_counts: float32 [4], replicated
The draws below stay inside these ranges and needn't reach their ends.
Inputs may be any that keep to these rules, and one draw needn't show every extreme that they name: `source_length`: at least 16; some pair has exactly 128. `target_length`: at least 16; some pair has exactly 128. `task_ids`: every task occurs in some pair.
All inputs are finite; a program needn't handle non-finite values.
Results may differ from the reference program's by a relative error of at most 0.006.
Values may be sent and summed in bfloat16 or wider, within the bound.
A program may use at most 384 MiB of HBM per device.

```python
import math
import jax
import jax.numpy as jnp
import numpy as np
from jax import lax

D = 1024
HEADS = 16
FF = 4096
HEAD_DIM = 64
ADAPT = 512
VOCAB = 25600
LEN = 128
TASKS = 4
STEP = 10
SEQS = 64


def heavy_lengths(key):
    first, second = jax.random.split(key)
    raw = jax.random.randint(first, (SEQS,), 0, 65)
    base = LEN // 8
    lengths = base + (LEN - base) * raw * raw * raw // (64 * 64 * 64)
    spot = jax.random.randint(second, (), 0, SEQS)
    return lengths.at[spot].set(LEN).astype(jnp.int32)


def draw_source_length(key, part):
    key = jax.random.fold_in(key, 1)
    return heavy_lengths(key)


def draw_target_length(key, part):
    key = jax.random.fold_in(key, 2)
    return heavy_lengths(key)


def draw_task_ids(key, part):
    key = jax.random.fold_in(key, 3)
    first, second = jax.random.split(key)
    labels = jax.random.randint(first, (SEQS,), 0, TASKS)
    spots = jax.random.permutation(second, SEQS)[:TASKS]
    return labels.at[spots].set(jnp.arange(TASKS)).astype(jnp.int32)


def draw_vocab_table(key, part):
    key = jax.random.fold_in(key, 4)
    place = jnp.arange(VOCAB, dtype=jnp.float32) / (VOCAB - 1)
    noise = jax.random.normal(key, (VOCAB, D), jnp.float32)
    factor = 1.0 + 2.0 * place
    return (noise * factor[:, None] * D ** (-0.5)).astype(jnp.bfloat16)


def draw_norm_params(key, part):
    key = jax.random.fold_in(key, 5)
    first, second = jax.random.split(key)
    place = jnp.arange(D, dtype=jnp.float32) / (D - 1)
    gains = (0.5 + 1.5 * place)[None, :] * jax.random.uniform(first, (7, D), jnp.float32, 0.8, 1.25)
    biases = 0.2 * jax.random.normal(second, (7, D), jnp.float32)
    return jnp.concatenate([gains, biases], 0)


def set_ends(values, rng, smallest, largest):
    spot = [jax.random.randint(jax.random.fold_in(rng, axis), (), 0, length) for axis, length in enumerate(values.shape)]
    main_axis = values.shape.index(max(values.shape))
    neighbour = spot[:main_axis] + [(spot[main_axis] + 1) % values.shape[main_axis]] + spot[main_axis + 1:]
    return values.at[tuple(spot)].set(smallest).at[tuple(neighbour)].set(largest)


def steps_of(key, extent, shards, least, largest):
    gain, own = 1.0, jax.random.fold_in(key, 6)
    for dim, blocks in shards:
        heights = jnp.exp(jax.random.uniform(jax.random.fold_in(own, dim), (blocks,), jnp.float32, least / len(shards), largest / len(shards)))
        gain = gain * jnp.repeat(heights, extent[dim] // blocks).reshape([-1 if axis == dim else 1 for axis in range(len(extent))])
    return gain


def rank_table(count, slope):
    loads = [(1 << 20) // math.isqrt(rank ** slope) + 1 for rank in range(1, count + 1)]
    spread = 1 + sum(loads) // (1 << 30)
    return np.cumsum(np.array([max(1, weight // spread) for weight in loads]))


def ranked_ids(stream_key, dims, number_of, skew):
    table = rank_table(number_of, skew)
    pick = jax.random.randint(jax.random.fold_in(stream_key, 1), dims, 0, int(table[number_of - 1]))
    rank = jnp.searchsorted(jnp.asarray(table, jnp.int32), pick, side="right")
    return jax.random.permutation(jax.random.fold_in(stream_key, 2), number_of)[rank].astype(jnp.int32)


def normal_values(key, dims, scale, limit, shards=(), kind=jnp.bfloat16):
    values = scale * jax.random.normal(key, dims, jnp.float32)
    if shards:
        values = values * steps_of(key, dims, shards, -0.22, 0.18)
    return jnp.clip(values, -limit, limit).astype(kind)


def setup_inputs(seed: int = 0) -> dict:
    streams_of = jax.random.split(jax.random.key(seed), 22)
    return {
        "source_ids": set_ends(ranked_ids(streams_of[0], (SEQS, LEN), VOCAB, 2), jax.random.fold_in(streams_of[0], 3), 0, VOCAB - 1).astype(jnp.int32),
        "target_in": set_ends(ranked_ids(streams_of[1], (SEQS, LEN), VOCAB, 2), jax.random.fold_in(streams_of[1], 3), 0, VOCAB - 1).astype(jnp.int32),
        "target_ids": set_ends(ranked_ids(streams_of[2], (SEQS, LEN), VOCAB, 2), jax.random.fold_in(streams_of[2], 3), 0, VOCAB - 1).astype(jnp.int32),
        "source_length": draw_source_length(jax.random.fold_in(streams_of[21], 71), 0),
        "target_length": draw_target_length(jax.random.fold_in(streams_of[21], 71), 0),
        "task_ids": draw_task_ids(jax.random.fold_in(streams_of[21], 71), 0),
        "vocab_table": draw_vocab_table(jax.random.fold_in(streams_of[21], 71), 0),
        "positions": normal_values(streams_of[7], (2, LEN, D), 0.05, 0.29882812),
        "attention_in": normal_values(streams_of[8], (3, D, 3 * D), D ** -0.5, 0.1875, ((1, 32),)),
        "attention_out": normal_values(streams_of[9], (3, D, D), (D // 4) ** -0.5, 0.375, ((1, 32),)),
        "widen_weight": normal_values(streams_of[10], (2, D, FF), D ** -0.5, 0.1875, ((1, 32),)),
        "narrow_weight": normal_values(streams_of[11], (2, FF, D), FF ** -0.5, 0.09375, ((1, 32),)),
        "adapt_down": normal_values(streams_of[12], (2, D, ADAPT), D ** -0.5, 0.1875, ((1, 32),), jnp.float32),
        "adapt_up": normal_values(streams_of[13], (2, ADAPT, D), (ADAPT * 16) ** -0.5, 0.0625, ((1, 32),), jnp.float32),
        "norm_params": draw_norm_params(jax.random.fold_in(streams_of[21], 71), 0),
        "down_first": normal_values(streams_of[15], (2, D, ADAPT), (0.00022 * (4 * D * ADAPT + 14 * D) ** -0.5), 2.384185791015625e-06, ((1, 32),), jnp.float32),
        "down_second": jnp.clip(jnp.exp(math.log(7.577594862619597e-15) - 1.3862944 * jax.random.uniform(streams_of[16], (2, D, ADAPT), jnp.float32) ** steps_of(streams_of[16], (2, D, ADAPT), ((1, 32),), -0.2, 0.2)), 1.8943987156548993e-15, 7.577594862619597e-15),
        "up_first": normal_values(streams_of[17], (2, ADAPT, D), (0.00022 * (4 * D * ADAPT + 14 * D) ** -0.5), 2.384185791015625e-06, ((1, 32),), jnp.float32),
        "up_second": jnp.clip(jnp.exp(math.log(7.577594862619597e-15) - 1.3862944 * jax.random.uniform(streams_of[18], (2, ADAPT, D), jnp.float32) ** steps_of(streams_of[18], (2, ADAPT, D), ((1, 32),), -0.2, 0.2)), 1.8943987156548993e-15, 7.577594862619597e-15),
        "norm_first": normal_values(streams_of[19], (14, D), (0.00044 * (4 * D * ADAPT + 14 * D) ** -0.5), 4.76837158203125e-06, ((1, 32),), jnp.float32),
        "norm_second": jnp.clip(jnp.exp(math.log(3.031037945047839e-14) - 1.3862944 * jax.random.uniform(streams_of[20], (14, D), jnp.float32) ** steps_of(streams_of[20], (14, D), ((1, 32),), -0.2, 0.2)), 7.577594862619597e-15, 3.031037945047839e-14),
    }


NEGATIVE = -1000000000.0
NORM_EPS = 1e-05
BRANCH_SCALE = 4.0
CLIP_LIMIT = 0.002
BETA_FIRST = 0.9
BETA_SECOND = 0.999
ADAM_EPSILON = 1e-08
WEIGHT_DECAY = 0.01
RATE_ADAPTER = 0.02
RATE_NORMS = 0.2
HIGHEST = lax.Precision.HIGHEST

@jax.custom_vjp
def low(v):
    return lax.optimization_barrier(v.astype(jnp.bfloat16)).astype(jnp.float32)

@jax.custom_vjp
def low_back(v):
    return v

def low_keep(v):
    return (low(v), None)

def low_pass(kept, grad):
    return (grad,)

def back_keep(v):
    return (v, None)

def back_low(kept, grad):
    return (low(grad),)
low.defvjp(low_keep, low_pass)
low_back.defvjp(back_keep, back_low)

def matmul_high(left, right):
    return jnp.einsum('...d,df->...f', left, right, precision=HIGHEST)

def layer_norm(value, norm_gain, norm_bias):
    centred = value - lax.optimization_barrier(jnp.mean(value, -1, keepdims=True))
    inv_std = lax.rsqrt(lax.optimization_barrier(jnp.mean(centred * centred, -1, keepdims=True)) + NORM_EPS)
    return centred * inv_std * norm_gain + norm_bias

def gelu_value(value):
    return jax.nn.gelu(value, approximate=False)

def attend(queries, key_rows, values, key_mask):
    batch, rows = (queries.shape[0], queries.shape[1])
    heads_q = queries.reshape(batch, rows, HEADS, HEAD_DIM)
    heads_k = key_rows.reshape(batch, -1, HEADS, HEAD_DIM)
    heads_v = values.reshape(batch, -1, HEADS, HEAD_DIM)
    scores = jnp.einsum('bqhd,bkhd->bhqk', heads_q, heads_k, precision=HIGHEST) * HEAD_DIM ** (-0.5)
    scores = low_back(jnp.where(key_mask[:, None], scores, NEGATIVE))
    probs = jax.nn.softmax(scores, axis=-1)
    output = jnp.einsum('bhqk,bkhd->bqhd', low(probs), heads_v, precision=HIGHEST)
    return output.reshape(batch, rows, -1)

def attend_block(inputs, memory, w_in, w_out, norm_gain, norm_bias, key_mask):
    width = inputs.shape[-1]
    low_in = low(inputs)
    if memory is None:
        packed = low(low_back(matmul_high(low_in, w_in)))
        queries, key_rows, values = (packed[..., :width], packed[..., width:2 * width], packed[..., 2 * width:])
    else:
        queries = low(low_back(matmul_high(low_in, w_in[:, :width])))
        pair = low(low_back(matmul_high(memory, w_in[:, width:])))
        key_rows, values = (pair[..., :width], pair[..., width:])
    attended = low(low_back(attend(queries, key_rows, values, key_mask)))
    branch = low_back(matmul_high(attended, w_out))
    return layer_norm(inputs + branch, norm_gain, norm_bias)

def feed_block(inputs, widen, narrow, down_part, up_part, norm_gain, norm_bias):
    low_in = low(inputs)
    hidden = low_back(matmul_high(low_in, widen))
    bottle = low_back(matmul_high(low_in, low(down_part)))
    branch = matmul_high(low(gelu_value(hidden)), narrow) + BRANCH_SCALE * matmul_high(low(gelu_value(bottle)), low(up_part))
    return layer_norm(inputs + low_back(branch), norm_gain, norm_bias)

def group_loss(trainable, frozen, source_ids, target_in, target_ids, source_length, token_weight):
    adapt_down, adapt_up, norm_params = trainable
    vocab_table, positions, attention_in, attention_out, widen_weight, narrow_weight = frozen
    gains, biases = (norm_params[:7], norm_params[7:])
    key_index = jnp.arange(LEN)
    source_mask = jnp.broadcast_to((key_index[None, :] < source_length[:, None])[:, None, :], (source_length.shape[0], LEN, LEN))
    causal = (key_index[:, None] >= key_index[None, :])[None]
    encoded = layer_norm(vocab_table[source_ids] + positions[0], gains[0], biases[0])
    encoded = attend_block(encoded, None, attention_in[0], attention_out[0], gains[1], biases[1], source_mask)
    encoded = feed_block(encoded, widen_weight[0], narrow_weight[0], adapt_down[0], adapt_up[0], gains[2], biases[2])
    memory = low(encoded)
    decoded = layer_norm(vocab_table[target_in] + positions[1], gains[3], biases[3])
    decoded = attend_block(decoded, None, attention_in[1], attention_out[1], gains[4], biases[4], causal)
    decoded = attend_block(decoded, memory, attention_in[2], attention_out[2], gains[5], biases[5], source_mask)
    decoded = feed_block(decoded, widen_weight[1], narrow_weight[1], adapt_down[1], adapt_up[1], gains[6], biases[6])
    logits = low_back(jnp.einsum('bld,vd->blv', low(decoded), vocab_table, precision=HIGHEST))
    log_total = jax.nn.logsumexp(logits, axis=-1)
    target_logit = jnp.take_along_axis(logits, target_ids[..., None], axis=-1)[..., 0]
    row_loss = log_total - target_logit
    return (jnp.sum(token_weight * row_loss), row_loss)

def adam_step(weight, first, second, grad, rate):
    first = BETA_FIRST * first + (1.0 - BETA_FIRST) * grad
    second = BETA_SECOND * second + (1.0 - BETA_SECOND) * grad * grad
    first_hat = first / (1.0 - BETA_FIRST ** STEP)
    second_hat = second / (1.0 - BETA_SECOND ** STEP)
    weight = weight - rate * (first_hat / (jnp.sqrt(second_hat) + ADAM_EPSILON) + WEIGHT_DECAY * weight)
    return (first, second, weight)

def reference(source_ids, target_in, target_ids, source_length, target_length, task_ids, vocab_table, positions, attention_in, attention_out, widen_weight, narrow_weight, adapt_down, adapt_up, norm_params, down_first, down_second, up_first, up_second, norm_first, norm_second):
    frozen = tuple((part.astype(jnp.float32) for part in (vocab_table, positions, attention_in, attention_out, widen_weight, narrow_weight)))
    task_hot = (task_ids[:, None] == jnp.arange(TASKS)[None, :]).astype(jnp.float32)
    task_counts = lax.optimization_barrier(jnp.sum(task_hot * target_length[:, None].astype(jnp.float32), 0))
    seq_scale = lax.optimization_barrier(jnp.sum(task_hot * (1.0 / (TASKS * task_counts))[None, :], 1))
    token_mask = (jnp.arange(LEN)[None, :] < target_length[:, None]).astype(jnp.float32)
    token_weight = token_mask * seq_scale[:, None]
    trainable = (adapt_down, adapt_up, norm_params)
    group_seqs = 8

    def one_group(carry, index):

        def take(array):
            return lax.dynamic_slice_in_dim(array, index * group_seqs, group_seqs, 0)

        def loss_of(train):
            return group_loss(train, frozen, take(source_ids), take(target_in), take(target_ids), take(source_length), take(token_weight))
        loss_value, pull_back, row_loss = jax.vjp(loss_of, trainable, has_aux=True)
        grads = pull_back(jnp.ones_like(loss_value))[0]
        sums = lax.optimization_barrier(jnp.sum(take(task_hot) * lax.optimization_barrier(jnp.sum(row_loss * take(token_mask), 1))[:, None], 0))
        return ((jax.tree.map(jnp.add, carry[0], grads), carry[1] + sums), None)
    start = (jax.tree.map(jnp.zeros_like, trainable), jnp.zeros((TASKS,), jnp.float32))
    (grads, task_sums), _ = lax.scan(one_group, start, jnp.arange(SEQS // group_seqs, dtype=jnp.int32))
    square = jnp.sum(grads[0] * grads[0]) + jnp.sum(grads[1] * grads[1]) + jnp.sum(grads[2] * grads[2])
    grad_norm = jnp.sqrt(square)
    factor = CLIP_LIMIT / jnp.maximum(grad_norm, CLIP_LIMIT)
    down_new = adam_step(adapt_down, down_first, down_second, grads[0] * factor, RATE_ADAPTER)
    up_new = adam_step(adapt_up, up_first, up_second, grads[1] * factor, RATE_ADAPTER)
    norm_new = adam_step(norm_params, norm_first, norm_second, grads[2] * factor, RATE_NORMS)
    return (down_new[0], down_new[1], down_new[2], up_new[0], up_new[1], up_new[2], norm_new[0], norm_new[1], norm_new[2], grad_norm, task_sums, task_counts)
```

```python
import functools

import jax
import jax.numpy as jnp
from jax import lax
from jax.experimental import pallas as pl
from jax.experimental.pallas import tpu as pltpu
from jax.sharding import PartitionSpec as P

HEADS = 16
ADAPT = 512
LEN = 128
MICRO = 2
TASKS = 4
STEP = 10


NEGATIVE = -1000000000.0
NORM_EPS = 1e-05
BRANCH_SCALE = 4.0
CLIP_LIMIT = 0.002
BETA_FIRST = 0.9
BETA_SECOND = 0.999
ADAM_EPSILON = 1e-08
WEIGHT_DECAY = 0.01
RATE_ADAPTER = 0.02
RATE_NORMS = 0.2


def as_low(value):
    return value.astype(jnp.bfloat16)


def times_weight(left, right):
    return jnp.dot(left, right, preferred_element_type=jnp.float32)


def times_transpose(left, right):
    return lax.dot_general(
        left, right, (((1,), (1,)), ((), ())), preferred_element_type=jnp.float32
    )


def outer_sum(left, right):
    return lax.dot_general(
        left, right, (((0,), (0,)), ((), ())), preferred_element_type=jnp.float32
    )


def gelu_value(value):
    return jax.nn.gelu(value, approximate=False)


def gelu_slope(value):
    return (
        0.5 * (1.0 + lax.erf(value * 0.7071067811865476))
        + value * jnp.exp(-0.5 * value * value) * 0.3989422804014327
    )


def norm_forward(value, norm_gain, norm_bias):
    centred = value - jnp.mean(value, -1, keepdims=True)
    inv_std = lax.rsqrt(jnp.mean(centred * centred, -1, keepdims=True) + NORM_EPS)
    normed = centred * inv_std
    return (normed * norm_gain + norm_bias, (normed, inv_std))


def norm_backward(grad_out, kept, norm_gain):
    normed, inv_std = kept
    scaled = grad_out * norm_gain
    grad_in = inv_std * (
        scaled
        - jnp.mean(scaled, -1, keepdims=True)
        - normed * jnp.mean(scaled * normed, -1, keepdims=True)
    )
    return (grad_in, jnp.sum(grad_out * normed, 0), jnp.sum(grad_out, 0))


def split_heads(value):
    return value.reshape(-1, LEN, HEADS, value.shape[1] // HEADS)


def head_scores(queries, key_rows, key_mask):
    scale = (queries.shape[1] // HEADS) ** (-0.5)
    scores = (
        jnp.einsum(
            "bqhd,bkhd->bhqk",
            split_heads(queries),
            split_heads(key_rows),
            preferred_element_type=jnp.float32,
        )
        * scale
    )
    return (jnp.where(key_mask[:, None], scores, NEGATIVE), scale)


def attend_forward(queries, key_rows, values, key_mask):
    scores, scale = head_scores(queries, key_rows, key_mask)
    top = jnp.max(scores, -1, keepdims=True)
    log_total = top + jnp.log(jnp.sum(jnp.exp(scores - top), -1, keepdims=True))
    probs = as_low(jnp.exp(scores - log_total))
    output = jnp.einsum(
        "bhqk,bkhd->bqhd", probs, split_heads(values), preferred_element_type=jnp.float32
    )
    return (output.reshape(queries.shape[0], -1), log_total)


def attend_backward(grad_low, queries, key_rows, values, key_mask, log_total):
    scores, scale = head_scores(queries, key_rows, key_mask)
    probs = jnp.exp(scores - log_total)
    grad_heads = split_heads(grad_low)
    grad_probs = jnp.einsum(
        "bqhd,bkhd->bhqk", grad_heads, split_heads(values), preferred_element_type=jnp.float32
    )
    grad_values = jnp.einsum(
        "bhqk,bqhd->bkhd", as_low(probs), grad_heads, preferred_element_type=jnp.float32
    )
    grad_scores = as_low(probs * (grad_probs - jnp.sum(probs * grad_probs, -1, keepdims=True)))
    grad_queries = (
        jnp.einsum(
            "bhqk,bkhd->bqhd", grad_scores, split_heads(key_rows), preferred_element_type=jnp.float32
        )
        * scale
    )
    grad_keys = (
        jnp.einsum(
            "bhqk,bqhd->bkhd", grad_scores, split_heads(queries), preferred_element_type=jnp.float32
        )
        * scale
    )
    rows_q, rows_k = (queries.shape[0], key_rows.shape[0])
    return (
        grad_queries.reshape(rows_q, -1),
        grad_keys.reshape(rows_k, -1),
        grad_values.reshape(rows_k, -1),
    )


def attend_block(inputs, memory, w_in, w_out, norm_gain, norm_bias, key_mask):
    width = inputs.shape[1]
    low_in = as_low(inputs)
    if memory is None:
        packed = as_low(times_weight(low_in, w_in))
        queries, key_rows, values = (
            packed[:, :width],
            packed[:, width : 2 * width],
            packed[:, 2 * width :],
        )
    else:
        queries = as_low(times_weight(low_in, w_in[:, :width]))
        pair = as_low(times_weight(memory, w_in[:, width:]))
        key_rows, values = (pair[:, :width], pair[:, width:])
    attended, log_total = attend_forward(queries, key_rows, values, key_mask)
    low_att = as_low(attended)
    result, norm_kept = norm_forward(inputs + times_weight(low_att, w_out), norm_gain, norm_bias)
    return (result, (queries, key_rows, values, log_total, norm_kept))


def attend_block_back(grad_out, kept, cross, w_in, w_out, norm_gain, key_mask):
    queries, key_rows, values, log_total, norm_kept = kept
    width = queries.shape[1]
    grad_sum, grad_gain, grad_bias = norm_backward(grad_out, norm_kept, norm_gain)
    grad_att = as_low(times_transpose(as_low(grad_sum), w_out))
    grad_q, grad_k, grad_v = attend_backward(
        grad_att, queries, key_rows, values, key_mask, log_total
    )
    if cross:
        grad_in = grad_sum + times_transpose(as_low(grad_q), w_in[:, :width])
        grad_memory = times_transpose(as_low(jnp.concatenate([grad_k, grad_v], 1)), w_in[:, width:])
    else:
        grad_in = grad_sum + times_transpose(
            as_low(jnp.concatenate([grad_q, grad_k, grad_v], 1)), w_in
        )
        grad_memory = None
    return (grad_in, grad_memory, grad_gain, grad_bias)


def feed_block(inputs, widen, narrow, down_part, up_part, norm_gain, norm_bias):
    low_in = as_low(inputs)
    hidden = times_weight(low_in, widen)
    bottle = times_weight(low_in, down_part)
    low_hidden = as_low(gelu_value(hidden))
    low_bottle = as_low(gelu_value(bottle))
    branch = times_weight(low_hidden, narrow) + BRANCH_SCALE * times_weight(low_bottle, up_part)
    result, norm_kept = norm_forward(inputs + branch, norm_gain, norm_bias)
    return (result, (low_in, hidden, bottle, low_bottle, norm_kept))


def feed_block_back(grad_out, kept, widen, narrow, down_part, up_part, norm_gain):
    low_in, hidden, bottle, low_bottle, norm_kept = kept
    grad_sum, grad_gain, grad_bias = norm_backward(grad_out, norm_kept, norm_gain)
    low_grad = as_low(grad_sum)
    grad_hidden = as_low(times_transpose(low_grad, narrow) * gelu_slope(hidden))
    grad_bottle = as_low(BRANCH_SCALE * times_transpose(low_grad, up_part) * gelu_slope(bottle))
    grad_in = (
        grad_sum + times_transpose(grad_hidden, widen) + times_transpose(grad_bottle, down_part)
    )
    grad_up = BRANCH_SCALE * outer_sum(low_bottle, low_grad)
    grad_down = outer_sum(low_in, grad_bottle)
    return (grad_in, grad_down, grad_up, grad_gain, grad_bias)


def layer_forward(inputs, memory, weights, norms, layer, self_mask, cross_mask):
    attention_in, attention_out, widen, narrow, down_all, up_all = weights
    base = 1 + 3 * layer
    final = base + 1 + layer
    hidden, kept_self = attend_block(
        inputs,
        None,
        attention_in[layer],
        attention_out[layer],
        norms[base],
        norms[base + 7],
        self_mask,
    )
    kept_cross = None
    if memory is not None:
        hidden, kept_cross = attend_block(
            hidden, memory, attention_in[2], attention_out[2], norms[5], norms[12], cross_mask
        )
    result, kept_feed = feed_block(
        hidden,
        widen[layer],
        narrow[layer],
        down_all[layer],
        up_all[layer],
        norms[final],
        norms[final + 7],
    )
    return (result, (kept_self, kept_cross, kept_feed))


def layer_backward(grad_out, kept, weights, norms, layer, self_mask, cross_mask, norm_grads):
    attention_in, attention_out, widen, narrow, down_all, up_all = weights
    kept_self, kept_cross, kept_feed = kept
    base = 1 + 3 * layer
    final = base + 1 + layer
    grad_hidden, grad_down, grad_up, grad_gain, grad_bias = feed_block_back(
        grad_out,
        kept_feed,
        widen[layer],
        narrow[layer],
        down_all[layer],
        up_all[layer],
        norms[final],
    )
    norm_grads = norm_grads.at[final].add(grad_gain).at[final + 7].add(grad_bias)
    grad_memory = None
    if kept_cross is not None:
        grad_hidden, grad_memory, grad_gain, grad_bias = attend_block_back(
            grad_hidden, kept_cross, True, attention_in[2], attention_out[2], norms[5], cross_mask
        )
        norm_grads = norm_grads.at[5].add(grad_gain).at[12].add(grad_bias)
    grad_in, _, grad_gain, grad_bias = attend_block_back(
        grad_hidden,
        kept_self,
        False,
        attention_in[layer],
        attention_out[layer],
        norms[base],
        self_mask,
    )
    norm_grads = norm_grads.at[base].add(grad_gain).at[base + 7].add(grad_bias)
    return (grad_in, grad_memory, grad_down, grad_up, norm_grads)


def adam_step(weight, first, second, grad, rate):
    first = BETA_FIRST * first + (1.0 - BETA_FIRST) * grad
    second = BETA_SECOND * second + (1.0 - BETA_SECOND) * grad * grad
    first_hat = first / (1.0 - BETA_FIRST**STEP)
    second_hat = second / (1.0 - BETA_SECOND**STEP)
    weight = weight - rate * (
        first_hat / (jnp.sqrt(second_hat) + ADAM_EPSILON) + WEIGHT_DECAY * weight
    )
    return (first, second, weight)


MESH_ID = pl.DeviceIdType.MESH
ORDERS = ("xzy", "yzx", "zyx", "xzy", "yzx", "zxy")


def grid_of(dp, vocab):
    cores = 2
    wide = vocab // cores
    high = wide
    return {"z": dp // high, "y": high, "x": wide, "c": cores}


def hops_of(order, sizes):
    return [(axis, hop) for axis in order for hop in range(1, sizes[axis])]


def plan_units(shapes, col_step, sequence):
    units = []
    for name, layer in sequence:
        rows, cols = shapes[name]
        row_step = min(rows, 32)
        if name == "norms":
            units.append((name, None, None, None))
            continue
        for top in range(0, rows, row_step):
            for left in range(0, cols, col_step):
                units.append((name, layer, (top, min(row_step, rows - top)), (left, min(col_step, cols - left))))
    return units


def gather_kernel(sizes, units, names, lags, *refs):
    count = len(names)
    ins = dict(zip(names, refs[:count]))
    outs = dict(zip(names, refs[count : 2 * count]))
    send_sem, recv_sem, local_sem, sib_send, sib_recv = refs[2 * count :]
    dp, vocab = lax.axis_index("dp"), lax.axis_index("vocab")
    here = {
        "z": dp // sizes["y"],
        "y": dp % sizes["y"],
        "x": vocab // sizes["c"],
        "c": vocab % sizes["c"],
    }

    def device(**moved):
        at = dict(here)
        at.update(moved)
        return (at["z"] * sizes["y"] + at["y"], at["x"] * sizes["c"] + at["c"])

    def ends(axis):
        return here[axis] > 0, here[axis] < sizes[axis] - 1

    barrier = pltpu.get_barrier_semaphore()
    axes = [axis for axis in "zyx" if sizes[axis] > 1]
    pl.semaphore_signal(barrier, inc=1, device_id=device(c=1 - here["c"]), device_id_type=MESH_ID)
    peers = jnp.int32(1)
    for axis in axes:
        low, high = ends(axis)
        peers = peers + low.astype(jnp.int32) + high.astype(jnp.int32)
        for ok, step in ((low, -1), (high, 1)):
            @pl.when(ok)
            def _(axis=axis, step=step):
                pl.semaphore_signal(
                    barrier, inc=1, device_id=device(**{axis: here[axis] + step}), device_id_type=MESH_ID
                )
    pl.semaphore_wait(barrier, peers)

    def own_source(unit):
        name, layer, rows, cols = unit
        if name == "norms":
            return ins[name]
        return ins[name].at[layer, pl.ds(*rows), pl.ds(*cols)]

    def piece(unit, z, y, x, c):
        name, layer, rows, cols = unit
        index = (z, y, x, c)
        if name == "norms":
            return outs[name].at[index]
        return outs[name].at[(layer,) + index + (pl.ds(*rows), pl.ds(*cols))]

    everything = slice(None)

    def view(unit, order, axis, coordinate):
        at = {"c": here["c"]}
        place = order.index(axis)
        for other in "zyx":
            position = order.index(other)
            at[other] = everything if position < place else here[other]
        at[axis] = coordinate
        return piece(unit, at["z"], at["y"], at["x"], at["c"])

    def sends(number, stage):
        unit, order = units[number], ORDERS[number % len(ORDERS)]
        axis, hop = hops_of(order, sizes)[stage]
        size, mine = sizes[axis], here[axis]
        first = order.index(axis) == 0
        found = []
        for way, (step, sem) in enumerate(((1, 0), (-1, 1))):
            origin = mine - step * (hop - 1)
            ok = (origin >= 0) & (origin < size) & (mine + step >= 0) & (mine + step < size)
            def build(step=step, sem=sem, origin=origin):
                src = own_source(unit) if first and hop == 1 else view(unit, order, axis, origin)
                return pltpu.make_async_remote_copy(
                    src_ref=src,
                    dst_ref=view(unit, order, axis, origin),
                    send_sem=send_sem.at[number, stage * 2 + sem],
                    recv_sem=recv_sem.at[number, stage * 2 + sem],
                    device_id=device(**{axis: mine + step}),
                    device_id_type=MESH_ID,
                )
            origin_r = mine - step * hop
            ok_r = (origin_r >= 0) & (origin_r < size)
            def build_r(step=step, sem=sem, origin=origin_r):
                return pltpu.make_async_remote_copy(
                    src_ref=view(unit, order, axis, origin),
                    dst_ref=view(unit, order, axis, origin),
                    send_sem=send_sem.at[number, stage * 2 + sem],
                    recv_sem=recv_sem.at[number, stage * 2 + sem],
                    device_id=device(**{axis: mine + step}),
                    device_id_type=MESH_ID,
                )
            found.append((ok, build, ok_r, build_r))
        return found

    def local_copy(number):
        unit = units[number]
        return pltpu.make_async_copy(
            own_source(unit), piece(unit, here["z"], here["y"], here["x"], here["c"]), local_sem.at[number]
        )

    def sibling(number):
        unit = units[number]
        everywhere = piece(unit, everything, everything, everything, here["c"])
        return pltpu.make_async_remote_copy(
            src_ref=everywhere, dst_ref=everywhere,
            send_sem=sib_send.at[number], recv_sem=sib_recv.at[number],
            device_id=device(c=1 - here["c"]), device_id_type=MESH_ID,
        )

    depth = sum(sizes[axis] - 1 for axis in "zyx")
    stages = depth + 2
    events = sorted(
        (number + lags[stage], -stage, number, stage) for number in range(len(units)) for stage in range(stages)
    )
    for _, _, number, stage in events:
        if stage == 0:
            local_copy(number).start()
        if 1 <= stage <= depth:
            for _, _, ok_r, build_r in sends(number, stage - 1):
                @pl.when(ok_r)
                def _(build_r=build_r):
                    build_r().wait_recv()
        order = ORDERS[number % len(ORDERS)]
        if stage == sizes[order[0]] - 1:
            local_copy(number).wait()
        if stage < depth:
            for ok, build, _, _ in sends(number, stage):
                @pl.when(ok)
                def _(build=build):
                    build().start()
        if stage == depth:
            sibling(number).start()
        if stage == depth + 1:
            sibling(number).wait_recv()
    for number in range(len(units)):
        sibling(number).wait_send()
        for stage in range(depth):
            for ok, build, _, _ in sends(number, stage):
                @pl.when(ok)
                def _(build=build):
                    build().wait_send()


def gather_all(arrays, dp, vocab, sequence, col_step=512, lags=None):
    sizes = grid_of(dp, vocab)
    names = list(arrays)
    shapes = {name: arrays[name].shape[-2:] for name in names}
    units = plan_units(shapes, col_step, sequence)
    depth = sum(sizes[axis] - 1 for axis in "zyx")
    if lags is None:
        lags = [2 * stage for stage in range(depth + 2)]
    grid = tuple(sizes[axis] for axis in "zyxc")
    out_shape = []
    for name in names:
        value = arrays[name]
        lead = value.shape[:-2]
        out_shape.append(jax.ShapeDtypeStruct(lead + grid + value.shape[-2:], value.dtype))
    anywhere = pl.BlockSpec(memory_space=pl.ANY)
    n = len(units)
    out = pl.pallas_call(
        functools.partial(gather_kernel, sizes, units, names, lags),
        out_shape=out_shape,
        in_specs=[anywhere] * len(names),
        out_specs=[anywhere] * len(names),
        scratch_shapes=[
            pltpu.SemaphoreType.DMA((n, 2 * depth)),
            pltpu.SemaphoreType.DMA((n, 2 * depth)),
            pltpu.SemaphoreType.DMA((n,)),
            pltpu.SemaphoreType.DMA((n,)),
            pltpu.SemaphoreType.DMA((n,)),
        ],
        compiler_params=pltpu.CompilerParams(collective_id=0, has_side_effects=True),
    )(*[arrays[name] for name in names])
    return dict(zip(names, out))


SEQUENCE = [("norms", None), ("attn_in", 0), ("attn_out", 0), ("down", 0), ("widen", 0), ("up", 0), ("narrow", 0),
            ("attn_in", 1), ("attn_out", 1), ("attn_in", 2), ("attn_out", 2), ("down", 1), ("widen", 1), ("up", 1), ("narrow", 1)]


def local(
    source_ids,
    target_in,
    target_ids,
    source_length,
    target_length,
    task_ids,
    vocab_table,
    positions,
    attention_in,
    attention_out,
    widen_weight,
    narrow_weight,
    adapt_down,
    adapt_up,
    norm_params,
    down_first,
    down_second,
    up_first,
    up_second,
    norm_first,
    norm_second,
):
    groups = lax.axis_size("vocab")
    vocab_rank = lax.axis_index("vocab")
    rows_local = vocab_table.shape[0]
    width = vocab_table.shape[1]
    joined_ids = (
        jnp.stack([source_ids.reshape(groups, -1), target_in.reshape(groups, -1)], 1).reshape(-1)
        - vocab_rank * rows_local
    )
    inside = (joined_ids >= 0) & (joined_ids < rows_local)
    picked = jnp.where(
        inside[:, None],
        jnp.take(vocab_table, jnp.clip(joined_ids, 0, rows_local - 1), axis=0),
        jnp.zeros((), jnp.bfloat16),
    )
    embedded = lax.psum_scatter(
        picked.astype(jnp.float32).astype(jnp.bfloat16), "vocab", scatter_dimension=0, tiled=True
    ).astype(jnp.float32)
    task_hot = (task_ids[:, None] == jnp.arange(TASKS)[None, :]).astype(jnp.float32)
    task_counts = lax.psum(jnp.sum(task_hot * target_length[:, None].astype(jnp.float32), 0), "dp")
    seq_scale = jnp.sum(task_hot * (1.0 / (TASKS * task_counts))[None, :], 1)
    positions_wide = positions.astype(jnp.float32)
    key_index = jnp.arange(LEN)
    causal = key_index[:, None] >= key_index[None, :]
    parts = {
        "norms": norm_params,
        "attn_in": attention_in,
        "attn_out": attention_out,
        "widen": widen_weight,
        "narrow": narrow_weight,
        "down": as_low(adapt_down),
        "up": as_low(adapt_up),
    }
    held = gather_all(parts, lax.axis_size("dp"), groups, SEQUENCE)
    norms = held["norms"].reshape(-1, 14, norm_params.shape[1]).transpose(1, 0, 2).reshape(14, width)
    weights = tuple(
        held[name].reshape(held[name].shape[0], -1, held[name].shape[-1])
        for name in ("attn_in", "attn_out", "widen", "narrow", "down", "up")
    )
    norm_grads = jnp.zeros((14, width), jnp.float32)
    own = vocab_rank * MICRO
    rows = MICRO * LEN
    source_count = lax.dynamic_slice_in_dim(source_length, own, MICRO)
    cross_mask = jnp.broadcast_to(
        key_index[None, None, :] < source_count[:, None, None], (MICRO, LEN, LEN)
    )
    causal = jnp.broadcast_to(causal[None], (MICRO, LEN, LEN))
    source_rows = embedded[:rows] + jnp.tile(positions_wide[0], (MICRO, 1))
    enc_input, kept_enc_norm = norm_forward(source_rows, norms[0], norms[7])
    encoded, kept_enc = layer_forward(enc_input, None, weights, norms, 0, cross_mask, cross_mask)
    memory = as_low(encoded)
    target_rows = embedded[rows:] + jnp.tile(positions_wide[1], (MICRO, 1))
    dec_input, kept_dec_norm = norm_forward(target_rows, norms[3], norms[10])
    decoded, kept_dec = layer_forward(dec_input, memory, weights, norms, 1, causal, cross_mask)
    head_rows = lax.all_gather(as_low(decoded), "vocab", axis=0, tiled=True)
    logits = times_transpose(head_rows, vocab_table)
    local_target = target_ids.reshape(-1) - vocab_rank * rows_local
    target_hot = lax.broadcasted_iota(jnp.int32, logits.shape, 1) == local_target[:, None]
    target_logit = jnp.sum(jnp.where(target_hot, logits, 0.0), 1)
    local_max = jnp.max(logits, 1)
    row_max = lax.pmax(local_max, "vocab")
    row_total, row_target = lax.psum(
        (jnp.sum(jnp.exp(logits - row_max[:, None]), 1), target_logit), "vocab"
    )
    log_total = row_max + jnp.log(row_total)
    row_mask = (key_index[None, :] < target_length[:, None]).astype(jnp.float32)
    row_weight = (row_mask * seq_scale[:, None]).reshape(-1)
    row_loss = (log_total - row_target).reshape(-1, LEN) * row_mask
    own_loss = lax.dynamic_slice_in_dim(row_loss, own, MICRO)
    task_local = jnp.sum(
        lax.dynamic_slice_in_dim(task_hot, own, MICRO) * jnp.sum(own_loss, 1)[:, None], 0
    )
    grad_logits = as_low(
        row_weight[:, None]
        * (jnp.exp(logits - log_total[:, None]) - target_hot.astype(jnp.float32))
    )
    grad_decoded = lax.psum_scatter(
        times_weight(grad_logits, vocab_table).astype(jnp.bfloat16),
        "vocab",
        scatter_dimension=0,
        tiled=True,
    ).astype(jnp.float32)
    grad_dec_in, grad_memory, down_part, up_part, norm_grads = layer_backward(
        grad_decoded, kept_dec, weights, norms, 1, causal, cross_mask, norm_grads
    )
    _, grad_gain, grad_bias = norm_backward(grad_dec_in, kept_dec_norm, norms[3])
    norm_grads = norm_grads.at[3].add(grad_gain).at[10].add(grad_bias)
    everyone = ("dp", "vocab")
    dec_down = lax.psum_scatter(down_part, everyone, scatter_dimension=0, tiled=True)
    dec_up = lax.psum_scatter(up_part, everyone, scatter_dimension=0, tiled=True)
    grad_enc_in, _, down_part, up_part, norm_grads = layer_backward(
        grad_memory, kept_enc, weights, norms, 0, cross_mask, cross_mask, norm_grads
    )
    _, grad_gain, grad_bias = norm_backward(grad_enc_in, kept_enc_norm, norms[0])
    norm_grads = norm_grads.at[0].add(grad_gain).at[7].add(grad_bias)
    enc_down = lax.psum_scatter(down_part, everyone, scatter_dimension=0, tiled=True)
    enc_up = lax.psum_scatter(up_part, everyone, scatter_dimension=0, tiled=True)
    full_norm, task_sums = lax.psum((norm_grads, task_local), everyone)
    shard_down = jnp.stack([enc_down, dec_down])
    shard_up = jnp.stack([enc_up, dec_up])
    square_total = jnp.sum(full_norm * full_norm) + lax.psum(
        jnp.sum(shard_down * shard_down) + jnp.sum(shard_up * shard_up), everyone
    )
    member = lax.axis_index(everyone)
    cut = width // lax.axis_size(everyone)
    shard_norm = lax.dynamic_slice_in_dim(full_norm, member * cut, cut, 1)
    grad_norm = jnp.sqrt(square_total)
    factor = CLIP_LIMIT / jnp.maximum(grad_norm, CLIP_LIMIT)
    down_new = adam_step(adapt_down, down_first, down_second, shard_down * factor, RATE_ADAPTER)
    up_new = adam_step(adapt_up, up_first, up_second, shard_up * factor, RATE_ADAPTER)
    norm_new = adam_step(norm_params, norm_first, norm_second, shard_norm * factor, RATE_NORMS)
    return (
        down_new[0],
        down_new[1],
        down_new[2],
        up_new[0],
        up_new[1],
        up_new[2],
        norm_new[0],
        norm_new[1],
        norm_new[2],
        grad_norm,
        task_sums,
        task_counts,
    )


def solution(mesh):
    return jax.shard_map(
        local,
        mesh=mesh,
        in_specs=(
            P("dp", None),
            P("dp", None),
            P("dp", None),
            P("dp"),
            P("dp"),
            P("dp"),
            P("vocab", None),
            P(),
            P(None, ("dp", "vocab"), None),
            P(None, ("dp", "vocab"), None),
            P(None, ("dp", "vocab"), None),
            P(None, ("dp", "vocab"), None),
            P(None, ("dp", "vocab"), None),
            P(None, ("dp", "vocab"), None),
            P(None, ("dp", "vocab")),
            P(None, ("dp", "vocab"), None),
            P(None, ("dp", "vocab"), None),
            P(None, ("dp", "vocab"), None),
            P(None, ("dp", "vocab"), None),
            P(None, ("dp", "vocab")),
            P(None, ("dp", "vocab")),
        ),
        out_specs=(
            P(None, ("dp", "vocab"), None),
            P(None, ("dp", "vocab"), None),
            P(None, ("dp", "vocab"), None),
            P(None, ("dp", "vocab"), None),
            P(None, ("dp", "vocab"), None),
            P(None, ("dp", "vocab"), None),
            P(None, ("dp", "vocab")),
            P(None, ("dp", "vocab")),
            P(None, ("dp", "vocab")),
            P(),
            P(),
            P(),
        ),
        check_vma=False,
    )
```

```python
import functools

import jax
import jax.numpy as jnp
from jax import lax
from jax.experimental import pallas as pl
from jax.experimental.pallas import tpu as pltpu
from jax.sharding import PartitionSpec as P

HEADS = 16
ADAPT = 512
LEN = 128
MICRO = 2
TASKS = 4
STEP = 10


NEGATIVE = -1000000000.0
NORM_EPS = 1e-05
BRANCH_SCALE = 4.0
CLIP_LIMIT = 0.002
BETA_FIRST = 0.9
BETA_SECOND = 0.999
ADAM_EPSILON = 1e-08
WEIGHT_DECAY = 0.01
RATE_ADAPTER = 0.02
RATE_NORMS = 0.2


def as_low(value):
    return value.astype(jnp.bfloat16)


def times_weight(left, right):
    return jnp.dot(left, right, preferred_element_type=jnp.float32)


def times_transpose(left, right):
    return lax.dot_general(
        left, right, (((1,), (1,)), ((), ())), preferred_element_type=jnp.float32
    )


def outer_sum(left, right):
    return lax.dot_general(
        left, right, (((0,), (0,)), ((), ())), preferred_element_type=jnp.float32
    )


def gelu_value(value):
    return jax.nn.gelu(value, approximate=False)


def gelu_slope(value):
    return (
        0.5 * (1.0 + lax.erf(value * 0.7071067811865476))
        + value * jnp.exp(-0.5 * value * value) * 0.3989422804014327
    )


def norm_forward(value, norm_gain, norm_bias):
    centred = value - jnp.mean(value, -1, keepdims=True)
    inv_std = lax.rsqrt(jnp.mean(centred * centred, -1, keepdims=True) + NORM_EPS)
    normed = centred * inv_std
    return (normed * norm_gain + norm_bias, (normed, inv_std))


def norm_backward(grad_out, kept, norm_gain):
    normed, inv_std = kept
    scaled = grad_out * norm_gain
    grad_in = inv_std * (
        scaled
        - jnp.mean(scaled, -1, keepdims=True)
        - normed * jnp.mean(scaled * normed, -1, keepdims=True)
    )
    return (grad_in, jnp.sum(grad_out * normed, 0), jnp.sum(grad_out, 0))


def split_heads(value):
    return value.reshape(-1, LEN, HEADS, value.shape[1] // HEADS)


def head_scores(queries, key_rows, key_mask):
    scale = (queries.shape[1] // HEADS) ** (-0.5)
    scores = (
        jnp.einsum(
            "bqhd,bkhd->bhqk",
            split_heads(queries),
            split_heads(key_rows),
            preferred_element_type=jnp.float32,
        )
        * scale
    )
    return (jnp.where(key_mask[:, None], scores, NEGATIVE), scale)


def attend_forward(queries, key_rows, values, key_mask):
    scores, scale = head_scores(queries, key_rows, key_mask)
    top = jnp.max(scores, -1, keepdims=True)
    log_total = top + jnp.log(jnp.sum(jnp.exp(scores - top), -1, keepdims=True))
    probs = as_low(jnp.exp(scores - log_total))
    output = jnp.einsum(
        "bhqk,bkhd->bqhd", probs, split_heads(values), preferred_element_type=jnp.float32
    )
    return (output.reshape(queries.shape[0], -1), log_total)


def attend_backward(grad_low, queries, key_rows, values, key_mask, log_total):
    scores, scale = head_scores(queries, key_rows, key_mask)
    probs = jnp.exp(scores - log_total)
    grad_heads = split_heads(grad_low)
    grad_probs = jnp.einsum(
        "bqhd,bkhd->bhqk", grad_heads, split_heads(values), preferred_element_type=jnp.float32
    )
    grad_values = jnp.einsum(
        "bhqk,bqhd->bkhd", as_low(probs), grad_heads, preferred_element_type=jnp.float32
    )
    grad_scores = as_low(probs * (grad_probs - jnp.sum(probs * grad_probs, -1, keepdims=True)))
    grad_queries = (
        jnp.einsum(
            "bhqk,bkhd->bqhd", grad_scores, split_heads(key_rows), preferred_element_type=jnp.float32
        )
        * scale
    )
    grad_keys = (
        jnp.einsum(
            "bhqk,bqhd->bkhd", grad_scores, split_heads(queries), preferred_element_type=jnp.float32
        )
        * scale
    )
    rows_q, rows_k = (queries.shape[0], key_rows.shape[0])
    return (
        grad_queries.reshape(rows_q, -1),
        grad_keys.reshape(rows_k, -1),
        grad_values.reshape(rows_k, -1),
    )


def attend_block(inputs, memory, w_in, w_out, norm_gain, norm_bias, key_mask):
    width = inputs.shape[1]
    low_in = as_low(inputs)
    if memory is None:
        packed = as_low(times_weight(low_in, w_in))
        queries, key_rows, values = (
            packed[:, :width],
            packed[:, width : 2 * width],
            packed[:, 2 * width :],
        )
    else:
        queries = as_low(times_weight(low_in, w_in[:, :width]))
        pair = as_low(times_weight(memory, w_in[:, width:]))
        key_rows, values = (pair[:, :width], pair[:, width:])
    attended, log_total = attend_forward(queries, key_rows, values, key_mask)
    low_att = as_low(attended)
    result, norm_kept = norm_forward(inputs + times_weight(low_att, w_out), norm_gain, norm_bias)
    return (result, (queries, key_rows, values, log_total, norm_kept))


def attend_block_back(grad_out, kept, cross, w_in, w_out, norm_gain, key_mask):
    queries, key_rows, values, log_total, norm_kept = kept
    width = queries.shape[1]
    grad_sum, grad_gain, grad_bias = norm_backward(grad_out, norm_kept, norm_gain)
    grad_att = as_low(times_transpose(as_low(grad_sum), w_out))
    grad_q, grad_k, grad_v = attend_backward(
        grad_att, queries, key_rows, values, key_mask, log_total
    )
    if cross:
        grad_in = grad_sum + times_transpose(as_low(grad_q), w_in[:, :width])
        grad_memory = times_transpose(as_low(jnp.concatenate([grad_k, grad_v], 1)), w_in[:, width:])
    else:
        grad_in = grad_sum + times_transpose(
            as_low(jnp.concatenate([grad_q, grad_k, grad_v], 1)), w_in
        )
        grad_memory = None
    return (grad_in, grad_memory, grad_gain, grad_bias)


def feed_block(inputs, widen, narrow, down_part, up_part, norm_gain, norm_bias):
    low_in = as_low(inputs)
    hidden = times_weight(low_in, widen)
    bottle = times_weight(low_in, down_part)
    low_hidden = as_low(gelu_value(hidden))
    low_bottle = as_low(gelu_value(bottle))
    branch = times_weight(low_hidden, narrow) + BRANCH_SCALE * times_weight(low_bottle, up_part)
    result, norm_kept = norm_forward(inputs + branch, norm_gain, norm_bias)
    return (result, (low_in, hidden, bottle, low_bottle, norm_kept))


def feed_block_back(grad_out, kept, widen, narrow, down_part, up_part, norm_gain):
    low_in, hidden, bottle, low_bottle, norm_kept = kept
    grad_sum, grad_gain, grad_bias = norm_backward(grad_out, norm_kept, norm_gain)
    low_grad = as_low(grad_sum)
    grad_hidden = as_low(times_transpose(low_grad, narrow) * gelu_slope(hidden))
    grad_bottle = as_low(BRANCH_SCALE * times_transpose(low_grad, up_part) * gelu_slope(bottle))
    grad_in = (
        grad_sum + times_transpose(grad_hidden, widen) + times_transpose(grad_bottle, down_part)
    )
    grad_up = BRANCH_SCALE * outer_sum(low_bottle, low_grad)
    grad_down = outer_sum(low_in, grad_bottle)
    return (grad_in, grad_down, grad_up, grad_gain, grad_bias)


def layer_forward(inputs, memory, weights, norms, layer, self_mask, cross_mask):
    attention_in, attention_out, widen, narrow, down_all, up_all = weights
    base = 1 + 3 * layer
    final = base + 1 + layer
    hidden, kept_self = attend_block(
        inputs,
        None,
        attention_in[layer],
        attention_out[layer],
        norms[base],
        norms[base + 7],
        self_mask,
    )
    kept_cross = None
    if memory is not None:
        hidden, kept_cross = attend_block(
            hidden, memory, attention_in[2], attention_out[2], norms[5], norms[12], cross_mask
        )
    result, kept_feed = feed_block(
        hidden,
        widen[layer],
        narrow[layer],
        down_all[layer],
        up_all[layer],
        norms[final],
        norms[final + 7],
    )
    return (result, (kept_self, kept_cross, kept_feed))


def layer_backward(grad_out, kept, weights, norms, layer, self_mask, cross_mask, norm_grads):
    attention_in, attention_out, widen, narrow, down_all, up_all = weights
    kept_self, kept_cross, kept_feed = kept
    base = 1 + 3 * layer
    final = base + 1 + layer
    grad_hidden, grad_down, grad_up, grad_gain, grad_bias = feed_block_back(
        grad_out,
        kept_feed,
        widen[layer],
        narrow[layer],
        down_all[layer],
        up_all[layer],
        norms[final],
    )
    norm_grads = norm_grads.at[final].add(grad_gain).at[final + 7].add(grad_bias)
    grad_memory = None
    if kept_cross is not None:
        grad_hidden, grad_memory, grad_gain, grad_bias = attend_block_back(
            grad_hidden, kept_cross, True, attention_in[2], attention_out[2], norms[5], cross_mask
        )
        norm_grads = norm_grads.at[5].add(grad_gain).at[12].add(grad_bias)
    grad_in, _, grad_gain, grad_bias = attend_block_back(
        grad_hidden,
        kept_self,
        False,
        attention_in[layer],
        attention_out[layer],
        norms[base],
        self_mask,
    )
    norm_grads = norm_grads.at[base].add(grad_gain).at[base + 7].add(grad_bias)
    return (grad_in, grad_memory, grad_down, grad_up, norm_grads)


def adam_step(weight, first, second, grad, rate):
    first = BETA_FIRST * first + (1.0 - BETA_FIRST) * grad
    second = BETA_SECOND * second + (1.0 - BETA_SECOND) * grad * grad
    first_hat = first / (1.0 - BETA_FIRST**STEP)
    second_hat = second / (1.0 - BETA_SECOND**STEP)
    weight = weight - rate * (
        first_hat / (jnp.sqrt(second_hat) + ADAM_EPSILON) + WEIGHT_DECAY * weight
    )
    return (first, second, weight)


MESH_ID = pl.DeviceIdType.MESH
ORDERS = ("xzy", "yzx", "zyx", "xzy", "yzx", "zxy")


def grid_of(dp, vocab):
    cores = 2
    wide = vocab // cores
    high = wide
    return {"z": dp // high, "y": high, "x": wide, "c": cores}


def hops_of(order, sizes):
    return [(axis, hop) for axis in order for hop in range(1, sizes[axis])]


def plan_units(shapes, col_step, sequence):
    units = []
    for name, layer in sequence:
        rows, cols = shapes[name]
        row_step = min(rows, 32)
        if name == "norms":
            units.append((name, None, None, None))
            continue
        for top in range(0, rows, row_step):
            for left in range(0, cols, col_step):
                units.append((name, layer, (top, min(row_step, rows - top)), (left, min(col_step, cols - left))))
    return units


def gather_kernel(sizes, units, names, lags, *refs):
    count = len(names)
    ins = dict(zip(names, refs[:count]))
    outs = dict(zip(names, refs[count : 2 * count]))
    send_sem, recv_sem, local_sem, sib_send, sib_recv = refs[2 * count :]
    dp, vocab = lax.axis_index("dp"), lax.axis_index("vocab")
    here = {
        "z": dp // sizes["y"],
        "y": dp % sizes["y"],
        "x": vocab // sizes["c"],
        "c": vocab % sizes["c"],
    }

    def device(**moved):
        at = dict(here)
        at.update(moved)
        return (at["z"] * sizes["y"] + at["y"], at["x"] * sizes["c"] + at["c"])

    def ends(axis):
        return here[axis] > 0, here[axis] < sizes[axis] - 1

    barrier = pltpu.get_barrier_semaphore()
    axes = [axis for axis in "zyx" if sizes[axis] > 1]
    pl.semaphore_signal(barrier, inc=1, device_id=device(c=1 - here["c"]), device_id_type=MESH_ID)
    peers = jnp.int32(1)
    for axis in axes:
        low, high = ends(axis)
        peers = peers + low.astype(jnp.int32) + high.astype(jnp.int32)
        for ok, step in ((low, -1), (high, 1)):
            @pl.when(ok)
            def _(axis=axis, step=step):
                pl.semaphore_signal(
                    barrier, inc=1, device_id=device(**{axis: here[axis] + step}), device_id_type=MESH_ID
                )
    pl.semaphore_wait(barrier, peers)

    def own_source(unit):
        name, layer, rows, cols = unit
        if name == "norms":
            return ins[name]
        return ins[name].at[layer, pl.ds(*rows), pl.ds(*cols)]

    def piece(unit, z, y, x, c):
        name, layer, rows, cols = unit
        index = (z, y, x, c)
        if name == "norms":
            return outs[name].at[index]
        return outs[name].at[(layer,) + index + (pl.ds(*rows), pl.ds(*cols))]

    everything = slice(None)

    def view(unit, order, axis, coordinate):
        at = {"c": here["c"]}
        place = order.index(axis)
        for other in "zyx":
            position = order.index(other)
            at[other] = everything if position < place else here[other]
        at[axis] = coordinate
        return piece(unit, at["z"], at["y"], at["x"], at["c"])

    def sends(number, stage):
        unit, order = units[number], ORDERS[number % len(ORDERS)]
        axis, hop = hops_of(order, sizes)[stage]
        size, mine = sizes[axis], here[axis]
        first = order.index(axis) == 0
        found = []
        for way, (step, sem) in enumerate(((1, 0), (-1, 1))):
            origin = mine - step * (hop - 1)
            ok = (origin >= 0) & (origin < size) & (mine + step >= 0) & (mine + step < size)
            def build(step=step, sem=sem, origin=origin):
                src = own_source(unit) if first and hop == 1 else view(unit, order, axis, origin)
                return pltpu.make_async_remote_copy(
                    src_ref=src,
                    dst_ref=view(unit, order, axis, origin),
                    send_sem=send_sem.at[number, stage * 2 + sem],
                    recv_sem=recv_sem.at[number, stage * 2 + sem],
                    device_id=device(**{axis: mine + step}),
                    device_id_type=MESH_ID,
                )
            origin_r = mine - step * hop
            ok_r = (origin_r >= 0) & (origin_r < size)
            def build_r(step=step, sem=sem, origin=origin_r):
                return pltpu.make_async_remote_copy(
                    src_ref=view(unit, order, axis, origin),
                    dst_ref=view(unit, order, axis, origin),
                    send_sem=send_sem.at[number, stage * 2 + sem],
                    recv_sem=recv_sem.at[number, stage * 2 + sem],
                    device_id=device(**{axis: mine + step}),
                    device_id_type=MESH_ID,
                )
            found.append((ok, build, ok_r, build_r))
        return found

    def local_copy(number):
        unit = units[number]
        return pltpu.make_async_copy(
            own_source(unit), piece(unit, here["z"], here["y"], here["x"], here["c"]), local_sem.at[number]
        )

    def sibling(number):
        unit = units[number]
        everywhere = piece(unit, everything, everything, everything, here["c"])
        return pltpu.make_async_remote_copy(
            src_ref=everywhere, dst_ref=everywhere,
            send_sem=sib_send.at[number], recv_sem=sib_recv.at[number],
            device_id=device(c=1 - here["c"]), device_id_type=MESH_ID,
        )

    depth = sum(sizes[axis] - 1 for axis in "zyx")
    stages = depth + 2
    events = sorted(
        (number + lags[stage], -stage, number, stage) for number in range(len(units)) for stage in range(stages)
    )
    for _, _, number, stage in events:
        if stage == 0:
            local_copy(number).start()
        if 1 <= stage <= depth:
            for _, _, ok_r, build_r in sends(number, stage - 1):
                @pl.when(ok_r)
                def _(build_r=build_r):
                    build_r().wait_recv()
        order = ORDERS[number % len(ORDERS)]
        if stage == sizes[order[0]] - 1:
            local_copy(number).wait()
        if stage < depth:
            for ok, build, _, _ in sends(number, stage):
                @pl.when(ok)
                def _(build=build):
                    build().start()
        if stage == depth:
            sibling(number).start()
        if stage == depth + 1:
            sibling(number).wait_recv()
    for number in range(len(units)):
        sibling(number).wait_send()
        for stage in range(depth):
            for ok, build, _, _ in sends(number, stage):
                @pl.when(ok)
                def _(build=build):
                    build().wait_send()


def gather_all(arrays, dp, vocab, sequence, col_step=512, lags=None):
    sizes = grid_of(dp, vocab)
    names = list(arrays)
    shapes = {name: arrays[name].shape[-2:] for name in names}
    units = plan_units(shapes, col_step, sequence)
    depth = sum(sizes[axis] - 1 for axis in "zyx")
    if lags is None:
        lags = [2 * stage for stage in range(depth + 2)]
    grid = tuple(sizes[axis] for axis in "zyxc")
    out_shape = []
    for name in names:
        value = arrays[name]
        lead = value.shape[:-2]
        out_shape.append(jax.ShapeDtypeStruct(lead + grid + value.shape[-2:], value.dtype))
    anywhere = pl.BlockSpec(memory_space=pl.ANY)
    n = len(units)
    out = pl.pallas_call(
        functools.partial(gather_kernel, sizes, units, names, lags),
        out_shape=out_shape,
        in_specs=[anywhere] * len(names),
        out_specs=[anywhere] * len(names),
        scratch_shapes=[
            pltpu.SemaphoreType.DMA((n, 2 * depth)),
            pltpu.SemaphoreType.DMA((n, 2 * depth)),
            pltpu.SemaphoreType.DMA((n,)),
            pltpu.SemaphoreType.DMA((n,)),
            pltpu.SemaphoreType.DMA((n,)),
        ],
        compiler_params=pltpu.CompilerParams(collective_id=0, has_side_effects=True),
    )(*[arrays[name] for name in names])
    return dict(zip(names, out))


SEQUENCE = [("norms", None), ("attn_in", 0), ("attn_out", 0), ("down", 0), ("widen", 0), ("up", 0), ("narrow", 0),
            ("attn_in", 1), ("attn_out", 1), ("attn_in", 2), ("attn_out", 2), ("down", 1), ("widen", 1), ("up", 1), ("narrow", 1)]


def position(sizes):
    dp, vocab = lax.axis_index("dp"), lax.axis_index("vocab")
    return {
        "z": dp // sizes["y"],
        "y": dp % sizes["y"],
        "x": vocab // sizes["c"],
        "c": vocab % sizes["c"],
    }


def device_at(here, sizes, **moved):
    at = dict(here)
    at.update(moved)
    return (at["z"] * sizes["y"] + at["y"], at["x"] * sizes["c"] + at["c"])


def lines_barrier(here, sizes):
    barrier = pltpu.get_barrier_semaphore()
    peers = 0
    for axis in "zyxc":
        for step in range(1, sizes[axis]):
            other = (here[axis] + step) % sizes[axis]
            pl.semaphore_signal(
                barrier, inc=1, device_id=device_at(here, sizes, **{axis: other}), device_id_type=MESH_ID
            )
            peers += 1
    pl.semaphore_wait(barrier, peers)


def reduce_kernel(sizes, *refs):
    grads = refs[0:4]
    small = refs[4]
    shards = refs[5:9]
    small_out, square_out = refs[9:11]
    sums, core_send, core_recv = refs[11:15], refs[15:19], refs[19:23]
    wide_send, wide_recv, mid_send, mid_recv, last_send, last_recv = (
        refs[23:27], refs[27:31], refs[31:35], refs[35:39], refs[39:43], refs[43:47]
    )
    small_slots, square_slots = refs[47:51], refs[51:55]
    send_sem, recv_sem = refs[55:57]
    here = position(sizes)
    lines_barrier(here, sizes)
    used = [0]
    started = []

    def copy_to(src, dst, **moved):
        number = used[0]
        used[0] += 1
        copy = pltpu.make_async_remote_copy(
            src_ref=src,
            dst_ref=dst,
            send_sem=send_sem.at[number],
            recv_sem=recv_sem.at[number],
            device_id=device_at(here, sizes, **moved),
            device_id_type=MESH_ID,
        )
        copy.start()
        started.append(copy)
        return copy

    def low(value):
        return value.astype(jnp.bfloat16)

    mine = here["c"]

    def share(slots, value, axis):
        slots[here[axis]] = value
        return [
            copy_to(slots.at[here[axis]], slots.at[here[axis]], **{axis: (here[axis] + step) % sizes[axis]})
            for step in range(1, sizes[axis])
        ]

    def total(slots, axis, copies):
        for copy in copies:
            copy.wait_recv()
        value = slots[0]
        for index in range(1, sizes[axis]):
            value = value + slots[index]
        return value

    first = []
    for part in range(4):
        core_send[part][...] = low(grads[part][:, :, :, 1 - mine])
        first.append(copy_to(core_send[part], core_recv[part], c=1 - mine))
    copies = share(small_slots[0], small[...], "c")
    plans = (("x", "y"), ("x", "y"), ("y", "x"), ("y", "x"))

    second = []
    for part in range(4):
        first[part].wait_recv()
        sums[part][...] = grads[part][:, :, :, mine] + core_recv[part][...].astype(jnp.float32)
        axis = plans[part][0]
        found = []
        for step in range(1, sizes[axis]):
            other = (here[axis] + step) % sizes[axis]
            piece = sums[part][:, :, other] if axis == "x" else sums[part][:, other]
            wide_send[part][step - 1] = low(piece)
            found.append(copy_to(wide_send[part].at[step - 1], wide_recv[part].at[step - 1], **{axis: other}))
        second.append(found)
    copies = share(small_slots[1], total(small_slots[0], "c", copies), "x")
    third = []
    for part in range(4):
        axis, later = plans[part]
        held = sums[part].at[:, :, here["x"]] if axis == "x" else sums[part].at[:, here["y"]]
        value = held[...]
        for step, copy in enumerate(second[part]):
            copy.wait_recv()
            value = value + wide_recv[part][step].astype(jnp.float32)
        held[...] = value
        found = []
        for step in range(1, sizes[later]):
            other = (here[later] + step) % sizes[later]
            mid_send[part][step - 1] = low(held[:, other])
            found.append(copy_to(mid_send[part].at[step - 1], mid_recv[part].at[step - 1], **{later: other}))
        third.append(found)
    copies = share(small_slots[2], total(small_slots[1], "x", copies), "y")
    fourth = []
    for part in range(4):
        axis, later = plans[part]
        held = sums[part].at[:, here["y"], here["x"]]
        value = held[...]
        for step, copy in enumerate(third[part]):
            copy.wait_recv()
            value = value + mid_recv[part][step].astype(jnp.float32)
        held[...] = value
        found = []
        for step in range(1, sizes["z"]):
            other = (here["z"] + step) % sizes["z"]
            last_send[part][step - 1] = low(held[other])
            found.append(copy_to(last_send[part].at[step - 1], last_recv[part].at[step - 1], z=other))
        fourth.append(found)
    copies = share(small_slots[3], total(small_slots[2], "y", copies), "z")
    square = jnp.zeros((1, 1), jnp.float32)
    for part in range(4):
        value = sums[part][here["z"], here["y"], here["x"]]
        for step, copy in enumerate(fourth[part]):
            copy.wait_recv()
            value = value + last_recv[part][step].astype(jnp.float32)
        shards[part][...] = value
        square = square + jnp.sum(value * value, keepdims=True)
    square = jnp.broadcast_to(square, (8, 128))
    for place, axis in enumerate("cxyz"):
        parts = share(square_slots[place], square, axis)
        if place == 0:
            whole = total(small_slots[3], "z", copies)
            small_out[...] = whole
            norm_square = jnp.sum(whole[:14] * whole[:14], keepdims=True)
        square = total(square_slots[place], axis, parts)
    square_out[...] = square + norm_square
    for copy in started:
        copy.wait_send()


def reduce_gradients(down_enc, up_enc, down_dec, up_dec, small, dp, vocab):
    sizes = grid_of(dp, vocab)
    grid = tuple(sizes[axis] for axis in "zyxc")
    whole = dp * vocab
    grads = [
        value.reshape(grid + (value.shape[0] // whole, value.shape[1]))
        for value in (down_enc, up_enc, down_dec, up_dec)
    ]
    z, y, x, c = grid
    tails = [value.shape[4:] for value in grads]
    vmem = pl.BlockSpec(memory_space=pltpu.VMEM)
    scratch = [pltpu.VMEM((z, y, x) + tail, jnp.float32) for tail in tails]
    for _ in range(2):
        scratch += [pltpu.VMEM((z, y, x) + tail, jnp.bfloat16) for tail in tails]
    for _ in range(2):
        scratch += [
            pltpu.VMEM(((x - 1, z, y) if place < 2 else (y - 1, z, x)) + tail, jnp.bfloat16)
            for place, tail in enumerate(tails)
        ]
    for _ in range(2):
        scratch += [
            pltpu.VMEM(((y - 1, z) if place < 2 else (x - 1, z)) + tail, jnp.bfloat16)
            for place, tail in enumerate(tails)
        ]
    for _ in range(2):
        scratch += [pltpu.VMEM((z - 1,) + tail, jnp.bfloat16) for tail in tails]
    scratch += [pltpu.VMEM((sizes[axis],) + small.shape, jnp.float32) for axis in "cxyz"]
    scratch += [pltpu.VMEM((sizes[axis], 8, 128), jnp.float32) for axis in "cxyz"]
    links = 6 * (x + y + z + c)
    scratch += [pltpu.SemaphoreType.DMA((links,)), pltpu.SemaphoreType.DMA((links,))]
    return pl.pallas_call(
        functools.partial(reduce_kernel, sizes),
        out_shape=[jax.ShapeDtypeStruct(tail, jnp.float32) for tail in tails]
        + [jax.ShapeDtypeStruct(small.shape, jnp.float32), jax.ShapeDtypeStruct((8, 128), jnp.float32)],
        in_specs=[vmem] * 5,
        out_specs=[vmem] * 6,
        scratch_shapes=scratch,
        compiler_params=pltpu.CompilerParams(
            collective_id=1, has_side_effects=True, vmem_limit_bytes=48 * 2**20
        ),
    )(*grads, small)


def local(
    source_ids,
    target_in,
    target_ids,
    source_length,
    target_length,
    task_ids,
    vocab_table,
    positions,
    attention_in,
    attention_out,
    widen_weight,
    narrow_weight,
    adapt_down,
    adapt_up,
    norm_params,
    down_first,
    down_second,
    up_first,
    up_second,
    norm_first,
    norm_second,
):
    groups = lax.axis_size("vocab")
    vocab_rank = lax.axis_index("vocab")
    rows_local = vocab_table.shape[0]
    width = vocab_table.shape[1]
    joined_ids = (
        jnp.stack([source_ids.reshape(groups, -1), target_in.reshape(groups, -1)], 1).reshape(-1)
        - vocab_rank * rows_local
    )
    inside = (joined_ids >= 0) & (joined_ids < rows_local)
    picked = jnp.where(
        inside[:, None],
        jnp.take(vocab_table, jnp.clip(joined_ids, 0, rows_local - 1), axis=0),
        jnp.zeros((), jnp.bfloat16),
    )
    embedded = lax.psum_scatter(
        picked.astype(jnp.float32).astype(jnp.bfloat16), "vocab", scatter_dimension=0, tiled=True
    ).astype(jnp.float32)
    task_hot = (task_ids[:, None] == jnp.arange(TASKS)[None, :]).astype(jnp.float32)
    task_counts = lax.psum(jnp.sum(task_hot * target_length[:, None].astype(jnp.float32), 0), "dp")
    seq_scale = jnp.sum(task_hot * (1.0 / (TASKS * task_counts))[None, :], 1)
    positions_wide = positions.astype(jnp.float32)
    key_index = jnp.arange(LEN)
    causal = key_index[:, None] >= key_index[None, :]
    parts = {
        "norms": norm_params,
        "attn_in": attention_in,
        "attn_out": attention_out,
        "widen": widen_weight,
        "narrow": narrow_weight,
        "down": as_low(adapt_down),
        "up": as_low(adapt_up),
    }
    held = gather_all(parts, lax.axis_size("dp"), groups, SEQUENCE)
    norms = held["norms"].reshape(-1, 14, norm_params.shape[1]).transpose(1, 0, 2).reshape(14, width)
    weights = tuple(
        held[name].reshape(held[name].shape[0], -1, held[name].shape[-1])
        for name in ("attn_in", "attn_out", "widen", "narrow", "down", "up")
    )
    norm_grads = jnp.zeros((14, width), jnp.float32)
    own = vocab_rank * MICRO
    rows = MICRO * LEN
    source_count = lax.dynamic_slice_in_dim(source_length, own, MICRO)
    cross_mask = jnp.broadcast_to(
        key_index[None, None, :] < source_count[:, None, None], (MICRO, LEN, LEN)
    )
    causal = jnp.broadcast_to(causal[None], (MICRO, LEN, LEN))
    source_rows = embedded[:rows] + jnp.tile(positions_wide[0], (MICRO, 1))
    enc_input, kept_enc_norm = norm_forward(source_rows, norms[0], norms[7])
    encoded, kept_enc = layer_forward(enc_input, None, weights, norms, 0, cross_mask, cross_mask)
    memory = as_low(encoded)
    target_rows = embedded[rows:] + jnp.tile(positions_wide[1], (MICRO, 1))
    dec_input, kept_dec_norm = norm_forward(target_rows, norms[3], norms[10])
    decoded, kept_dec = layer_forward(dec_input, memory, weights, norms, 1, causal, cross_mask)
    head_rows = lax.all_gather(as_low(decoded), "vocab", axis=0, tiled=True)
    logits = times_transpose(head_rows, vocab_table)
    local_target = target_ids.reshape(-1) - vocab_rank * rows_local
    target_hot = lax.broadcasted_iota(jnp.int32, logits.shape, 1) == local_target[:, None]
    target_logit = jnp.sum(jnp.where(target_hot, logits, 0.0), 1)
    local_max = jnp.max(logits, 1)
    row_max = lax.pmax(local_max, "vocab")
    row_total, row_target = lax.psum(
        (jnp.sum(jnp.exp(logits - row_max[:, None]), 1), target_logit), "vocab"
    )
    log_total = row_max + jnp.log(row_total)
    row_mask = (key_index[None, :] < target_length[:, None]).astype(jnp.float32)
    row_weight = (row_mask * seq_scale[:, None]).reshape(-1)
    row_loss = (log_total - row_target).reshape(-1, LEN) * row_mask
    own_loss = lax.dynamic_slice_in_dim(row_loss, own, MICRO)
    task_local = jnp.sum(
        lax.dynamic_slice_in_dim(task_hot, own, MICRO) * jnp.sum(own_loss, 1)[:, None], 0
    )
    grad_logits = as_low(
        row_weight[:, None]
        * (jnp.exp(logits - log_total[:, None]) - target_hot.astype(jnp.float32))
    )
    grad_decoded = lax.psum_scatter(
        times_weight(grad_logits, vocab_table).astype(jnp.bfloat16),
        "vocab",
        scatter_dimension=0,
        tiled=True,
    ).astype(jnp.float32)
    grad_dec_in, grad_memory, down_part, up_part, norm_grads = layer_backward(
        grad_decoded, kept_dec, weights, norms, 1, causal, cross_mask, norm_grads
    )
    _, grad_gain, grad_bias = norm_backward(grad_dec_in, kept_dec_norm, norms[3])
    norm_grads = norm_grads.at[3].add(grad_gain).at[10].add(grad_bias)
    grad_enc_in, _, down_first_part, up_first_part, norm_grads = layer_backward(
        grad_memory, kept_enc, weights, norms, 0, cross_mask, cross_mask, norm_grads
    )
    _, grad_gain, grad_bias = norm_backward(grad_enc_in, kept_enc_norm, norms[0])
    norm_grads = norm_grads.at[0].add(grad_gain).at[7].add(grad_bias)
    small = jnp.concatenate(
        [norm_grads, jnp.zeros((1, width), jnp.float32).at[0, :TASKS].set(task_local), jnp.zeros((1, width), jnp.float32)], 0
    )
    enc_down, enc_up, dec_down, dec_up, small, square = reduce_gradients(
        down_first_part, up_first_part, down_part, up_part, small, lax.axis_size("dp"), groups
    )
    shard_down = jnp.stack([enc_down, dec_down])
    shard_up = jnp.stack([enc_up, dec_up])
    full_norm, task_sums = small[:14], small[14, :TASKS]
    square_total = square[0, 0]
    everyone = ("dp", "vocab")
    member = lax.axis_index(everyone)
    cut = width // lax.axis_size(everyone)
    shard_norm = lax.dynamic_slice_in_dim(full_norm, member * cut, cut, 1)
    grad_norm = jnp.sqrt(square_total)
    factor = CLIP_LIMIT / jnp.maximum(grad_norm, CLIP_LIMIT)
    down_new = adam_step(adapt_down, down_first, down_second, shard_down * factor, RATE_ADAPTER)
    up_new = adam_step(adapt_up, up_first, up_second, shard_up * factor, RATE_ADAPTER)
    norm_new = adam_step(norm_params, norm_first, norm_second, shard_norm * factor, RATE_NORMS)
    return (
        down_new[0],
        down_new[1],
        down_new[2],
        up_new[0],
        up_new[1],
        up_new[2],
        norm_new[0],
        norm_new[1],
        norm_new[2],
        grad_norm,
        task_sums,
        task_counts,
    )


def solution(mesh):
    return jax.shard_map(
        local,
        mesh=mesh,
        in_specs=(
            P("dp", None),
            P("dp", None),
            P("dp", None),
            P("dp"),
            P("dp"),
            P("dp"),
            P("vocab", None),
            P(),
            P(None, ("dp", "vocab"), None),
            P(None, ("dp", "vocab"), None),
            P(None, ("dp", "vocab"), None),
            P(None, ("dp", "vocab"), None),
            P(None, ("dp", "vocab"), None),
            P(None, ("dp", "vocab"), None),
            P(None, ("dp", "vocab")),
            P(None, ("dp", "vocab"), None),
            P(None, ("dp", "vocab"), None),
            P(None, ("dp", "vocab"), None),
            P(None, ("dp", "vocab"), None),
            P(None, ("dp", "vocab")),
            P(None, ("dp", "vocab")),
        ),
        out_specs=(
            P(None, ("dp", "vocab"), None),
            P(None, ("dp", "vocab"), None),
            P(None, ("dp", "vocab"), None),
            P(None, ("dp", "vocab"), None),
            P(None, ("dp", "vocab"), None),
            P(None, ("dp", "vocab"), None),
            P(None, ("dp", "vocab")),
            P(None, ("dp", "vocab")),
            P(None, ("dp", "vocab")),
            P(),
            P(),
            P(),
        ),
        check_vma=False,
    )
```

```python
import functools

import jax
import jax.numpy as jnp
from jax import lax
from jax.experimental import pallas as pl
from jax.experimental.pallas import tpu as pltpu
from jax.sharding import PartitionSpec as P

MESH_ID = pl.DeviceIdType.MESH
TASKS = 4
STEP = 10
CLIP_LIMIT = 0.002
BETA_FIRST = 0.9
BETA_SECOND = 0.999
ADAM_EPSILON = 1e-08
WEIGHT_DECAY = 0.01
RATE_ADAPTER = 0.02
RATE_NORMS = 0.2


def grid_of(dp, vocab):
    cores = 2
    across = vocab // cores
    return {"z": dp // across, "y": across, "x": across, "c": cores}


def position(sizes):
    dp, vocab = lax.axis_index("dp"), lax.axis_index("vocab")
    return {
        "z": dp // sizes["y"],
        "y": dp % sizes["y"],
        "x": vocab // sizes["c"],
        "c": vocab % sizes["c"],
    }


def device_at(here, sizes, **moved):
    at = dict(here)
    at.update(moved)
    return (at["z"] * sizes["y"] + at["y"], at["x"] * sizes["c"] + at["c"])


def lines_barrier(here, sizes):
    barrier = pltpu.get_barrier_semaphore()
    peers = 0
    for axis in "zyxc":
        for step in range(1, sizes[axis]):
            other = (here[axis] + step) % sizes[axis]
            pl.semaphore_signal(
                barrier, inc=1, device_id=device_at(here, sizes, **{axis: other}), device_id_type=MESH_ID
            )
            peers += 1
    pl.semaphore_wait(barrier, peers)


def reduce_kernel(sizes, *refs):
    grads = refs[0:4]
    small = refs[4]
    shards = refs[5:9]
    small_out, square_out = refs[9:11]
    sums, core_send, core_recv = refs[11:15], refs[15:19], refs[19:23]
    wide_send, wide_recv, mid_send, mid_recv, last_send, last_recv = (
        refs[23:27], refs[27:31], refs[31:35], refs[35:39], refs[39:43], refs[43:47]
    )
    small_slots, square_slots = refs[47:51], refs[51:55]
    send_sem, recv_sem = refs[55:57]
    here = position(sizes)
    lines_barrier(here, sizes)
    used = [0]
    started = []

    def copy_to(src, dst, **moved):
        number = used[0]
        used[0] += 1
        copy = pltpu.make_async_remote_copy(
            src_ref=src,
            dst_ref=dst,
            send_sem=send_sem.at[number],
            recv_sem=recv_sem.at[number],
            device_id=device_at(here, sizes, **moved),
            device_id_type=MESH_ID,
        )
        copy.start()
        started.append(copy)
        return copy

    def low(value):
        return value.astype(jnp.bfloat16)

    mine = here["c"]

    def share(slots, value, axis):
        slots[here[axis]] = value
        return [
            copy_to(slots.at[here[axis]], slots.at[here[axis]], **{axis: (here[axis] + step) % sizes[axis]})
            for step in range(1, sizes[axis])
        ]

    def total(slots, axis, copies):
        for copy in copies:
            copy.wait_recv()
        value = slots[0]
        for index in range(1, sizes[axis]):
            value = value + slots[index]
        return value

    first = []
    for part in range(4):
        core_send[part][...] = low(grads[part][:, :, :, 1 - mine])
        first.append(copy_to(core_send[part], core_recv[part], c=1 - mine))
    copies = share(small_slots[0], small[...], "c")
    plans = (("x", "y"), ("x", "y"), ("y", "x"), ("y", "x"))

    second = []
    for part in range(4):
        first[part].wait_recv()
        sums[part][...] = grads[part][:, :, :, mine] + core_recv[part][...].astype(jnp.float32)
        axis = plans[part][0]
        found = []
        for step in range(1, sizes[axis]):
            other = (here[axis] + step) % sizes[axis]
            piece = sums[part][:, :, other] if axis == "x" else sums[part][:, other]
            wide_send[part][step - 1] = low(piece)
            found.append(copy_to(wide_send[part].at[step - 1], wide_recv[part].at[step - 1], **{axis: other}))
        second.append(found)
    copies = share(small_slots[1], total(small_slots[0], "c", copies), "x")
    third = []
    for part in range(4):
        axis, later = plans[part]
        held = sums[part].at[:, :, here["x"]] if axis == "x" else sums[part].at[:, here["y"]]
        value = held[...]
        for step, copy in enumerate(second[part]):
            copy.wait_recv()
            value = value + wide_recv[part][step].astype(jnp.float32)
        held[...] = value
        found = []
        for step in range(1, sizes[later]):
            other = (here[later] + step) % sizes[later]
            mid_send[part][step - 1] = low(held[:, other])
            found.append(copy_to(mid_send[part].at[step - 1], mid_recv[part].at[step - 1], **{later: other}))
        third.append(found)
    copies = share(small_slots[2], total(small_slots[1], "x", copies), "y")
    fourth = []
    for part in range(4):
        axis, later = plans[part]
        held = sums[part].at[:, here["y"], here["x"]]
        value = held[...]
        for step, copy in enumerate(third[part]):
            copy.wait_recv()
            value = value + mid_recv[part][step].astype(jnp.float32)
        held[...] = value
        found = []
        for step in range(1, sizes["z"]):
            other = (here["z"] + step) % sizes["z"]
            last_send[part][step - 1] = low(held[other])
            found.append(copy_to(last_send[part].at[step - 1], last_recv[part].at[step - 1], z=other))
        fourth.append(found)
    copies = share(small_slots[3], total(small_slots[2], "y", copies), "z")
    square = jnp.zeros((1, 1), jnp.float32)
    for part in range(4):
        value = sums[part][here["z"], here["y"], here["x"]]
        for step, copy in enumerate(fourth[part]):
            copy.wait_recv()
            value = value + last_recv[part][step].astype(jnp.float32)
        shards[part][...] = value
        square = square + jnp.sum(value * value, keepdims=True)
    square = jnp.broadcast_to(square, (8, 128))
    for place, axis in enumerate("cxyz"):
        parts = share(square_slots[place], square, axis)
        if place == 0:
            whole = total(small_slots[3], "z", copies)
            small_out[...] = whole
            norm_square = jnp.sum(whole[:14] * whole[:14], keepdims=True)
        square = total(square_slots[place], axis, parts)
    square_out[...] = square + norm_square
    for copy in started:
        copy.wait_send()


def reduce_gradients(down_enc, up_enc, down_dec, up_dec, small, dp, vocab):
    sizes = grid_of(dp, vocab)
    grid = tuple(sizes[axis] for axis in "zyxc")
    whole = dp * vocab
    grads = [
        value.reshape(grid + (value.shape[0] // whole, value.shape[1]))
        for value in (down_enc, up_enc, down_dec, up_dec)
    ]
    z, y, x, c = grid
    tails = [value.shape[4:] for value in grads]
    vmem = pl.BlockSpec(memory_space=pltpu.VMEM)
    scratch = [pltpu.VMEM((z, y, x) + tail, jnp.float32) for tail in tails]
    for _ in range(2):
        scratch += [pltpu.VMEM((z, y, x) + tail, jnp.bfloat16) for tail in tails]
    for _ in range(2):
        scratch += [
            pltpu.VMEM(((x - 1, z, y) if place < 2 else (y - 1, z, x)) + tail, jnp.bfloat16)
            for place, tail in enumerate(tails)
        ]
    for _ in range(2):
        scratch += [
            pltpu.VMEM(((y - 1, z) if place < 2 else (x - 1, z)) + tail, jnp.bfloat16)
            for place, tail in enumerate(tails)
        ]
    for _ in range(2):
        scratch += [pltpu.VMEM((z - 1,) + tail, jnp.bfloat16) for tail in tails]
    scratch += [pltpu.VMEM((sizes[axis],) + small.shape, jnp.float32) for axis in "cxyz"]
    scratch += [pltpu.VMEM((sizes[axis], 8, 128), jnp.float32) for axis in "cxyz"]
    links = 6 * (x + y + z + c)
    scratch += [pltpu.SemaphoreType.DMA((links,)), pltpu.SemaphoreType.DMA((links,))]
    return pl.pallas_call(
        functools.partial(reduce_kernel, sizes),
        out_shape=[jax.ShapeDtypeStruct(tail, jnp.float32) for tail in tails]
        + [jax.ShapeDtypeStruct(small.shape, jnp.float32), jax.ShapeDtypeStruct((8, 128), jnp.float32)],
        in_specs=[vmem] * 5,
        out_specs=[vmem] * 6,
        scratch_shapes=scratch,
        compiler_params=pltpu.CompilerParams(
            collective_id=1, has_side_effects=True, vmem_limit_bytes=48 * 2**20
        ),
    )(*grads, small)


ORDERS = ("xzy", "yzx", "zyx", "xzy", "yzx", "zxy")
SEQUENCE = (
    ("norms", 0), ("attn_in", 0), ("attn_out", 0), ("down", 0), ("widen", 0), ("up", 0), ("narrow", 0),
    ("attn_in", 1), ("attn_out", 1), ("attn_in", 2), ("attn_out", 2), ("down", 1), ("widen", 1), ("up", 1),
    ("narrow", 1),
)
COLUMNS = {"norms": 128, "attn_in": 512, "attn_out": 512, "down": 512, "widen": 512, "up": 512, "narrow": 256}
LAG = 3.0
PACE = 0.7
HEADS = 16
LEN = 128
MICRO = 2
ROWS = 256
NORM_EPS = 1e-05
NEGATIVE = -1000000000.0
BRANCH_SCALE = 4.0


def hops_of(order, sizes):
    return [(axis, hop) for axis in order for hop in range(1, sizes[axis])]


def plan_units(shapes, names, devices):
    units, clock = [], 0.0
    for name, layer in SEQUENCE:
        if name not in names:
            continue
        rows, columns = shapes[name]
        step = min(COLUMNS[name], columns)
        for left in range(0, columns, step):
            units.append((name, layer, left, step, clock))
            clock += rows * devices * step / 2**19
    return units


def dot(left, right):
    return jnp.dot(left, right, preferred_element_type=jnp.float32)


def dot_rows(left, right):
    return lax.dot_general(left, right, (((1,), (1,)), ((), ())), preferred_element_type=jnp.float32)


def dot_columns(left, right):
    return lax.dot_general(left, right, (((0,), (0,)), ((), ())), preferred_element_type=jnp.float32)


def low(value):
    return value.astype(jnp.bfloat16)


def wide(value):
    return value.astype(jnp.float32)


def norm_rows(value, gain, bias):
    centred = value - jnp.mean(value, -1, keepdims=True)
    inv_std = lax.rsqrt(jnp.mean(centred * centred, -1, keepdims=True) + NORM_EPS)
    normed = centred * inv_std
    return normed * gain + bias, normed, inv_std


def gelu_pair(value):
    half = 0.5 * (1.0 + lax.erf(value * 0.7071067811865476))
    return value * half, half + value * jnp.exp(-0.5 * value * value) * 0.3989422804014327


def lane_masks():
    lanes = lax.broadcasted_iota(jnp.int32, (LEN, 128), 1)
    first = (lanes < 64).astype(jnp.float32).astype(jnp.bfloat16)
    return first, (lanes >= 64).astype(jnp.float32).astype(jnp.bfloat16)


def stack_heads(value, masks):
    return jnp.concatenate([value * masks[0], value * masks[1]], 0)


def attend_pair(qkv, probs, attended, seq, pair, keep):
    masks = lane_masks()
    rows = pl.ds(pl.multiple_of(seq * LEN, LEN), LEN)

    def columns(part):
        return pl.ds(pl.multiple_of(part * 1024 + pair * 128, 128), 128)

    queries, keys, values = (qkv[rows, columns(part)] for part in range(3))
    scores = dot_rows(stack_heads(queries, masks), keys) * 0.125
    scores = jnp.where(keep(seq), scores, NEGATIVE)
    spread = jnp.exp(scores - jnp.max(scores, -1, keepdims=True))
    chance = low(spread / jnp.sum(spread, -1, keepdims=True))
    probs[seq, pair] = chance
    side = jnp.concatenate([chance[:LEN], chance[LEN:]], 1)
    attended[rows, columns(0)] = low(dot(side, stack_heads(values, masks)))


def forward_kernel(sizes, units, names, *refs):
    refs = list(refs)

    def take(count):
        found = refs[:count]
        del refs[:count]
        return found

    count = len(names)
    ins = dict(zip(names, take(count)))
    picked, places, key_keep = take(3)
    extra_up = None if "up" in names else take(1)[0]
    outs = dict(zip(names, take(count)))
    saved_out = take(8)
    send_sem, recv_sem, local_sem, sib_send, sib_recv = take(5)
    saved = take(8)
    qkv_all, probs_all, normed_all, inv_all, feed_in, slopes, bottles, decoded = saved
    embed_sem, embed_here, embed_core, embed_line = take(4)
    norm_tile, norms = take(2)
    stream, stream_low, memory, attended, branch, hidden = take(6)
    tiles, tall_tiles, tile_sem, tall_sem, save_sem = take(5)
    here = position(sizes)

    def at_device(**moved):
        return device_at(here, sizes, **moved)

    barrier = pltpu.get_barrier_semaphore()
    pl.semaphore_signal(barrier, inc=1, device_id=at_device(c=1 - here["c"]), device_id_type=MESH_ID)
    peers = jnp.int32(1)
    for step in range(1, sizes["x"]):
        other = (here["x"] + step) % sizes["x"]
        pl.semaphore_signal(barrier, inc=1, device_id=at_device(x=other), device_id_type=MESH_ID)
        peers = peers + 1
    for axis in "zy":
        for step in (-1, 1):
            ok = (here[axis] + step >= 0) & (here[axis] + step < sizes[axis])
            peers = peers + ok.astype(jnp.int32)

            @pl.when(ok)
            def _(axis=axis, step=step):
                pl.semaphore_signal(
                    barrier, inc=1, device_id=at_device(**{axis: here[axis] + step}), device_id_type=MESH_ID
                )

    pl.semaphore_wait(barrier, peers)

    everything = slice(None)

    def own_source(unit):
        name, layer, left, width, _ = unit
        return ins[name].at[layer, :, pl.ds(left, width)]

    def piece(unit, index):
        name, layer, left, width, _ = unit
        return outs[name].at[(layer,) + index + (everything, pl.ds(left, width))]

    def view(unit, order, axis, coordinate):
        place = order.index(axis)
        at = {other: everything if order.index(other) < place else here[other] for other in "zyx"}
        at[axis] = coordinate
        return piece(unit, (at["z"], at["y"], at["x"], here["c"]))

    def sends(number, stage):
        unit, order = units[number], ORDERS[number % len(ORDERS)]
        axis, hop = hops_of(order, sizes)[stage]
        size, mine = sizes[axis], here[axis]
        first = order.index(axis) == 0
        found = []
        for way, step in enumerate((1, -1)):
            origin = mine - step * (hop - 1)
            ok = (origin >= 0) & (origin < size) & (mine + step >= 0) & (mine + step < size)
            origin_r = mine - step * hop
            ok_r = (origin_r >= 0) & (origin_r < size)

            def build(receive, step=step, way=way, origin=origin, origin_r=origin_r):
                which = origin_r if receive else origin
                fresh = first and hop == 1 and not receive
                return pltpu.make_async_remote_copy(
                    src_ref=own_source(unit) if fresh else view(unit, order, axis, which),
                    dst_ref=view(unit, order, axis, which),
                    send_sem=send_sem.at[number, stage * 2 + way],
                    recv_sem=recv_sem.at[number, stage * 2 + way],
                    device_id=at_device(**{axis: mine + step}),
                    device_id_type=MESH_ID,
                )

            found.append((ok, ok_r, build))
        return found

    def local_copy(number):
        index = tuple(here[axis] for axis in "zyxc")
        return pltpu.make_async_copy(own_source(units[number]), piece(units[number], index), local_sem.at[number])

    def sibling(number):
        plane = piece(units[number], (everything, everything, everything, here["c"]))
        return pltpu.make_async_remote_copy(
            src_ref=plane,
            dst_ref=plane,
            send_sem=sib_send.at[number],
            recv_sem=sib_recv.at[number],
            device_id=at_device(c=1 - here["c"]),
            device_id_type=MESH_ID,
        )

    depth = sum(sizes[axis] - 1 for axis in "zyx")

    def comm_step(number, stage):
        if stage == 0:
            local_copy(number).start()
        if 1 <= stage <= depth:
            for _, ok_r, build in sends(number, stage - 1):

                @pl.when(ok_r)
                def _(build=build):
                    build(True).wait_recv()

        if stage == sizes[ORDERS[number % len(ORDERS)][0]] - 1:
            local_copy(number).wait()
        if stage < depth:
            for ok, _, build in sends(number, stage):

                @pl.when(ok)
                def _(build=build):
                    build(False).start()

        if stage == depth:
            sibling(number).start()
        if stage == depth + 1:
            sibling(number).wait_recv()

    mine, column = here["c"], here["x"]

    def embed_first(group):
        return pltpu.make_async_remote_copy(
            src_ref=picked.at[:, 1 - mine, group],
            dst_ref=embed_core.at[group],
            send_sem=embed_sem.at[0, group],
            recv_sem=embed_sem.at[1, group],
            device_id=at_device(c=1 - mine),
            device_id_type=MESH_ID,
        )

    def embed_local(group):
        return pltpu.make_async_copy(picked.at[:, mine, group], embed_here.at[group], embed_sem.at[2, group])

    def embed_second(group, step):
        other = (column + step) % sizes["x"]
        return pltpu.make_async_remote_copy(
            src_ref=embed_here.at[group, other],
            dst_ref=embed_line.at[group, step - 1],
            send_sem=embed_sem.at[2 + step * 2 - 1, group],
            recv_sem=embed_sem.at[2 + step * 2, group],
            device_id=at_device(x=other),
            device_id_type=MESH_ID,
        )

    def embed_pass(group):
        embed_first(group).wait_recv()
        embed_local(group).wait()
        embed_here[group] = embed_here[group] + embed_core[group]
        for step in range(1, sizes["x"]):
            embed_second(group, step).start()

    def embed_rows(group):
        rows = wide(embed_here[group, column])
        for step in range(1, sizes["x"]):
            embed_second(group, step).wait_recv()
            rows = rows + wide(embed_line[group, step - 1])
        place = wide(places[group])
        return rows + jnp.concatenate([place] * MICRO, 0)

    saves = []

    def save(place, index):
        def build(number=len(saves)):
            return pltpu.make_async_copy(
                saved[place].at[index] if index else saved[place],
                saved_out[place].at[index] if index else saved_out[place],
                save_sem.at[number],
            )

        saves.append(build)
        build().start()

    def norm_step(value, which, side):
        result, normed, inv_std = norm_rows(value, norms[which : which + 1, :], norms[which + 7 : which + 8, :])
        normed_all[which] = normed
        inv_all[which] = jnp.broadcast_to(inv_std, (ROWS, 128))
        save(2, (which,))
        save(3, (which,))
        stream[side] = result
        stream_low[side] = low(result)

    def begin(side):
        def run():
            if side == 0:
                copy = pltpu.make_async_copy(outs["norms"].at[0], norm_tile, tile_sem.at[len(tiles_used)])
                copy.start()
                copy.wait()
                columns = norm_tile[...].reshape(-1, 128)
                norms[...] = columns.T[:16]
            norm_step(embed_rows(side), 3 * side, side)

        return run

    tiles_used = [None] * tiles.shape[0]

    def project(which, left, side, from_memory):
        def run(tile):
            source = memory[...] if from_memory else stream_low[side]
            qkv_all[which, :, pl.ds(left, 512)] = low(dot(source, tile()))

        return run

    def attention(which, start, keep):
        def run():
            def body(number, _):
                seq, pair = number // 8, number % 8
                attend_pair(qkv_all.at[which], probs_all.at[which], attended, seq, pair, keep)
                return 0

            lax.fori_loop(start, start + 4, body, 0)

        return run

    def project_out(left):
        def run(tile):
            branch[:, pl.ds(left, 512)] = dot(attended[...], tile())

        return run

    def finish_attention(which, norm, side):
        def run():
            save(0, (which,))
            save(1, (which,))
            norm_step(stream[side] + branch[...], norm, side)

        return run

    def narrow_down(side):
        def run(tile):
            feed_in[side] = stream_low[side]
            value, slope = gelu_pair(dot(stream_low[side], tile()))
            bottles[side, 0] = low(value)
            bottles[side, 1] = low(slope)
            save(4, (side,))
            save(6, (side,))

        return run

    def widen(left, side):
        def run(tile):
            value, slope = gelu_pair(dot(stream_low[side], tile()))
            hidden[:, pl.ds(left, 512)] = low(value)
            slopes[side, :, pl.ds(left, 512)] = low(slope)

        return run

    def raise_up(left, side):
        def run(tile):
            branch[:, pl.ds(left, 512)] = BRANCH_SCALE * dot(bottles[side, 0], tile())

        return run

    def narrow(left, side):
        def run(tile):
            branch[:, pl.ds(left, 256)] += dot(hidden[...], tile())

        return run

    def finish_feed(norm, side):
        def run():
            save(5, (side,))
            norm_step(stream[side] + branch[...], norm, side)
            if side == 0:
                memory[...] = stream_low[0]
            else:
                decoded[...] = stream_low[1]
                save(7, ())

        return run

    def source_keep(seq):
        return jnp.broadcast_to(key_keep[seq, 0:1, :] > 0.0, (2 * LEN, LEN))

    def causal_keep(seq):
        query = lax.broadcasted_iota(jnp.int32, (2 * LEN, LEN), 0) % LEN
        return lax.broadcasted_iota(jnp.int32, (2 * LEN, LEN), 1) <= query

    steps = []
    unit_of = {}
    for number, unit in enumerate(units):
        unit_of[unit[:3]] = number

    def add(run, cost, unit=None, clock=0.0):
        steps.append((unit, cost, clock, run))

    def attention_steps(which, norm, side, keep):
        for left in range(0, 3072, 512):
            from_memory = which == 2 and left >= 1024
            add(project(which, left, side, from_memory), 0.6, unit_of["attn_in", which, left])
        for start in range(0, 16, 4):
            add(attention(which, start, keep), 2.0)
        for left in range(0, 1024, 512):
            add(project_out(left), 0.6, unit_of["attn_out", which, left])
        add(finish_attention(which, norm, side), 1.0)

    def feed_steps(norm, side):
        add(narrow_down(side), 1.3, unit_of["down", side, 0])
        for left in range(0, 4096, 512):
            add(widen(left, side), 1.3, unit_of["widen", side, left])
        for left in range(0, 1024, 512):
            if "up" in names:
                add(raise_up(left, side), 0.4, unit_of["up", side, left])
            else:
                part = functools.partial(lambda left, side: extra_up[side, :, pl.ds(left, 512)], left, side)
                add(functools.partial(raise_up(left, side), part), 0.4)
        for left in range(0, 1024, 256):
            add(narrow(left, side), 1.0, unit_of["narrow", side, left])
        add(finish_feed(norm, side), 1.0)

    add(begin(0), 2.0, unit_of["norms", 0, 0], 8.0)
    attention_steps(0, 1, 0, source_keep)
    feed_steps(2, 0)
    add(begin(1), 1.5, None, 20.0)
    attention_steps(1, 4, 1, causal_keep)
    attention_steps(2, 5, 1, source_keep)
    feed_steps(6, 1)

    loads = [step[0] for step in steps if isinstance(step[0], int) and units[step[0]][0] != "norms"]
    slot_of, rings = {}, {"tall": [], "flat": []}
    for unit in loads:
        kind = "tall" if units[unit][0] == "narrow" else "flat"
        ring = rings[kind]
        size = (tall_tiles if kind == "tall" else tiles).shape[0]
        slot_of[unit] = (kind, len(ring) % size, ring[len(ring) - size] if len(ring) >= size else None)
        ring.append(unit)

    def tile_parts(unit):
        kind, slot, _ = slot_of[unit]
        name, layer, left, width, _ = units[unit]
        source = outs[name].at[layer, :, :, :, :, :, pl.ds(left, width)]
        buffer = (tall_tiles if kind == "tall" else tiles).at[slot]
        sem = (tall_sem if kind == "tall" else tile_sem).at[slot]
        rows = ins[name].shape[1] * sizes["z"] * sizes["y"] * sizes["x"] * sizes["c"]
        target = buffer.at[pl.ds(0, rows)]
        shape = tuple(sizes[axis] for axis in "zyxc") + (ins[name].shape[1], width)
        return pltpu.make_async_copy(source, target.reshape(shape), sem), target

    complete, loaded, done = set(), set(), set()
    waiting = list(loads)

    def try_loads():
        while waiting:
            unit = waiting[0]
            before = slot_of[unit][2]
            if unit not in complete or (before is not None and before not in done):
                return
            tile_parts(unit)[0].start()
            loaded.add(unit)
            waiting.pop(0)

    queue = list(steps)

    def run_step():
        unit, cost, _, run = queue.pop(0)
        if unit is None or units[unit][0] == "norms":
            run()
        else:
            copy, target = tile_parts(unit)
            copy.wait()
            run(lambda: target[...])
            done.add(unit)
        try_loads()
        return cost

    def ready(clock):
        if not queue:
            return False
        unit, _, earliest, _ = queue[0]
        if earliest > clock:
            return False
        if unit is None:
            return True
        return unit in complete if units[unit][0] == "norms" else unit in loaded

    for group in range(2):
        embed_first(group).start()
        embed_local(group).start()
    events = sorted(
        (unit[4] + LAG * stage, -stage, number) for number, unit in enumerate(units) for stage in range(depth + 2)
    )
    embed_done, credit, last = [], 0.0, 0.0
    for clock, minus, number in events:
        stage = -minus
        comm_step(number, stage)
        for group in range(2):
            if group not in embed_done and clock >= 1.5 + 1.5 * group:
                embed_done.append(group)
                embed_pass(group)
        if stage == depth + 1:
            complete.add(number)
            try_loads()
        credit = min(credit + 3.7 * PACE * (clock - last) , 4.0)
        last = clock
        while ready(clock) and credit > 0.0:
            credit -= run_step()
    while queue:
        run_step()
    for build in saves:
        build().wait()
    for group in range(2):
        embed_first(group).wait_send()
        for step in range(1, sizes["x"]):
            embed_second(group, step).wait_send()
    for number in range(len(units)):
        sibling(number).wait_send()
        for stage in range(depth):
            for ok, _, build in sends(number, stage):

                @pl.when(ok)
                def _(build=build):
                    build(False).wait_send()


def run_forward(arrays, picked, places, key_keep, dp, vocab):
    sizes = grid_of(dp, vocab)
    devices = dp * vocab
    grid = tuple(sizes[axis] for axis in "zyxc")
    extra = []
    arrays = dict(arrays)
    if arrays["up"].shape[1] % 8:
        extra = [lax.all_gather(arrays.pop("up"), ("dp", "vocab"), axis=1, tiled=True)]
    names = list(arrays)
    shapes = {name: arrays[name].shape[1:] for name in names}
    units = plan_units(shapes, names, devices)
    depth = sum(sizes[axis] - 1 for axis in "zyx")
    anywhere, vmem = pl.BlockSpec(memory_space=pl.ANY), pl.BlockSpec(memory_space=pltpu.VMEM)
    f32, b16 = jnp.float32, jnp.bfloat16
    saved = [
        ((3, ROWS, 3072), b16),
        ((3, MICRO, 8, 2 * LEN, LEN), b16),
        ((7, ROWS, 1024), f32),
        ((7, ROWS, 128), f32),
        ((2, ROWS, 1024), b16),
        ((2, ROWS, 4096), b16),
        ((2, 2, ROWS, 512), b16),
        ((ROWS, 1024), b16),
    ]
    out_shape = [
        jax.ShapeDtypeStruct((arrays[name].shape[0],) + grid + arrays[name].shape[1:], arrays[name].dtype)
        for name in names
    ] + [jax.ShapeDtypeStruct(shape, kind) for shape, kind in saved]
    x, n = sizes["x"], len(units)
    dma = pltpu.SemaphoreType.DMA
    out = pl.pallas_call(
        functools.partial(forward_kernel, sizes, units, names),
        out_shape=out_shape,
        in_specs=[anywhere] * (len(names) + 1) + [vmem] * (2 + len(extra)),
        out_specs=[anywhere] * len(out_shape),
        scratch_shapes=[dma((n, 2 * depth)), dma((n, 2 * depth)), dma((n,)), dma((n,)), dma((n,))]
        + [pltpu.VMEM(shape, kind) for shape, kind in saved]
        + [
            dma((3 + 2 * x, 2)),
            pltpu.VMEM((2, x, ROWS, 1024), b16),
            pltpu.VMEM((2, x, ROWS, 1024), b16),
            pltpu.VMEM((2, x - 1, ROWS, 1024), b16),
            pltpu.VMEM(grid + arrays["norms"].shape[1:], f32),
            pltpu.VMEM((16, 1024), f32),
            pltpu.VMEM((2, ROWS, 1024), f32),
            pltpu.VMEM((2, ROWS, 1024), b16),
            pltpu.VMEM((ROWS, 1024), b16),
            pltpu.VMEM((ROWS, 1024), b16),
            pltpu.VMEM((ROWS, 1024), f32),
            pltpu.VMEM((ROWS, 4096), b16),
            pltpu.VMEM((4, 1024, 512), b16),
            pltpu.VMEM((2, 4096, 256), b16),
            dma((5,)),
            dma((2,)),
            dma((32,)),
        ],
        compiler_params=pltpu.CompilerParams(
            collective_id=0, has_side_effects=True, vmem_limit_bytes=61 * 2**20
        ),
    )(*[arrays[name] for name in names], picked, places, key_keep, *extra)
    held = dict(zip(names, out[: len(names)]))
    held = {name: value.reshape(value.shape[0], -1, value.shape[-1]) for name, value in held.items()}
    if extra:
        held["up"] = extra[0]
    return held, out[len(names) :]


def attend_back(grad_low, queries, key_rows, values, probs, scale):
    grad_heads = split_heads(grad_low)
    grad_probs = jnp.einsum(
        "bqhd,bkhd->bhqk", grad_heads, split_heads(values), preferred_element_type=jnp.float32
    )
    grad_values = jnp.einsum("bhqk,bqhd->bkhd", probs, grad_heads, preferred_element_type=jnp.float32)
    probs = wide(probs)
    grad_scores = low(probs * (grad_probs - jnp.sum(probs * grad_probs, -1, keepdims=True)))
    grad_queries = (
        jnp.einsum("bhqk,bkhd->bqhd", grad_scores, split_heads(key_rows), preferred_element_type=jnp.float32)
        * scale
    )
    grad_keys = (
        jnp.einsum("bhqk,bqhd->bkhd", grad_scores, split_heads(queries), preferred_element_type=jnp.float32)
        * scale
    )
    return tuple(value.reshape(ROWS, -1) for value in (grad_queries, grad_keys, grad_values))


def split_heads(value):
    return value.reshape(MICRO, LEN, HEADS, value.shape[1] // HEADS)


def norm_back(grad_out, normed, inv_std, norm_gain):
    scaled = grad_out * norm_gain
    grad_in = inv_std * (
        scaled
        - jnp.mean(scaled, -1, keepdims=True)
        - normed * jnp.mean(scaled * normed, -1, keepdims=True)
    )
    return grad_in, jnp.sum(grad_out * normed, 0), jnp.sum(grad_out, 0)


def backward(grad_decoded, held, norms, saved):
    qkv_all, probs_all, normed_all, inv_all, feed_in, slopes, bottles = saved
    gains, biases = [None] * 7, [None] * 7

    def norm(grad, which):
        grad, gains[which], biases[which] = norm_back(grad, normed_all[which], inv_all[which, :, :1], norms[which])
        return grad

    def feed(grad, side, which):
        grad_sum = norm(grad, which)
        low_grad = low(grad_sum)
        grad_hidden = low(dot_rows(low_grad, held["narrow"][side]) * wide(slopes[side]))
        grad_bottle = low(BRANCH_SCALE * dot_rows(low_grad, held["up"][side]) * wide(bottles[side, 1]))
        grad_in = grad_sum + dot_rows(grad_hidden, held["widen"][side]) + dot_rows(grad_bottle, held["down"][side])
        grad_up = BRANCH_SCALE * dot_columns(bottles[side, 0], low_grad)
        return grad_in, dot_columns(feed_in[side], grad_bottle), grad_up

    def attend(grad, layer, which):
        grad_sum = norm(grad, which)
        grad_att = low(dot_rows(low(grad_sum), held["attn_out"][layer]))
        qkv = qkv_all[layer]
        probs = probs_all[layer].reshape(MICRO, HEADS, LEN, LEN)
        parts = attend_back(grad_att, qkv[:, :1024], qkv[:, 1024:2048], qkv[:, 2048:], probs, 0.125)
        packed = low(jnp.concatenate(parts, 1))
        w_in = held["attn_in"][layer]
        if layer == 2:
            return grad_sum + dot_rows(packed[:, :1024], w_in[:, :1024]), dot_rows(packed[:, 1024:], w_in[:, 1024:])
        return grad_sum + dot_rows(packed, w_in), None

    grad, down_dec, up_dec = feed(grad_decoded, 1, 6)
    grad, grad_memory = attend(grad, 2, 5)
    grad, _ = attend(grad, 1, 4)
    norm(grad, 3)
    grad, down_enc, up_enc = feed(grad_memory, 0, 2)
    grad, _ = attend(grad, 0, 1)
    norm(grad, 0)
    return down_enc, up_enc, down_dec, up_dec, jnp.stack(gains + biases)


def adam_step(weight, first, second, grad, rate):
    first = BETA_FIRST * first + (1.0 - BETA_FIRST) * grad
    second = BETA_SECOND * second + (1.0 - BETA_SECOND) * grad * grad
    first_hat = first / (1.0 - BETA_FIRST**STEP)
    second_hat = second / (1.0 - BETA_SECOND**STEP)
    weight = weight - rate * (
        first_hat / (jnp.sqrt(second_hat) + ADAM_EPSILON) + WEIGHT_DECAY * weight
    )
    return (first, second, weight)


def head(decoded, vocab_table, target_ids, target_length, seq_scale, groups, vocab_rank):
    rows_local = vocab_table.shape[0]
    key_index = jnp.arange(LEN)
    head_rows = lax.all_gather(decoded, "vocab", axis=0, tiled=True)
    logits = dot_rows(head_rows, vocab_table)
    local_target = target_ids.reshape(-1) - vocab_rank * rows_local
    target_hot = lax.broadcasted_iota(jnp.int32, logits.shape, 1) == local_target[:, None]
    target_logit = jnp.sum(jnp.where(target_hot, logits, 0.0), 1)
    local_max = jnp.max(logits, 1)
    row_max = lax.pmax(local_max, "vocab")
    row_total, row_target = lax.psum(
        (jnp.sum(jnp.exp(logits - row_max[:, None]), 1), target_logit), "vocab"
    )
    log_total = row_max + jnp.log(row_total)
    row_mask = (key_index[None, :] < target_length[:, None]).astype(jnp.float32)
    row_weight = (row_mask * seq_scale[:, None]).reshape(-1)
    row_loss = (log_total - row_target).reshape(-1, LEN) * row_mask
    own_loss = lax.dynamic_slice_in_dim(row_loss, vocab_rank * MICRO, MICRO)
    grad_logits = low(
        row_weight[:, None] * (jnp.exp(logits - log_total[:, None]) - target_hot.astype(jnp.float32))
    )
    grad_decoded = lax.psum_scatter(
        dot(grad_logits, vocab_table).astype(jnp.bfloat16), "vocab", scatter_dimension=0, tiled=True
    ).astype(jnp.float32)
    return grad_decoded, jnp.sum(own_loss, 1)


def local(
    source_ids,
    target_in,
    target_ids,
    source_length,
    target_length,
    task_ids,
    vocab_table,
    positions,
    attention_in,
    attention_out,
    widen_weight,
    narrow_weight,
    adapt_down,
    adapt_up,
    norm_params,
    down_first,
    down_second,
    up_first,
    up_second,
    norm_first,
    norm_second,
):
    dp, groups = lax.axis_size("dp"), lax.axis_size("vocab")
    vocab_rank = lax.axis_index("vocab")
    rows_local, width = vocab_table.shape
    joined_ids = (
        jnp.stack([source_ids.reshape(groups, -1), target_in.reshape(groups, -1)], 1).reshape(-1)
        - vocab_rank * rows_local
    )
    inside = (joined_ids >= 0) & (joined_ids < rows_local)
    picked = jnp.where(
        inside[:, None],
        jnp.take(vocab_table, jnp.clip(joined_ids, 0, rows_local - 1), axis=0),
        jnp.zeros((), jnp.bfloat16),
    ).reshape(groups // 2, 2, 2, ROWS, width)
    task_hot = (task_ids[:, None] == jnp.arange(TASKS)[None, :]).astype(jnp.float32)
    task_counts = lax.psum(jnp.sum(task_hot * target_length[:, None].astype(jnp.float32), 0), "dp")
    seq_scale = jnp.sum(task_hot * (1.0 / (TASKS * task_counts))[None, :], 1)
    own = vocab_rank * MICRO
    source_count = lax.dynamic_slice_in_dim(source_length, own, MICRO)
    key_keep = jnp.broadcast_to(
        (jnp.arange(LEN)[None, None, :] < source_count[:, None, None]).astype(jnp.float32), (MICRO, 8, LEN)
    )
    parts = {
        "norms": jnp.pad(norm_params.T, ((0, 0), (0, 114)))[None],
        "attn_in": attention_in,
        "attn_out": attention_out,
        "widen": widen_weight,
        "narrow": narrow_weight,
        "down": low(adapt_down),
        "up": low(adapt_up),
    }
    held, saved = run_forward(parts, picked, positions, key_keep, dp, groups)
    norms = held["norms"][0, :, :14].T
    decoded = saved[7]
    grad_decoded, own_loss = head(decoded, vocab_table, target_ids, target_length, seq_scale, groups, vocab_rank)
    task_local = jnp.sum(lax.dynamic_slice_in_dim(task_hot, own, MICRO) * own_loss[:, None], 0)
    down_enc, up_enc, down_dec, up_dec, norm_grads = backward(grad_decoded, held, norms, saved[:7])
    small = jnp.concatenate(
        [norm_grads, jnp.pad(task_local[None], ((0, 1), (0, width - TASKS)))], 0
    )
    down_enc, up_enc, down_dec, up_dec, small, square = reduce_gradients(
        down_enc, up_enc, down_dec, up_dec, small, dp, groups
    )
    shard_down = jnp.stack([down_enc, down_dec])
    shard_up = jnp.stack([up_enc, up_dec])
    full_norm, task_sums = small[:14], small[14, :TASKS]
    cut = norm_params.shape[1]
    shard_norm = lax.dynamic_slice_in_dim(full_norm, lax.axis_index(("dp", "vocab")) * cut, cut, 1)
    grad_norm = jnp.sqrt(square[0, 0])
    factor = CLIP_LIMIT / jnp.maximum(grad_norm, CLIP_LIMIT)
    down_new = adam_step(adapt_down, down_first, down_second, shard_down * factor, RATE_ADAPTER)
    up_new = adam_step(adapt_up, up_first, up_second, shard_up * factor, RATE_ADAPTER)
    norm_new = adam_step(norm_params, norm_first, norm_second, shard_norm * factor, RATE_NORMS)
    return (*down_new, *up_new, *norm_new, grad_norm, task_sums, task_counts)


def solution(mesh):
    return jax.shard_map(
        local,
        mesh=mesh,
        in_specs=(
            P("dp", None),
            P("dp", None),
            P("dp", None),
            P("dp"),
            P("dp"),
            P("dp"),
            P("vocab", None),
            P(),
            P(None, ("dp", "vocab"), None),
            P(None, ("dp", "vocab"), None),
            P(None, ("dp", "vocab"), None),
            P(None, ("dp", "vocab"), None),
            P(None, ("dp", "vocab"), None),
            P(None, ("dp", "vocab"), None),
            P(None, ("dp", "vocab")),
            P(None, ("dp", "vocab"), None),
            P(None, ("dp", "vocab"), None),
            P(None, ("dp", "vocab"), None),
            P(None, ("dp", "vocab"), None),
            P(None, ("dp", "vocab")),
            P(None, ("dp", "vocab")),
        ),
        out_specs=(
            P(None, ("dp", "vocab"), None),
            P(None, ("dp", "vocab"), None),
            P(None, ("dp", "vocab"), None),
            P(None, ("dp", "vocab"), None),
            P(None, ("dp", "vocab"), None),
            P(None, ("dp", "vocab"), None),
            P(None, ("dp", "vocab")),
            P(None, ("dp", "vocab")),
            P(None, ("dp", "vocab")),
            P(),
            P(),
            P(),
        ),
        check_vma=False,
    )
```

```python
import functools

import jax
import jax.numpy as jnp
from jax import lax
from jax.experimental import pallas as pl
from jax.experimental.pallas import tpu as pltpu
from jax.sharding import PartitionSpec as P

MESH_ID = pl.DeviceIdType.MESH
TASKS = 4
STEP = 10
CLIP_LIMIT = 0.002
BETA_FIRST = 0.9
BETA_SECOND = 0.999
ADAM_EPSILON = 1e-08
WEIGHT_DECAY = 0.01
RATE_ADAPTER = 0.02
RATE_NORMS = 0.2


def grid_of(dp, vocab):
    cores = 2
    across = vocab // cores
    return {"z": dp // across, "y": across, "x": across, "c": cores}


def position(sizes):
    dp, vocab = lax.axis_index("dp"), lax.axis_index("vocab")
    return {
        "z": dp // sizes["y"],
        "y": dp % sizes["y"],
        "x": vocab // sizes["c"],
        "c": vocab % sizes["c"],
    }


def device_at(here, sizes, **moved):
    at = dict(here)
    at.update(moved)
    return (at["z"] * sizes["y"] + at["y"], at["x"] * sizes["c"] + at["c"])


def lines_barrier(here, sizes):
    barrier = pltpu.get_barrier_semaphore()
    peers = 0
    for axis in "zyxc":
        for step in range(1, sizes[axis]):
            other = (here[axis] + step) % sizes[axis]
            pl.semaphore_signal(
                barrier, inc=1, device_id=device_at(here, sizes, **{axis: other}), device_id_type=MESH_ID
            )
            peers += 1
    pl.semaphore_wait(barrier, peers)


def reduce_kernel(sizes, *refs):
    grads = refs[0:4]
    small = refs[4]
    shards = refs[5:9]
    small_out, square_out = refs[9:11]
    sums, core_send, core_recv = refs[11:15], refs[15:19], refs[19:23]
    wide_send, wide_recv, mid_send, mid_recv, last_send, last_recv = (
        refs[23:27], refs[27:31], refs[31:35], refs[35:39], refs[39:43], refs[43:47]
    )
    small_slots, square_slots = refs[47:51], refs[51:55]
    send_sem, recv_sem = refs[55:57]
    here = position(sizes)
    lines_barrier(here, sizes)
    used = [0]
    started = []

    def copy_to(src, dst, **moved):
        number = used[0]
        used[0] += 1
        copy = pltpu.make_async_remote_copy(
            src_ref=src,
            dst_ref=dst,
            send_sem=send_sem.at[number],
            recv_sem=recv_sem.at[number],
            device_id=device_at(here, sizes, **moved),
            device_id_type=MESH_ID,
        )
        copy.start()
        started.append(copy)
        return copy

    def low(value):
        return value.astype(jnp.bfloat16)

    mine = here["c"]

    def share(slots, value, axis):
        slots[here[axis]] = value
        return [
            copy_to(slots.at[here[axis]], slots.at[here[axis]], **{axis: (here[axis] + step) % sizes[axis]})
            for step in range(1, sizes[axis])
        ]

    def total(slots, axis, copies):
        for copy in copies:
            copy.wait_recv()
        value = slots[0]
        for index in range(1, sizes[axis]):
            value = value + slots[index]
        return value

    first = []
    for part in range(4):
        core_send[part][...] = low(grads[part][:, :, :, 1 - mine])
        first.append(copy_to(core_send[part], core_recv[part], c=1 - mine))
    copies = share(small_slots[0], small[...], "c")
    plans = (("x", "y"), ("x", "y"), ("y", "x"), ("y", "x"))

    second = []
    for part in range(4):
        first[part].wait_recv()
        sums[part][...] = grads[part][:, :, :, mine] + core_recv[part][...].astype(jnp.float32)
        axis = plans[part][0]
        found = []
        for step in range(1, sizes[axis]):
            other = (here[axis] + step) % sizes[axis]
            piece = sums[part][:, :, other] if axis == "x" else sums[part][:, other]
            wide_send[part][step - 1] = low(piece)
            found.append(copy_to(wide_send[part].at[step - 1], wide_recv[part].at[step - 1], **{axis: other}))
        second.append(found)
    copies = share(small_slots[1], total(small_slots[0], "c", copies), "x")
    third = []
    for part in range(4):
        axis, later = plans[part]
        held = sums[part].at[:, :, here["x"]] if axis == "x" else sums[part].at[:, here["y"]]
        value = held[...]
        for step, copy in enumerate(second[part]):
            copy.wait_recv()
            value = value + wide_recv[part][step].astype(jnp.float32)
        held[...] = value
        found = []
        for step in range(1, sizes[later]):
            other = (here[later] + step) % sizes[later]
            mid_send[part][step - 1] = low(held[:, other])
            found.append(copy_to(mid_send[part].at[step - 1], mid_recv[part].at[step - 1], **{later: other}))
        third.append(found)
    copies = share(small_slots[2], total(small_slots[1], "x", copies), "y")
    fourth = []
    for part in range(4):
        axis, later = plans[part]
        held = sums[part].at[:, here["y"], here["x"]]
        value = held[...]
        for step, copy in enumerate(third[part]):
            copy.wait_recv()
            value = value + mid_recv[part][step].astype(jnp.float32)
        held[...] = value
        found = []
        for step in range(1, sizes["z"]):
            other = (here["z"] + step) % sizes["z"]
            last_send[part][step - 1] = low(held[other])
            found.append(copy_to(last_send[part].at[step - 1], last_recv[part].at[step - 1], z=other))
        fourth.append(found)
    copies = share(small_slots[3], total(small_slots[2], "y", copies), "z")
    square = jnp.zeros((1, 1), jnp.float32)
    for part in range(4):
        value = sums[part][here["z"], here["y"], here["x"]]
        for step, copy in enumerate(fourth[part]):
            copy.wait_recv()
            value = value + last_recv[part][step].astype(jnp.float32)
        shards[part][...] = value
        square = square + jnp.sum(value * value, keepdims=True)
    square = jnp.broadcast_to(square, (8, 128))
    for place, axis in enumerate("cxyz"):
        parts = share(square_slots[place], square, axis)
        if place == 0:
            whole = total(small_slots[3], "z", copies)
            small_out[...] = whole
            norm_square = jnp.sum(whole[:14] * whole[:14], keepdims=True)
        square = total(square_slots[place], axis, parts)
    square_out[...] = square + norm_square
    for copy in started:
        copy.wait_send()


def reduce_gradients(down_enc, up_enc, down_dec, up_dec, small, dp, vocab):
    sizes = grid_of(dp, vocab)
    grid = tuple(sizes[axis] for axis in "zyxc")
    whole = dp * vocab
    grads = [
        value.reshape(grid + (value.shape[0] // whole, value.shape[1]))
        for value in (down_enc, up_enc, down_dec, up_dec)
    ]
    z, y, x, c = grid
    tails = [value.shape[4:] for value in grads]
    vmem = pl.BlockSpec(memory_space=pltpu.VMEM)
    scratch = [pltpu.VMEM((z, y, x) + tail, jnp.float32) for tail in tails]
    for _ in range(2):
        scratch += [pltpu.VMEM((z, y, x) + tail, jnp.bfloat16) for tail in tails]
    for _ in range(2):
        scratch += [
            pltpu.VMEM(((x - 1, z, y) if place < 2 else (y - 1, z, x)) + tail, jnp.bfloat16)
            for place, tail in enumerate(tails)
        ]
    for _ in range(2):
        scratch += [
            pltpu.VMEM(((y - 1, z) if place < 2 else (x - 1, z)) + tail, jnp.bfloat16)
            for place, tail in enumerate(tails)
        ]
    for _ in range(2):
        scratch += [pltpu.VMEM((z - 1,) + tail, jnp.bfloat16) for tail in tails]
    scratch += [pltpu.VMEM((sizes[axis],) + small.shape, jnp.float32) for axis in "cxyz"]
    scratch += [pltpu.VMEM((sizes[axis], 8, 128), jnp.float32) for axis in "cxyz"]
    links = 6 * (x + y + z + c)
    scratch += [pltpu.SemaphoreType.DMA((links,)), pltpu.SemaphoreType.DMA((links,))]
    return pl.pallas_call(
        functools.partial(reduce_kernel, sizes),
        out_shape=[jax.ShapeDtypeStruct(tail, jnp.float32) for tail in tails]
        + [jax.ShapeDtypeStruct(small.shape, jnp.float32), jax.ShapeDtypeStruct((8, 128), jnp.float32)],
        in_specs=[vmem] * 5,
        out_specs=[vmem] * 6,
        scratch_shapes=scratch,
        compiler_params=pltpu.CompilerParams(
            collective_id=1, has_side_effects=True, vmem_limit_bytes=48 * 2**20
        ),
    )(*grads, small)


ORDERS = ("xzy", "yzx", "zyx", "xzy", "yzx", "zxy")
SEQUENCE = (
    ("norms", 0), ("attn_in", 0), ("attn_out", 0), ("down", 0), ("widen", 0), ("up", 0), ("narrow", 0),
    ("attn_in", 1), ("attn_out", 1), ("attn_in", 2), ("attn_out", 2), ("down", 1), ("widen", 1), ("up", 1),
    ("narrow", 1),
)
COLUMNS = {"norms": 128, "attn_in": 512, "attn_out": 512, "down": 512, "widen": 512, "up": 512, "narrow": 256}
LAG = 3.0
PACE = 0.7
HEADS = 16
LEN = 128
MICRO = 2
ROWS = 256
NORM_EPS = 1e-05
NEGATIVE = -1000000000.0
BRANCH_SCALE = 4.0


def hops_of(order, sizes):
    return [(axis, hop) for axis in order for hop in range(1, sizes[axis])]


def plan_units(shapes, names, devices):
    units, clock = [], 0.0
    for name, layer in SEQUENCE:
        if name not in names:
            continue
        rows, columns = shapes[name]
        step = min(COLUMNS[name], columns)
        for left in range(0, columns, step):
            units.append((name, layer, left, step, clock))
            clock += rows * devices * step / 2**19
    return units


def dot(left, right):
    return jnp.dot(left, right, preferred_element_type=jnp.float32)


def dot_rows(left, right):
    return lax.dot_general(left, right, (((1,), (1,)), ((), ())), preferred_element_type=jnp.float32)


def dot_columns(left, right):
    return lax.dot_general(left, right, (((0,), (0,)), ((), ())), preferred_element_type=jnp.float32)


def low(value):
    return value.astype(jnp.bfloat16)


def wide(value):
    return value.astype(jnp.float32)


def norm_rows(value, gain, bias):
    centred = value - jnp.mean(value, -1, keepdims=True)
    inv_std = lax.rsqrt(jnp.mean(centred * centred, -1, keepdims=True) + NORM_EPS)
    normed = centred * inv_std
    return normed * gain + bias, normed, inv_std


def gelu_pair(value):
    half = 0.5 * (1.0 + lax.erf(value * 0.7071067811865476))
    return value * half, half + value * jnp.exp(-0.5 * value * value) * 0.3989422804014327


def lane_masks():
    lanes = lax.broadcasted_iota(jnp.int32, (LEN, 128), 1)
    first = (lanes < 64).astype(jnp.float32).astype(jnp.bfloat16)
    return first, (lanes >= 64).astype(jnp.float32).astype(jnp.bfloat16)


def stack_heads(value, masks):
    return jnp.concatenate([value * masks[0], value * masks[1]], 0)


def attend_pair(qkv, probs, attended, seq, pair, keep):
    masks = lane_masks()
    rows = pl.ds(pl.multiple_of(seq * LEN, LEN), LEN)

    def columns(part):
        return pl.ds(pl.multiple_of(part * 1024 + pair * 128, 128), 128)

    queries, keys, values = (qkv[rows, columns(part)] for part in range(3))
    scores = dot_rows(stack_heads(queries, masks), keys) * 0.125
    scores = jnp.where(keep(seq), scores, NEGATIVE)
    spread = jnp.exp(scores - jnp.max(scores, -1, keepdims=True))
    chance = low(spread / jnp.sum(spread, -1, keepdims=True))
    probs[seq, pair] = chance
    side = jnp.concatenate([chance[:LEN], chance[LEN:]], 1)
    attended[rows, columns(0)] = low(dot(side, stack_heads(values, masks)))


def forward_kernel(sizes, units, names, *refs):
    refs = list(refs)

    def take(count):
        found = refs[:count]
        del refs[:count]
        return found

    count = len(names)
    ins = dict(zip(names, take(count)))
    picked, places, key_keep = take(3)
    extra_up = None if "up" in names else take(1)[0]
    outs = dict(zip(names, take(count)))
    saved_out = take(8)
    send_sem, recv_sem, local_sem, sib_send, sib_recv = take(5)
    saved = take(8)
    qkv_all, probs_all, normed_all, inv_all, feed_in, slopes, bottles, decoded = saved
    embed_sem, embed_here, embed_core, embed_line = take(4)
    norm_tile, norms = take(2)
    stream, stream_low, memory, attended, branch, hidden = take(6)
    tiles, tall_tiles, tile_sem, tall_sem, save_sem = take(5)
    here = position(sizes)

    def at_device(**moved):
        return device_at(here, sizes, **moved)

    barrier = pltpu.get_barrier_semaphore()
    pl.semaphore_signal(barrier, inc=1, device_id=at_device(c=1 - here["c"]), device_id_type=MESH_ID)
    peers = jnp.int32(1)
    for step in range(1, sizes["x"]):
        other = (here["x"] + step) % sizes["x"]
        pl.semaphore_signal(barrier, inc=1, device_id=at_device(x=other), device_id_type=MESH_ID)
        peers = peers + 1
    for axis in "zy":
        for step in (-1, 1):
            ok = (here[axis] + step >= 0) & (here[axis] + step < sizes[axis])
            peers = peers + ok.astype(jnp.int32)

            @pl.when(ok)
            def _(axis=axis, step=step):
                pl.semaphore_signal(
                    barrier, inc=1, device_id=at_device(**{axis: here[axis] + step}), device_id_type=MESH_ID
                )

    pl.semaphore_wait(barrier, peers)

    everything = slice(None)

    def own_source(unit):
        name, layer, left, width, _ = unit
        return ins[name].at[layer, :, pl.ds(left, width)]

    def piece(unit, index):
        name, layer, left, width, _ = unit
        return outs[name].at[(layer,) + index + (everything, pl.ds(left, width))]

    def view(unit, order, axis, coordinate):
        place = order.index(axis)
        at = {other: everything if order.index(other) < place else here[other] for other in "zyx"}
        at[axis] = coordinate
        return piece(unit, (at["z"], at["y"], at["x"], here["c"]))

    def sends(number, stage):
        unit, order = units[number], ORDERS[number % len(ORDERS)]
        axis, hop = hops_of(order, sizes)[stage]
        size, mine = sizes[axis], here[axis]
        first = order.index(axis) == 0
        found = []
        for way, step in enumerate((1, -1)):
            origin = mine - step * (hop - 1)
            ok = (origin >= 0) & (origin < size) & (mine + step >= 0) & (mine + step < size)
            origin_r = mine - step * hop
            ok_r = (origin_r >= 0) & (origin_r < size)

            def build(receive, step=step, way=way, origin=origin, origin_r=origin_r):
                which = origin_r if receive else origin
                fresh = first and hop == 1 and not receive
                return pltpu.make_async_remote_copy(
                    src_ref=own_source(unit) if fresh else view(unit, order, axis, which),
                    dst_ref=view(unit, order, axis, which),
                    send_sem=send_sem.at[number, stage * 2 + way],
                    recv_sem=recv_sem.at[number, stage * 2 + way],
                    device_id=at_device(**{axis: mine + step}),
                    device_id_type=MESH_ID,
                )

            found.append((ok, ok_r, build))
        return found

    def local_copy(number):
        index = tuple(here[axis] for axis in "zyxc")
        return pltpu.make_async_copy(own_source(units[number]), piece(units[number], index), local_sem.at[number])

    def sibling(number):
        plane = piece(units[number], (everything, everything, everything, here["c"]))
        return pltpu.make_async_remote_copy(
            src_ref=plane,
            dst_ref=plane,
            send_sem=sib_send.at[number],
            recv_sem=sib_recv.at[number],
            device_id=at_device(c=1 - here["c"]),
            device_id_type=MESH_ID,
        )

    depth = sum(sizes[axis] - 1 for axis in "zyx")

    def comm_step(number, stage):
        if stage == 0:
            local_copy(number).start()
        if 1 <= stage <= depth:
            for _, ok_r, build in sends(number, stage - 1):

                @pl.when(ok_r)
                def _(build=build):
                    build(True).wait_recv()

        if stage == sizes[ORDERS[number % len(ORDERS)][0]] - 1:
            local_copy(number).wait()
        if stage < depth:
            for ok, _, build in sends(number, stage):

                @pl.when(ok)
                def _(build=build):
                    build(False).start()

        if stage == depth:
            sibling(number).start()
        if stage == depth + 1:
            sibling(number).wait_recv()

    mine, column = here["c"], here["x"]

    def embed_first(group):
        return pltpu.make_async_remote_copy(
            src_ref=picked.at[:, 1 - mine, group],
            dst_ref=embed_core.at[group],
            send_sem=embed_sem.at[0, group],
            recv_sem=embed_sem.at[1, group],
            device_id=at_device(c=1 - mine),
            device_id_type=MESH_ID,
        )

    def embed_local(group):
        return pltpu.make_async_copy(picked.at[:, mine, group], embed_here.at[group], embed_sem.at[2, group])

    def embed_second(group, step):
        other = (column + step) % sizes["x"]
        return pltpu.make_async_remote_copy(
            src_ref=embed_here.at[group, other],
            dst_ref=embed_line.at[group, step - 1],
            send_sem=embed_sem.at[2 + step * 2 - 1, group],
            recv_sem=embed_sem.at[2 + step * 2, group],
            device_id=at_device(x=other),
            device_id_type=MESH_ID,
        )

    def embed_pass(group):
        embed_first(group).wait_recv()
        embed_local(group).wait()
        embed_here[group] = embed_here[group] + embed_core[group]
        for step in range(1, sizes["x"]):
            embed_second(group, step).start()

    def embed_rows(group):
        rows = wide(embed_here[group, column])
        for step in range(1, sizes["x"]):
            embed_second(group, step).wait_recv()
            rows = rows + wide(embed_line[group, step - 1])
        place = wide(places[group])
        return rows + jnp.concatenate([place] * MICRO, 0)

    saves = []

    def save(place, index):
        def build(number=len(saves)):
            return pltpu.make_async_copy(
                saved[place].at[index] if index else saved[place],
                saved_out[place].at[index] if index else saved_out[place],
                save_sem.at[number],
            )

        saves.append(build)
        build().start()

    def norm_step(value, which, side):
        result, normed, inv_std = norm_rows(value, norms[which : which + 1, :], norms[which + 7 : which + 8, :])
        normed_all[which] = normed
        inv_all[which] = jnp.broadcast_to(inv_std, (ROWS, 128))
        save(2, (which,))
        save(3, (which,))
        stream[side] = result
        stream_low[side] = low(result)

    def begin(side):
        def run():
            if side == 0:
                copy = pltpu.make_async_copy(outs["norms"].at[0], norm_tile, tile_sem.at[len(tiles_used)])
                copy.start()
                copy.wait()
                columns = norm_tile[...].reshape(-1, 128)
                norms[...] = columns.T[:16]
            norm_step(embed_rows(side), 3 * side, side)

        return run

    tiles_used = [None] * tiles.shape[0]

    def project(which, left, side, from_memory):
        def run(tile):
            source = memory[...] if from_memory else stream_low[side]
            qkv_all[which, :, pl.ds(left, 512)] = low(dot(source, tile()))

        return run

    def attention(which, start, keep):
        def run():
            def body(number, _):
                seq, pair = number // 8, number % 8
                attend_pair(qkv_all.at[which], probs_all.at[which], attended, seq, pair, keep)
                return 0

            lax.fori_loop(start, start + 4, body, 0)

        return run

    def project_out(left):
        def run(tile):
            branch[:, pl.ds(left, 512)] = dot(attended[...], tile())

        return run

    def finish_attention(which, norm, side):
        def run():
            save(0, (which,))
            save(1, (which,))
            norm_step(stream[side] + branch[...], norm, side)

        return run

    def narrow_down(side):
        def run(tile):
            feed_in[side] = stream_low[side]
            value, slope = gelu_pair(dot(stream_low[side], tile()))
            bottles[side, 0] = low(value)
            bottles[side, 1] = low(slope)
            save(4, (side,))
            save(6, (side,))

        return run

    def widen(left, side):
        def run(tile):
            value, slope = gelu_pair(dot(stream_low[side], tile()))
            hidden[:, pl.ds(left, 512)] = low(value)
            slopes[side, :, pl.ds(left, 512)] = low(slope)

        return run

    def raise_up(left, side):
        def run(tile):
            branch[:, pl.ds(left, 512)] = BRANCH_SCALE * dot(bottles[side, 0], tile())

        return run

    def narrow(left, side):
        def run(tile):
            branch[:, pl.ds(left, 256)] += dot(hidden[...], tile())

        return run

    def finish_feed(norm, side):
        def run():
            save(5, (side,))
            norm_step(stream[side] + branch[...], norm, side)
            if side == 0:
                memory[...] = stream_low[0]
            else:
                decoded[...] = stream_low[1]
                save(7, ())

        return run

    def source_keep(seq):
        return jnp.broadcast_to(key_keep[seq, 0:1, :] > 0.0, (2 * LEN, LEN))

    def causal_keep(seq):
        query = lax.broadcasted_iota(jnp.int32, (2 * LEN, LEN), 0) % LEN
        return lax.broadcasted_iota(jnp.int32, (2 * LEN, LEN), 1) <= query

    steps = []
    unit_of = {}
    for number, unit in enumerate(units):
        unit_of[unit[:3]] = number

    def add(run, cost, unit=None, clock=0.0):
        steps.append((unit, cost, clock, run))

    def attention_steps(which, norm, side, keep):
        for left in range(0, 3072, 512):
            from_memory = which == 2 and left >= 1024
            add(project(which, left, side, from_memory), 0.6, unit_of["attn_in", which, left])
        for start in range(0, 16, 4):
            add(attention(which, start, keep), 2.0)
        for left in range(0, 1024, 512):
            add(project_out(left), 0.6, unit_of["attn_out", which, left])
        add(finish_attention(which, norm, side), 1.0)

    def feed_steps(norm, side):
        add(narrow_down(side), 1.3, unit_of["down", side, 0])
        for left in range(0, 4096, 512):
            add(widen(left, side), 1.3, unit_of["widen", side, left])
        for left in range(0, 1024, 512):
            if "up" in names:
                add(raise_up(left, side), 0.4, unit_of["up", side, left])
            else:
                part = functools.partial(lambda left, side: extra_up[side, :, pl.ds(left, 512)], left, side)
                add(functools.partial(raise_up(left, side), part), 0.4)
        for left in range(0, 1024, 256):
            add(narrow(left, side), 1.0, unit_of["narrow", side, left])
        add(finish_feed(norm, side), 1.0)

    add(begin(0), 2.0, unit_of["norms", 0, 0], 8.0)
    attention_steps(0, 1, 0, source_keep)
    feed_steps(2, 0)
    add(begin(1), 1.5, None, 20.0)
    attention_steps(1, 4, 1, causal_keep)
    attention_steps(2, 5, 1, source_keep)
    feed_steps(6, 1)

    loads = [step[0] for step in steps if isinstance(step[0], int) and units[step[0]][0] != "norms"]
    slot_of, rings = {}, {"tall": [], "flat": []}
    for unit in loads:
        kind = "tall" if units[unit][0] == "narrow" else "flat"
        ring = rings[kind]
        size = (tall_tiles if kind == "tall" else tiles).shape[0]
        slot_of[unit] = (kind, len(ring) % size, ring[len(ring) - size] if len(ring) >= size else None)
        ring.append(unit)

    def tile_parts(unit):
        kind, slot, _ = slot_of[unit]
        name, layer, left, width, _ = units[unit]
        source = outs[name].at[layer, :, :, :, :, :, pl.ds(left, width)]
        buffer = (tall_tiles if kind == "tall" else tiles).at[slot]
        sem = (tall_sem if kind == "tall" else tile_sem).at[slot]
        rows = ins[name].shape[1] * sizes["z"] * sizes["y"] * sizes["x"] * sizes["c"]
        target = buffer.at[pl.ds(0, rows)]
        shape = tuple(sizes[axis] for axis in "zyxc") + (ins[name].shape[1], width)
        return pltpu.make_async_copy(source, target.reshape(shape), sem), target

    complete, loaded, done = set(), set(), set()
    waiting = list(loads)

    def try_loads():
        while waiting:
            unit = waiting[0]
            before = slot_of[unit][2]
            if unit not in complete or (before is not None and before not in done):
                return
            tile_parts(unit)[0].start()
            loaded.add(unit)
            waiting.pop(0)

    queue = list(steps)

    def run_step():
        unit, cost, _, run = queue.pop(0)
        if unit is None or units[unit][0] == "norms":
            run()
        else:
            copy, target = tile_parts(unit)
            copy.wait()
            run(lambda: target[...])
            done.add(unit)
        try_loads()
        return cost

    def ready(clock):
        if not queue:
            return False
        unit, _, earliest, _ = queue[0]
        if earliest > clock:
            return False
        if unit is None:
            return True
        return unit in complete if units[unit][0] == "norms" else unit in loaded

    for group in range(2):
        embed_first(group).start()
        embed_local(group).start()
    events = sorted(
        (unit[4] + LAG * stage, -stage, number) for number, unit in enumerate(units) for stage in range(depth + 2)
    )
    embed_done, credit, last = [], 0.0, 0.0
    for clock, minus, number in events:
        stage = -minus
        comm_step(number, stage)
        for group in range(2):
            if group not in embed_done and clock >= 1.5 + 1.5 * group:
                embed_done.append(group)
                embed_pass(group)
        if stage == depth + 1:
            complete.add(number)
            try_loads()
        credit = min(credit + 3.7 * PACE * (clock - last) , 4.0)
        last = clock
        while ready(clock) and credit > 0.0:
            credit -= run_step()
    while queue:
        run_step()
    for build in saves:
        build().wait()
    for group in range(2):
        embed_first(group).wait_send()
        for step in range(1, sizes["x"]):
            embed_second(group, step).wait_send()
    for number in range(len(units)):
        sibling(number).wait_send()
        for stage in range(depth):
            for ok, _, build in sends(number, stage):

                @pl.when(ok)
                def _(build=build):
                    build(False).wait_send()


def run_forward(arrays, picked, places, key_keep, dp, vocab):
    sizes = grid_of(dp, vocab)
    devices = dp * vocab
    grid = tuple(sizes[axis] for axis in "zyxc")
    extra = []
    arrays = dict(arrays)
    if arrays["up"].shape[1] % 8:
        extra = [lax.all_gather(arrays.pop("up"), ("dp", "vocab"), axis=1, tiled=True)]
    names = list(arrays)
    shapes = {name: arrays[name].shape[1:] for name in names}
    units = plan_units(shapes, names, devices)
    depth = sum(sizes[axis] - 1 for axis in "zyx")
    anywhere, vmem = pl.BlockSpec(memory_space=pl.ANY), pl.BlockSpec(memory_space=pltpu.VMEM)
    f32, b16 = jnp.float32, jnp.bfloat16
    saved = [
        ((3, ROWS, 3072), b16),
        ((3, MICRO, 8, 2 * LEN, LEN), b16),
        ((7, ROWS, 1024), f32),
        ((7, ROWS, 128), f32),
        ((2, ROWS, 1024), b16),
        ((2, ROWS, 4096), b16),
        ((2, 2, ROWS, 512), b16),
        ((ROWS, 1024), b16),
    ]
    out_shape = [
        jax.ShapeDtypeStruct((arrays[name].shape[0],) + grid + arrays[name].shape[1:], arrays[name].dtype)
        for name in names
    ] + [jax.ShapeDtypeStruct(shape, kind) for shape, kind in saved]
    x, n = sizes["x"], len(units)
    dma = pltpu.SemaphoreType.DMA
    out = pl.pallas_call(
        functools.partial(forward_kernel, sizes, units, names),
        out_shape=out_shape,
        in_specs=[anywhere] * (len(names) + 1) + [vmem] * (2 + len(extra)),
        out_specs=[anywhere] * len(out_shape),
        scratch_shapes=[dma((n, 2 * depth)), dma((n, 2 * depth)), dma((n,)), dma((n,)), dma((n,))]
        + [pltpu.VMEM(shape, kind) for shape, kind in saved]
        + [
            dma((3 + 2 * x, 2)),
            pltpu.VMEM((2, x, ROWS, 1024), b16),
            pltpu.VMEM((2, x, ROWS, 1024), b16),
            pltpu.VMEM((2, x - 1, ROWS, 1024), b16),
            pltpu.VMEM(grid + arrays["norms"].shape[1:], f32),
            pltpu.VMEM((16, 1024), f32),
            pltpu.VMEM((2, ROWS, 1024), f32),
            pltpu.VMEM((2, ROWS, 1024), b16),
            pltpu.VMEM((ROWS, 1024), b16),
            pltpu.VMEM((ROWS, 1024), b16),
            pltpu.VMEM((ROWS, 1024), f32),
            pltpu.VMEM((ROWS, 4096), b16),
            pltpu.VMEM((4, 1024, 512), b16),
            pltpu.VMEM((2, 4096, 256), b16),
            dma((5,)),
            dma((2,)),
            dma((32,)),
        ],
        compiler_params=pltpu.CompilerParams(
            collective_id=0, has_side_effects=True, vmem_limit_bytes=61 * 2**20
        ),
    )(*[arrays[name] for name in names], picked, places, key_keep, *extra)
    held = dict(zip(names, out[: len(names)]))
    if extra:
        held["up"] = extra[0]
    return held, out[len(names) :]


TILE = 1280


def head_kernel(sizes, *refs):
    decoded, targets, weight, table_hbm, grad_out, loss_out = refs[:6]
    rows, table, logits, partial, core_send, core_part, line_send, line_part, stats = refs[6:15]
    table_sem, row_sem, stat_sem, core_sem, line_sem, send_sem = refs[15:]
    here = position(sizes)
    mine, column, cores, across = here["c"], here["x"], sizes["c"], sizes["x"]
    owners = across * cores
    me, twin = column * cores + mine, column * cores + 1 - mine
    count = table.shape[0]
    steps = count // TILE

    def table_copy(number):
        part = pl.ds(number * TILE, TILE)
        return pltpu.make_async_copy(table_hbm.at[part], table.at[part], table_sem.at[number])

    for number in range(steps):
        table_copy(number).start()
    barrier = pltpu.get_barrier_semaphore()
    for step in range(1, owners):
        other = (me + step) % owners
        pl.semaphore_signal(
            barrier,
            inc=1,
            device_id=device_at(here, sizes, x=other // cores, c=other % cores),
            device_id_type=MESH_ID,
        )
    pl.semaphore_wait(barrier, owners - 1)
    started = []

    def remote(src, dst, arrival, **moved):
        copy = pltpu.make_async_remote_copy(
            src_ref=src,
            dst_ref=dst,
            send_sem=send_sem.at[len(started)],
            recv_sem=arrival,
            device_id=device_at(here, sizes, **moved),
            device_id_type=MESH_ID,
        )
        copy.start()
        started.append(copy)

    def arrived(ref, arrival):
        pltpu.make_async_remote_copy(
            src_ref=ref,
            dst_ref=ref,
            send_sem=send_sem.at[0],
            recv_sem=arrival,
            device_id=device_at(here, sizes, c=1 - mine),
            device_id_type=MESH_ID,
        ).wait_recv()

    def far(step, core):
        return (column + step) % across * cores + core

    rows[me] = decoded[...]
    for step in range(1, across):
        remote(rows.at[me], rows.at[me], row_sem.at[me], x=(column + step) % across)
    remote(rows.at[me], rows.at[me], row_sem.at[me], c=1 - mine)
    lane = lax.broadcasted_iota(jnp.int32, (ROWS, 128), 1)

    def first_pass(block, fresh=False):
        wanted = targets[block] - me * count

        def body(number, carry):
            top, spread, hit = carry
            start = pl.multiple_of(number * TILE, TILE)
            if fresh:
                part = pl.ds(start, TILE)
                pltpu.make_async_copy(table_hbm.at[part], table.at[part], table_sem.at[number]).wait()
            values = dot_rows(rows[block], table[pl.ds(start, TILE), :])
            logits[block, :, pl.ds(start, TILE)] = values
            parts = [values[:, at : at + 128] for at in range(0, TILE, 128)]
            new_top = top
            for part in parts:
                new_top = jnp.maximum(new_top, part)
            spread = spread * jnp.exp(top - new_top)
            near = wanted - start - lane
            for place, part in enumerate(parts):
                spread = spread + jnp.exp(part - new_top)
                hit = hit + jnp.where(near == place * 128, part, 0.0)
            return new_top, spread, hit

        zero = jnp.zeros((ROWS, 128), jnp.float32)
        low_start = jnp.full((ROWS, 128), -3e38, jnp.float32)
        top, spread, hit = lax.fori_loop(0, steps, body, (low_start, zero, zero))
        whole = jnp.max(top, -1, keepdims=True)
        spread = jnp.sum(spread * jnp.exp(top - whole), -1, keepdims=True)
        hit = jnp.sum(hit, -1, keepdims=True)
        stats[block, me] = jnp.where(lane == 0, whole, jnp.where(lane == 1, spread, hit)).T[:8]
        for step in range(1, owners):
            other = (me + step) % owners
            remote(
                stats.at[block, me],
                stats.at[block, me],
                stat_sem.at[block, me],
                x=other // cores,
                c=other % cores,
            )

    def second_pass(block, place):
        for step in range(1, owners):
            other = (me + step) % owners
            arrived(stats.at[block, other], stat_sem.at[block, other])
        found = [stats[block, index] for index in range(owners)]
        top = found[0][0:1]
        for value in found[1:]:
            top = jnp.maximum(top, value[0:1])
        spread, hit = jnp.zeros_like(top), jnp.zeros_like(top)
        for value in found:
            spread = spread + value[1:2] * jnp.exp(value[0:1] - top)
            hit = hit + value[2:3]
        log_total = top + jnp.log(spread)
        level = jnp.broadcast_to(log_total, (128, ROWS)).T
        wanted = targets[block] - me * count
        partial[place] = jnp.zeros((ROWS, 1024), jnp.float32)

        def body(number, _):
            start = pl.multiple_of(number * TILE, TILE)
            near = wanted - start - lane
            values = logits[block, :, pl.ds(start, TILE)]
            parts = []
            for index in range(TILE // 128):
                value = jnp.exp(values[:, index * 128 : (index + 1) * 128] - level)
                parts.append(low(jnp.where(near == index * 128, value - 1.0, value)))
            partial[place] += dot(jnp.concatenate(parts, 1), table[pl.ds(start, TILE), :])
            return 0

        lax.fori_loop(0, steps, body, 0)
        return log_total - hit

    first_pass(me, True)
    arrived(rows.at[twin], row_sem.at[twin])
    first_pass(twin)
    for step in range(1, across):
        block = far(step, mine)
        arrived(rows.at[block], row_sem.at[block])
        remote(rows.at[block], rows.at[block], row_sem.at[block], c=1 - mine)
        first_pass(block)
    for step in range(1, across):
        block = far(step, 1 - mine)
        arrived(rows.at[block], row_sem.at[block])
        first_pass(block)
    for step in range(1, across):
        for core in range(cores):
            second_pass(far(step, core), core)

            @pl.when(mine != core)
            def _(core=core, step=step):
                core_send[step - 1] = low(partial[core])
                pltpu.make_async_remote_copy(
                    src_ref=core_send.at[step - 1],
                    dst_ref=core_part.at[step - 1],
                    send_sem=core_sem.at[0, step - 1],
                    recv_sem=core_sem.at[1, step - 1],
                    device_id=device_at(here, sizes, c=1 - mine),
                    device_id_type=MESH_ID,
                ).start()

        arrived(core_part.at[step - 1], core_sem.at[1, step - 1])
        line_send[step - 1] = low(partial[mine] + wide(core_part[step - 1]))
        remote(
            line_send.at[step - 1],
            line_part.at[step - 1],
            line_sem.at[step - 1],
            x=(column + step) % across,
        )
    second_pass(twin, 0)
    last = across - 1
    core_send[last] = low(partial[0])
    remote(core_send.at[last], core_part.at[last], core_sem.at[1, last], c=1 - mine)
    loss = second_pass(me, 1)
    loss_out[...] = jnp.broadcast_to(loss, (8, ROWS))
    arrived(core_part.at[last], core_sem.at[1, last])
    value = partial[1] + wide(core_part[last])
    for step in range(1, across):
        arrived(line_part.at[step - 1], line_sem.at[step - 1])
        value = value + wide(line_part[step - 1])
    grad_out[...] = value * weight[:, :1]
    for copy in started:
        copy.wait_send()
    for step in range(1, across):
        pltpu.make_async_remote_copy(
            src_ref=core_send.at[step - 1],
            dst_ref=core_part.at[step - 1],
            send_sem=core_sem.at[0, step - 1],
            recv_sem=core_sem.at[1, step - 1],
            device_id=device_at(here, sizes, c=1 - mine),
            device_id_type=MESH_ID,
        ).wait_send()


def run_head(decoded, targets, weight, table, dp, vocab):
    sizes = grid_of(dp, vocab)
    across, owners = sizes["x"], vocab
    f32, b16 = jnp.float32, jnp.bfloat16
    anywhere, vmem = pl.BlockSpec(memory_space=pl.ANY), pl.BlockSpec(memory_space=pltpu.VMEM)
    dma = pltpu.SemaphoreType.DMA
    return pl.pallas_call(
        functools.partial(head_kernel, sizes),
        out_shape=[jax.ShapeDtypeStruct((ROWS, 1024), f32), jax.ShapeDtypeStruct((8, ROWS), f32)],
        in_specs=[vmem] * 3 + [anywhere],
        out_specs=[vmem] * 2,
        scratch_shapes=[
            pltpu.VMEM((owners, ROWS, 1024), b16),
            pltpu.VMEM(table.shape, b16),
            pltpu.VMEM((owners, ROWS, table.shape[0]), f32),
            pltpu.VMEM((2, ROWS, 1024), f32),
            pltpu.VMEM((across, ROWS, 1024), b16),
            pltpu.VMEM((across, ROWS, 1024), b16),
            pltpu.VMEM((across - 1, ROWS, 1024), b16),
            pltpu.VMEM((across - 1, ROWS, 1024), b16),
            pltpu.VMEM((owners, owners, 8, ROWS), f32),
            dma((table.shape[0] // TILE,)),
            dma((owners,)),
            dma((owners, owners)),
            dma((2, across)),
            dma((across,)),
            dma((8 * owners,)),
        ],
        compiler_params=pltpu.CompilerParams(
            collective_id=3, has_side_effects=True, vmem_limit_bytes=62 * 2**20
        ),
    )(
        decoded,
        jnp.broadcast_to(targets.reshape(owners, ROWS, 1), (owners, ROWS, 128)),
        jnp.broadcast_to(weight.reshape(ROWS, 1), (ROWS, 128)),
        table,
    )


def backward_kernel(sizes, *refs):
    refs = list(refs)

    def take(count):
        found = refs[:count]
        del refs[:count]
        return found

    grad_in, norms, extra = take(3)
    names = ("attn_in", "attn_out", "widen", "narrow", "down", "up")
    held = dict(zip(names, take(6)))
    saved_in = take(7)
    shards = take(4)
    small_out, square_out = take(2)
    saved = take(7)
    qkv_all, probs_all, normed_ring, inv_all, feed_in, slopes, bottles = saved
    saved_sem, normed_sem, tiles, tile_sem, down_tile, down_sem = take(6)
    grads = take(4)
    sums, core_send, core_recv = take(4), take(4), take(4)
    wide_send, wide_recv, mid_send, mid_recv, last_send, last_recv = (take(4) for _ in range(6))
    small, small_slots, square_slots = take(1)[0], take(4), take(4)
    grad_low, grad_sum, grad_memory, grad_hidden, grad_att, packed = take(6)
    send_sem, recv_sem = take(2)
    here = position(sizes)
    mine = here["c"]

    loads = {}

    def fetch(place, index):
        if (place, index) not in loads:
            copy = pltpu.make_async_copy(
                saved_in[place].at[index], saved[place].at[index], saved_sem.at[len(loads)]
            )
            loads[place, index] = copy
            copy.start()
        return loads[place, index]

    order = (6, 5, 4, 3, 2, 1, 0)

    def normed_copy(number):
        slot = number % normed_ring.shape[0]
        return pltpu.make_async_copy(saved_in[2].at[order[number]], normed_ring.at[slot], normed_sem.at[slot])

    plan = []
    block = 1024
    for kind, which in (("feed", 1), ("attend", 2), ("attend", 1), ("feed", 0), ("attend", 0)):
        if kind == "feed":
            for left in range(0, 4096, block):
                plan += [("narrow", which, left), ("widen", which, left)]
            plan.append(("up", which, 0))
        else:
            plan.append(("attn_out", which, 0))
            plan += [("attn_in", which, left) for left in range(0, 3072, block)]
    grid = tuple(sizes[axis] for axis in "zyxc")
    depth = tiles.shape[0]

    def tile_copy(number):
        name, layer, left = plan[number]
        rows, columns = held[name].shape[5:]
        buffer = tiles.at[number % depth]
        if name == "narrow":
            planes = left // block
            source, shape = held[name].at[layer, planes], grid[1:] + (rows, columns)
        else:
            columns = min(columns, block)
            source = held[name].at[layer, :, :, :, :, :, pl.ds(left, columns)]
            shape = grid + (rows, columns)
        count = 1
        for size in shape[:-1]:
            count *= size
        target = buffer.at[pl.ds(0, count), pl.ds(0, columns)]
        return pltpu.make_async_copy(source, target.reshape(shape), tile_sem.at[number % depth]), target

    def down_copy(side):
        target = down_tile.reshape(grid + held["down"].shape[5:])
        return pltpu.make_async_copy(held["down"].at[side], target, down_sem.at[0])

    turn = [0]

    def with_tile(use):
        number = turn[0]
        turn[0] += 1
        copy, target = tile_copy(number)
        copy.wait()
        result = use(target[...])
        if number + depth < len(plan):
            tile_copy(number + depth)[0].start()
        return result

    for number in range(2):
        normed_copy(number).start()
    fetch(3, slice(None))
    fetch(5, 1)
    for number in range(depth):
        tile_copy(number)[0].start()
    down_copy(1).start()
    for place, index in ((6, 1), (4, 1), (0, 2), (1, 2), (0, 1), (1, 1), (5, 0), (6, 0), (4, 0), (0, 0), (1, 0)):
        fetch(place, index)
    lines_barrier(here, sizes)

    used, started = [0], []

    def copy_to(src, dst, **moved):
        number = used[0]
        used[0] += 1
        copy = pltpu.make_async_remote_copy(
            src_ref=src,
            dst_ref=dst,
            send_sem=send_sem.at[number],
            recv_sem=recv_sem.at[number],
            device_id=device_at(here, sizes, **moved),
            device_id_type=MESH_ID,
        )
        copy.start()
        started.append(copy)
        return copy

    def share(slots, value, axis):
        slots[here[axis]] = value
        return [
            copy_to(slots.at[here[axis]], slots.at[here[axis]], **{axis: (here[axis] + step) % sizes[axis]})
            for step in range(1, sizes[axis])
        ]

    def total(slots, axis, copies):
        for copy in copies:
            copy.wait_recv()
        value = slots[0]
        for index in range(1, sizes[axis]):
            value = value + slots[index]
        return value

    plans = (("x", "y"), ("y", "x"), ("x", "y"), ("y", "x"))
    pending = [None] * 4

    def phase_core(parts):
        for part in parts:
            core_send[part][...] = low(grads[part][:, :, :, 1 - mine])
            pending[part] = copy_to(core_send[part], core_recv[part], c=1 - mine)

    def phase_wide(parts):
        for part in parts:
            pending[part].wait_recv()
            sums[part][...] = grads[part][:, :, :, mine] + wide(core_recv[part][...])
            axis = plans[part][0]
            found = []
            for step in range(1, sizes[axis]):
                other = (here[axis] + step) % sizes[axis]
                value = sums[part][:, :, other] if axis == "x" else sums[part][:, other]
                wide_send[part][step - 1] = low(value)
                found.append(copy_to(wide_send[part].at[step - 1], wide_recv[part].at[step - 1], **{axis: other}))
            pending[part] = found

    def phase_mid(parts):
        for part in parts:
            axis, later = plans[part]
            kept = sums[part].at[:, :, here["x"]] if axis == "x" else sums[part].at[:, here["y"]]
            value = kept[...]
            for step, copy in enumerate(pending[part]):
                copy.wait_recv()
                value = value + wide(wide_recv[part][step])
            kept[...] = value
            found = []
            for step in range(1, sizes[later]):
                other = (here[later] + step) % sizes[later]
                mid_send[part][step - 1] = low(kept[:, other])
                found.append(copy_to(mid_send[part].at[step - 1], mid_recv[part].at[step - 1], **{later: other}))
            pending[part] = found

    def phase_last(parts):
        for part in parts:
            kept = sums[part].at[:, here["y"], here["x"]]
            value = kept[...]
            for step, copy in enumerate(pending[part]):
                copy.wait_recv()
                value = value + wide(mid_recv[part][step])
            kept[...] = value
            found = []
            for step in range(1, sizes["z"]):
                other = (here["z"] + step) % sizes["z"]
                last_send[part][step - 1] = low(kept[other])
                found.append(copy_to(last_send[part].at[step - 1], last_recv[part].at[step - 1], z=other))
            pending[part] = found

    def phase_end(parts):
        square = jnp.zeros((1, 1), jnp.float32)
        for part in parts:
            value = sums[part][here["z"], here["y"], here["x"]]
            for step, copy in enumerate(pending[part]):
                copy.wait_recv()
                value = value + wide(last_recv[part][step])
            shards[part][...] = value
            square = square + jnp.sum(value * value, keepdims=True)
        return square

    norm_turn = [0]

    def norm_back(grad_out, which):
        number = norm_turn[0]
        norm_turn[0] += 1
        if number + 2 < len(order):
            normed_copy(number + 2).start()
        normed_copy(number).wait()
        normed = normed_ring[number % normed_ring.shape[0]]
        inv_std = inv_all[which][:, :1]
        scaled = grad_out * norms[which : which + 1, :]
        small[which : which + 1, :] = jnp.sum(grad_out * normed, 0, keepdims=True)
        small[which + 7 : which + 8, :] = jnp.sum(grad_out, 0, keepdims=True)
        grad = inv_std * (
            scaled - jnp.mean(scaled, -1, keepdims=True) - normed * jnp.mean(scaled * normed, -1, keepdims=True)
        )
        grad_sum[...] = grad
        grad_low[...] = low(grad)

    def feed_back(side):
        fetch(5, side).wait()
        for left in range(0, 4096, block):

            def first(tile, left=left):
                slope = wide(slopes[side, :, pl.ds(left, block)])
                grad_hidden[...] = low(dot_rows(grad_low[...], tile) * slope)

            def second(tile):
                grad_sum[...] += dot_rows(grad_hidden[...], tile)

            with_tile(first)
            with_tile(second)
        fetch(6, side).wait()
        fetch(4, side).wait()

        def up(tile):
            bottle = low(BRANCH_SCALE * dot_rows(grad_low[...], tile) * wide(bottles[side, 1]))
            grad_hidden[:, pl.ds(0, 512)] = bottle

        with_tile(up)
        down_copy(side).wait()
        grad_sum[...] += dot_rows(grad_hidden[:, pl.ds(0, 512)], down_tile[...])
        if side:
            down_copy(0).start()
        part = 2 * side
        grads[part + 1][...] = (BRANCH_SCALE * dot_columns(bottles[side, 0], grad_low[...])).reshape(
            grads[part + 1].shape
        )
        grads[part][...] = dot_columns(feed_in[side], grad_hidden[:, pl.ds(0, 512)]).reshape(grads[part].shape)

    def attend_back(layer, between=None):
        def first(tile):
            grad_att[...] = low(dot_rows(grad_low[...], tile))

        with_tile(first)
        fetch(0, layer).wait()
        fetch(1, layer).wait()

        def body(number, _):
            seq, pair = number // 8, number % 8
            masks = lane_masks()
            rows = pl.ds(pl.multiple_of(seq * LEN, LEN), LEN)

            def columns(part):
                return pl.ds(pl.multiple_of(part * 1024 + pair * 128, 128), 128)

            queries, keys, values = (qkv_all[layer, rows, columns(part)] for part in range(3))
            grad_out = stack_heads(grad_att[rows, columns(0)], masks)
            chance_low = probs_all[layer, seq, pair]
            chance = wide(chance_low)
            weighed = chance * dot_rows(grad_out, values)
            grad_scores = low(weighed - chance * jnp.sum(weighed, -1, keepdims=True))
            side = jnp.concatenate([grad_scores[:LEN], grad_scores[LEN:]], 1)
            packed[rows, columns(0)] = low(dot(side, stack_heads(keys, masks)) * 0.125)
            packed[rows, columns(1)] = low(dot_columns(grad_scores, stack_heads(queries, masks)) * 0.125)
            packed[rows, columns(2)] = low(dot_columns(chance_low, grad_out))
            return 0

        lax.fori_loop(0, 8 * MICRO, body, 0, unroll=2)
        if between is not None:
            between()
        for left in range(0, 3072, block):

            def second(tile, left=left):
                value = dot_rows(packed[:, pl.ds(left, block)], tile)
                if layer == 2 and left == block:
                    grad_memory[...] = value
                elif layer == 2 and left > block:
                    grad_memory[...] += value
                else:
                    grad_sum[...] += value

            with_tile(second)

    small[...] = extra[...]
    fetch(3, slice(None)).wait()
    norm_back(grad_in[...], 6)
    feed_back(1)
    phase_core((2, 3))
    norm_back(grad_sum[...], 5)
    attend_back(2)
    phase_wide((2, 3))
    norm_back(grad_sum[...], 4)
    attend_back(1)
    phase_mid((2, 3))
    norm_back(grad_sum[...], 3)
    norm_back(grad_memory[...], 2)
    feed_back(0)
    phase_core((0, 1))
    phase_last((2, 3))
    norm_back(grad_sum[...], 1)
    attend_back(0, lambda: phase_wide((0, 1)))
    square = phase_end((2, 3))
    phase_mid((0, 1))
    norm_back(grad_sum[...], 0)
    copies = share(small_slots[0], small[...], "c")
    phase_last((0, 1))
    copies = share(small_slots[1], total(small_slots[0], "c", copies), "x")
    copies = share(small_slots[2], total(small_slots[1], "x", copies), "y")
    copies = share(small_slots[3], total(small_slots[2], "y", copies), "z")
    square = jnp.broadcast_to(square + phase_end((0, 1)), (8, 128))
    for place, axis in enumerate("cxyz"):
        parts = share(square_slots[place], square, axis)
        if place == 0:
            whole = total(small_slots[3], "z", copies)
            small_out[...] = whole
            norm_square = jnp.sum(whole[:14] * whole[:14], keepdims=True)
        square = total(square_slots[place], axis, parts)
    square_out[...] = square + norm_square
    for copy in started:
        copy.wait_send()


def run_backward(grad_decoded, norms, extra, held, saved, dp, vocab):
    sizes = grid_of(dp, vocab)
    z, y, x, c = (sizes[axis] for axis in "zyxc")
    names = ("attn_in", "attn_out", "widen", "narrow", "down", "up")
    down, up = held["down"].shape[5:], held["up"].shape[5:]
    tails = (down, up, down, up)
    f32, b16 = jnp.float32, jnp.bfloat16
    anywhere, vmem = pl.BlockSpec(memory_space=pl.ANY), pl.BlockSpec(memory_space=pltpu.VMEM)
    dma = pltpu.SemaphoreType.DMA
    scratch = [pltpu.VMEM(value.shape, value.dtype) for value in saved]
    scratch[2] = pltpu.VMEM((3, ROWS, 1024), f32)
    scratch += [dma((16,)), dma((3,)), pltpu.VMEM((5, 1024, 1024), b16), dma((5,))]
    scratch += [pltpu.VMEM((1024, 512), b16), dma((1,))]
    scratch += [pltpu.VMEM((z, y, x, c) + tail, f32) for tail in tails]
    scratch += [pltpu.VMEM((z, y, x) + tail, f32) for tail in tails]
    for _ in range(2):
        scratch += [pltpu.VMEM((z, y, x) + tail, b16) for tail in tails]
    for lead in (((x - 1, z, y), (y - 1, z, x)), ((y - 1, z), (x - 1, z)), ((z - 1,), (z - 1,))):
        for _ in range(2):
            scratch += [pltpu.VMEM(lead[place % 2] + tail, b16) for place, tail in enumerate(tails)]
    scratch.append(pltpu.VMEM((16, 1024), f32))
    scratch += [pltpu.VMEM((sizes[axis], 16, 1024), f32) for axis in "cxyz"]
    scratch += [pltpu.VMEM((sizes[axis], 8, 128), f32) for axis in "cxyz"]
    scratch += [
        pltpu.VMEM((ROWS, 1024), b16),
        pltpu.VMEM((ROWS, 1024), f32),
        pltpu.VMEM((ROWS, 1024), f32),
        pltpu.VMEM((ROWS, 1024), b16),
        pltpu.VMEM((ROWS, 1024), b16),
        pltpu.VMEM((ROWS, 3072), b16),
    ]
    links = 6 * (x + y + z + c)
    scratch += [dma((links,)), dma((links,))]
    return pl.pallas_call(
        functools.partial(backward_kernel, sizes),
        out_shape=[jax.ShapeDtypeStruct(tail, f32) for tail in tails]
        + [jax.ShapeDtypeStruct((16, 1024), f32), jax.ShapeDtypeStruct((8, 128), f32)],
        in_specs=[vmem] * 3 + [anywhere] * 13,
        out_specs=[vmem] * 6,
        scratch_shapes=scratch,
        compiler_params=pltpu.CompilerParams(
            collective_id=2, has_side_effects=True, vmem_limit_bytes=62 * 2**20
        ),
    )(grad_decoded, norms, extra, *[held[name] for name in names], *saved)


def attend_back(grad_low, queries, key_rows, values, probs, scale):
    grad_heads = split_heads(grad_low)
    grad_probs = jnp.einsum(
        "bqhd,bkhd->bhqk", grad_heads, split_heads(values), preferred_element_type=jnp.float32
    )
    grad_values = jnp.einsum("bhqk,bqhd->bkhd", probs, grad_heads, preferred_element_type=jnp.float32)
    probs = wide(probs)
    grad_scores = low(probs * (grad_probs - jnp.sum(probs * grad_probs, -1, keepdims=True)))
    grad_queries = (
        jnp.einsum("bhqk,bkhd->bqhd", grad_scores, split_heads(key_rows), preferred_element_type=jnp.float32)
        * scale
    )
    grad_keys = (
        jnp.einsum("bhqk,bqhd->bkhd", grad_scores, split_heads(queries), preferred_element_type=jnp.float32)
        * scale
    )
    return tuple(value.reshape(ROWS, -1) for value in (grad_queries, grad_keys, grad_values))


def split_heads(value):
    return value.reshape(MICRO, LEN, HEADS, value.shape[1] // HEADS)


def norm_back(grad_out, normed, inv_std, norm_gain):
    scaled = grad_out * norm_gain
    grad_in = inv_std * (
        scaled
        - jnp.mean(scaled, -1, keepdims=True)
        - normed * jnp.mean(scaled * normed, -1, keepdims=True)
    )
    return grad_in, jnp.sum(grad_out * normed, 0), jnp.sum(grad_out, 0)


def backward(grad_decoded, held, norms, saved):
    qkv_all, probs_all, normed_all, inv_all, feed_in, slopes, bottles = saved
    gains, biases = [None] * 7, [None] * 7

    def norm(grad, which):
        grad, gains[which], biases[which] = norm_back(grad, normed_all[which], inv_all[which, :, :1], norms[which])
        return grad

    def feed(grad, side, which):
        grad_sum = norm(grad, which)
        low_grad = low(grad_sum)
        grad_hidden = low(dot_rows(low_grad, held["narrow"][side]) * wide(slopes[side]))
        grad_bottle = low(BRANCH_SCALE * dot_rows(low_grad, held["up"][side]) * wide(bottles[side, 1]))
        grad_in = grad_sum + dot_rows(grad_hidden, held["widen"][side]) + dot_rows(grad_bottle, held["down"][side])
        grad_up = BRANCH_SCALE * dot_columns(bottles[side, 0], low_grad)
        return grad_in, dot_columns(feed_in[side], grad_bottle), grad_up

    def attend(grad, layer, which):
        grad_sum = norm(grad, which)
        grad_att = low(dot_rows(low(grad_sum), held["attn_out"][layer]))
        qkv = qkv_all[layer]
        probs = probs_all[layer].reshape(MICRO, HEADS, LEN, LEN)
        parts = attend_back(grad_att, qkv[:, :1024], qkv[:, 1024:2048], qkv[:, 2048:], probs, 0.125)
        packed = low(jnp.concatenate(parts, 1))
        w_in = held["attn_in"][layer]
        if layer == 2:
            return grad_sum + dot_rows(packed[:, :1024], w_in[:, :1024]), dot_rows(packed[:, 1024:], w_in[:, 1024:])
        return grad_sum + dot_rows(packed, w_in), None

    grad, down_dec, up_dec = feed(grad_decoded, 1, 6)
    grad, grad_memory = attend(grad, 2, 5)
    grad, _ = attend(grad, 1, 4)
    norm(grad, 3)
    grad, down_enc, up_enc = feed(grad_memory, 0, 2)
    grad, _ = attend(grad, 0, 1)
    norm(grad, 0)
    return down_enc, up_enc, down_dec, up_dec, jnp.stack(gains + biases)


def adam_step(weight, first, second, grad, rate):
    first = BETA_FIRST * first + (1.0 - BETA_FIRST) * grad
    second = BETA_SECOND * second + (1.0 - BETA_SECOND) * grad * grad
    first_hat = first / (1.0 - BETA_FIRST**STEP)
    second_hat = second / (1.0 - BETA_SECOND**STEP)
    weight = weight - rate * (
        first_hat / (jnp.sqrt(second_hat) + ADAM_EPSILON) + WEIGHT_DECAY * weight
    )
    return (first, second, weight)


def head(decoded, vocab_table, target_ids, target_length, seq_scale, groups, vocab_rank):
    rows_local = vocab_table.shape[0]
    key_index = jnp.arange(LEN)
    head_rows = lax.all_gather(decoded, "vocab", axis=0, tiled=True)
    logits = dot_rows(head_rows, vocab_table)
    local_target = target_ids.reshape(-1) - vocab_rank * rows_local
    target_hot = lax.broadcasted_iota(jnp.int32, logits.shape, 1) == local_target[:, None]
    target_logit = jnp.sum(jnp.where(target_hot, logits, 0.0), 1)
    local_max = jnp.max(logits, 1)
    row_max = lax.pmax(local_max, "vocab")
    row_total, row_target = lax.psum(
        (jnp.sum(jnp.exp(logits - row_max[:, None]), 1), target_logit), "vocab"
    )
    log_total = row_max + jnp.log(row_total)
    row_mask = (key_index[None, :] < target_length[:, None]).astype(jnp.float32)
    row_weight = (row_mask * seq_scale[:, None]).reshape(-1)
    row_loss = (log_total - row_target).reshape(-1, LEN) * row_mask
    own_loss = lax.dynamic_slice_in_dim(row_loss, vocab_rank * MICRO, MICRO)
    grad_logits = low(
        row_weight[:, None] * (jnp.exp(logits - log_total[:, None]) - target_hot.astype(jnp.float32))
    )
    grad_decoded = lax.psum_scatter(
        dot(grad_logits, vocab_table).astype(jnp.bfloat16), "vocab", scatter_dimension=0, tiled=True
    ).astype(jnp.float32)
    return grad_decoded, jnp.sum(own_loss, 1)


def local(
    source_ids,
    target_in,
    target_ids,
    source_length,
    target_length,
    task_ids,
    vocab_table,
    positions,
    attention_in,
    attention_out,
    widen_weight,
    narrow_weight,
    adapt_down,
    adapt_up,
    norm_params,
    down_first,
    down_second,
    up_first,
    up_second,
    norm_first,
    norm_second,
):
    dp, groups = lax.axis_size("dp"), lax.axis_size("vocab")
    vocab_rank = lax.axis_index("vocab")
    rows_local, width = vocab_table.shape
    joined_ids = (
        jnp.stack([source_ids.reshape(groups, -1), target_in.reshape(groups, -1)], 1).reshape(-1)
        - vocab_rank * rows_local
    )
    inside = (joined_ids >= 0) & (joined_ids < rows_local)
    picked = jnp.where(
        inside[:, None],
        jnp.take(vocab_table, jnp.clip(joined_ids, 0, rows_local - 1), axis=0),
        jnp.zeros((), jnp.bfloat16),
    ).reshape(groups // 2, 2, 2, ROWS, width)
    task_hot = (task_ids[:, None] == jnp.arange(TASKS)[None, :]).astype(jnp.float32)
    group_counts = jnp.sum(task_hot * target_length[:, None].astype(jnp.float32), 0)
    own = vocab_rank * MICRO
    source_count = lax.dynamic_slice_in_dim(source_length, own, MICRO)
    key_keep = jnp.broadcast_to(
        (jnp.arange(LEN)[None, None, :] < source_count[:, None, None]).astype(jnp.float32), (MICRO, 8, LEN)
    )
    parts = {
        "norms": jnp.concatenate(
            [
                norm_params.T,
                jnp.pad(group_counts, (0, norm_params.shape[1] - TASKS))[:, None],
                jnp.zeros((norm_params.shape[1], 113), jnp.float32),
            ],
            1,
        )[None],
        "attn_in": attention_in,
        "attn_out": attention_out,
        "widen": widen_weight,
        "narrow": narrow_weight,
        "down": low(adapt_down),
        "up": low(adapt_up),
    }
    held, saved = run_forward(parts, picked, positions, key_keep, dp, groups)
    slab = held.pop("norms").reshape(dp, groups, -1, 128)
    task_counts = jnp.sum(slab[:, 0, :TASKS, 14], 0)
    seq_scale = jnp.sum(task_hot * (1.0 / (TASKS * task_counts))[None, :], 1)
    norms = slab.reshape(width, 128)[:, :16].T
    if groups <= 4 and rows_local % TILE == 0:
        own_length = lax.dynamic_slice_in_dim(target_length, own, MICRO)
        own_mask = (jnp.arange(LEN)[None, :] < own_length[:, None]).astype(jnp.float32)
        own_weight = own_mask * lax.dynamic_slice_in_dim(seq_scale, own, MICRO)[:, None]
        grad_decoded, row_loss = run_head(saved[7], target_ids, own_weight, vocab_table, dp, groups)
        own_loss = jnp.sum(row_loss[0].reshape(MICRO, LEN) * own_mask, 1)
    else:
        grad_decoded, own_loss = head(
            saved[7], vocab_table, target_ids, target_length, seq_scale, groups, vocab_rank
        )
    task_local = jnp.sum(lax.dynamic_slice_in_dim(task_hot, own, MICRO) * own_loss[:, None], 0)
    task_row = jnp.pad(task_local[None], ((0, 1), (0, width - TASKS)))
    if groups <= 4:
        extra = jnp.pad(task_row, ((14, 0), (0, 0)))
        down_enc, up_enc, down_dec, up_dec, small, square = run_backward(
            grad_decoded, norms, extra, held, saved[:7], dp, groups
        )
    else:
        held = {name: value.reshape(value.shape[0], -1, value.shape[-1]) for name, value in held.items()}
        down_enc, up_enc, down_dec, up_dec, norm_grads = backward(grad_decoded, held, norms, saved[:7])
        small = jnp.concatenate([norm_grads, task_row], 0)
        down_enc, up_enc, down_dec, up_dec, small, square = reduce_gradients(
            down_enc, up_enc, down_dec, up_dec, small, dp, groups
        )
    shard_down = jnp.stack([down_enc, down_dec])
    shard_up = jnp.stack([up_enc, up_dec])
    full_norm, task_sums = small[:14], small[14, :TASKS]
    cut = norm_params.shape[1]
    shard_norm = lax.dynamic_slice_in_dim(full_norm, lax.axis_index(("dp", "vocab")) * cut, cut, 1)
    grad_norm = jnp.sqrt(square[0, 0])
    factor = CLIP_LIMIT / jnp.maximum(grad_norm, CLIP_LIMIT)
    down_new = adam_step(adapt_down, down_first, down_second, shard_down * factor, RATE_ADAPTER)
    up_new = adam_step(adapt_up, up_first, up_second, shard_up * factor, RATE_ADAPTER)
    norm_new = adam_step(norm_params, norm_first, norm_second, shard_norm * factor, RATE_NORMS)
    return (*down_new, *up_new, *norm_new, grad_norm, task_sums, task_counts)


def solution(mesh):
    return jax.shard_map(
        local,
        mesh=mesh,
        in_specs=(
            P("dp", None),
            P("dp", None),
            P("dp", None),
            P("dp"),
            P("dp"),
            P("dp"),
            P("vocab", None),
            P(),
            P(None, ("dp", "vocab"), None),
            P(None, ("dp", "vocab"), None),
            P(None, ("dp", "vocab"), None),
            P(None, ("dp", "vocab"), None),
            P(None, ("dp", "vocab"), None),
            P(None, ("dp", "vocab"), None),
            P(None, ("dp", "vocab")),
            P(None, ("dp", "vocab"), None),
            P(None, ("dp", "vocab"), None),
            P(None, ("dp", "vocab"), None),
            P(None, ("dp", "vocab"), None),
            P(None, ("dp", "vocab")),
            P(None, ("dp", "vocab")),
        ),
        out_specs=(
            P(None, ("dp", "vocab"), None),
            P(None, ("dp", "vocab"), None),
            P(None, ("dp", "vocab"), None),
            P(None, ("dp", "vocab"), None),
            P(None, ("dp", "vocab"), None),
            P(None, ("dp", "vocab"), None),
            P(None, ("dp", "vocab")),
            P(None, ("dp", "vocab")),
            P(None, ("dp", "vocab")),
            P(),
            P(),
            P(),
        ),
        check_vma=False,
    )
```

```python
import functools

import jax
import jax.numpy as jnp
from jax import lax
from jax.experimental import pallas as pl
from jax.experimental.pallas import tpu as pltpu
from jax.sharding import PartitionSpec as P

MESH_ID = pl.DeviceIdType.MESH
TASKS = 4
STEP = 10
CLIP_LIMIT = 0.002
BETA_FIRST = 0.9
BETA_SECOND = 0.999
ADAM_EPSILON = 1e-08
WEIGHT_DECAY = 0.01
RATE_ADAPTER = 0.02
RATE_NORMS = 0.2


def grid_of(dp, vocab):
    cores = 2
    across = vocab // cores
    return {"z": dp // across, "y": across, "x": across, "c": cores}


def position(sizes):
    dp, vocab = lax.axis_index("dp"), lax.axis_index("vocab")
    return {
        "z": dp // sizes["y"],
        "y": dp % sizes["y"],
        "x": vocab // sizes["c"],
        "c": vocab % sizes["c"],
    }


def device_at(here, sizes, **moved):
    at = dict(here)
    at.update(moved)
    return (at["z"] * sizes["y"] + at["y"], at["x"] * sizes["c"] + at["c"])


def lines_barrier(here, sizes):
    barrier = pltpu.get_barrier_semaphore()
    peers = 0
    for axis in "zyxc":
        for step in range(1, sizes[axis]):
            other = (here[axis] + step) % sizes[axis]
            pl.semaphore_signal(
                barrier, inc=1, device_id=device_at(here, sizes, **{axis: other}), device_id_type=MESH_ID
            )
            peers += 1
    pl.semaphore_wait(barrier, peers)


def reduce_kernel(sizes, *refs):
    grads = refs[0:4]
    small = refs[4]
    shards = refs[5:9]
    small_out, square_out = refs[9:11]
    sums, core_send, core_recv = refs[11:15], refs[15:19], refs[19:23]
    wide_send, wide_recv, mid_send, mid_recv, last_send, last_recv = (
        refs[23:27], refs[27:31], refs[31:35], refs[35:39], refs[39:43], refs[43:47]
    )
    small_slots, square_slots = refs[47:51], refs[51:55]
    send_sem, recv_sem = refs[55:57]
    here = position(sizes)
    lines_barrier(here, sizes)
    used = [0]
    started = []

    def copy_to(src, dst, **moved):
        number = used[0]
        used[0] += 1
        copy = pltpu.make_async_remote_copy(
            src_ref=src,
            dst_ref=dst,
            send_sem=send_sem.at[number],
            recv_sem=recv_sem.at[number],
            device_id=device_at(here, sizes, **moved),
            device_id_type=MESH_ID,
        )
        copy.start()
        started.append(copy)
        return copy

    def low(value):
        return value.astype(jnp.bfloat16)

    mine = here["c"]

    def share(slots, value, axis):
        slots[here[axis]] = value
        return [
            copy_to(slots.at[here[axis]], slots.at[here[axis]], **{axis: (here[axis] + step) % sizes[axis]})
            for step in range(1, sizes[axis])
        ]

    def total(slots, axis, copies):
        for copy in copies:
            copy.wait_recv()
        value = slots[0]
        for index in range(1, sizes[axis]):
            value = value + slots[index]
        return value

    first = []
    for part in range(4):
        core_send[part][...] = low(grads[part][:, :, :, 1 - mine])
        first.append(copy_to(core_send[part], core_recv[part], c=1 - mine))
    copies = share(small_slots[0], small[...], "c")
    plans = (("x", "y"), ("x", "y"), ("y", "x"), ("y", "x"))

    second = []
    for part in range(4):
        first[part].wait_recv()
        sums[part][...] = grads[part][:, :, :, mine] + core_recv[part][...].astype(jnp.float32)
        axis = plans[part][0]
        found = []
        for step in range(1, sizes[axis]):
            other = (here[axis] + step) % sizes[axis]
            piece = sums[part][:, :, other] if axis == "x" else sums[part][:, other]
            wide_send[part][step - 1] = low(piece)
            found.append(copy_to(wide_send[part].at[step - 1], wide_recv[part].at[step - 1], **{axis: other}))
        second.append(found)
    copies = share(small_slots[1], total(small_slots[0], "c", copies), "x")
    third = []
    for part in range(4):
        axis, later = plans[part]
        held = sums[part].at[:, :, here["x"]] if axis == "x" else sums[part].at[:, here["y"]]
        value = held[...]
        for step, copy in enumerate(second[part]):
            copy.wait_recv()
            value = value + wide_recv[part][step].astype(jnp.float32)
        held[...] = value
        found = []
        for step in range(1, sizes[later]):
            other = (here[later] + step) % sizes[later]
            mid_send[part][step - 1] = low(held[:, other])
            found.append(copy_to(mid_send[part].at[step - 1], mid_recv[part].at[step - 1], **{later: other}))
        third.append(found)
    copies = share(small_slots[2], total(small_slots[1], "x", copies), "y")
    fourth = []
    for part in range(4):
        axis, later = plans[part]
        held = sums[part].at[:, here["y"], here["x"]]
        value = held[...]
        for step, copy in enumerate(third[part]):
            copy.wait_recv()
            value = value + mid_recv[part][step].astype(jnp.float32)
        held[...] = value
        found = []
        for step in range(1, sizes["z"]):
            other = (here["z"] + step) % sizes["z"]
            last_send[part][step - 1] = low(held[other])
            found.append(copy_to(last_send[part].at[step - 1], last_recv[part].at[step - 1], z=other))
        fourth.append(found)
    copies = share(small_slots[3], total(small_slots[2], "y", copies), "z")
    square = jnp.zeros((1, 1), jnp.float32)
    for part in range(4):
        value = sums[part][here["z"], here["y"], here["x"]]
        for step, copy in enumerate(fourth[part]):
            copy.wait_recv()
            value = value + last_recv[part][step].astype(jnp.float32)
        shards[part][...] = value
        square = square + jnp.sum(value * value, keepdims=True)
    square = jnp.broadcast_to(square, (8, 128))
    for place, axis in enumerate("cxyz"):
        parts = share(square_slots[place], square, axis)
        if place == 0:
            whole = total(small_slots[3], "z", copies)
            small_out[...] = whole
            norm_square = jnp.sum(whole[:14] * whole[:14], keepdims=True)
        square = total(square_slots[place], axis, parts)
    square_out[...] = square + norm_square
    for copy in started:
        copy.wait_send()


def reduce_gradients(down_enc, up_enc, down_dec, up_dec, small, dp, vocab):
    sizes = grid_of(dp, vocab)
    grid = tuple(sizes[axis] for axis in "zyxc")
    whole = dp * vocab
    grads = [
        value.reshape(grid + (value.shape[0] // whole, value.shape[1]))
        for value in (down_enc, up_enc, down_dec, up_dec)
    ]
    z, y, x, c = grid
    tails = [value.shape[4:] for value in grads]
    vmem = pl.BlockSpec(memory_space=pltpu.VMEM)
    scratch = [pltpu.VMEM((z, y, x) + tail, jnp.float32) for tail in tails]
    for _ in range(2):
        scratch += [pltpu.VMEM((z, y, x) + tail, jnp.bfloat16) for tail in tails]
    for _ in range(2):
        scratch += [
            pltpu.VMEM(((x - 1, z, y) if place < 2 else (y - 1, z, x)) + tail, jnp.bfloat16)
            for place, tail in enumerate(tails)
        ]
    for _ in range(2):
        scratch += [
            pltpu.VMEM(((y - 1, z) if place < 2 else (x - 1, z)) + tail, jnp.bfloat16)
            for place, tail in enumerate(tails)
        ]
    for _ in range(2):
        scratch += [pltpu.VMEM((z - 1,) + tail, jnp.bfloat16) for tail in tails]
    scratch += [pltpu.VMEM((sizes[axis],) + small.shape, jnp.float32) for axis in "cxyz"]
    scratch += [pltpu.VMEM((sizes[axis], 8, 128), jnp.float32) for axis in "cxyz"]
    links = 6 * (x + y + z + c)
    scratch += [pltpu.SemaphoreType.DMA((links,)), pltpu.SemaphoreType.DMA((links,))]
    return pl.pallas_call(
        functools.partial(reduce_kernel, sizes),
        out_shape=[jax.ShapeDtypeStruct(tail, jnp.float32) for tail in tails]
        + [jax.ShapeDtypeStruct(small.shape, jnp.float32), jax.ShapeDtypeStruct((8, 128), jnp.float32)],
        in_specs=[vmem] * 5,
        out_specs=[vmem] * 6,
        scratch_shapes=scratch,
        compiler_params=pltpu.CompilerParams(
            collective_id=1, has_side_effects=True, vmem_limit_bytes=48 * 2**20
        ),
    )(*grads, small)


ORDERS = ("xzy", "yzx", "zyx", "zxy")
SEQUENCE = (
    ("norms", 0), ("attn_in", 0), ("attn_out", 0), ("down", 0), ("widen", 0), ("up", 0), ("narrow", 0),
    ("attn_in", 1), ("attn_out", 1), ("attn_in", 2), ("attn_out", 2), ("down", 1), ("widen", 1), ("up", 1),
    ("narrow", 1),
)
COLUMNS = {"norms": 128, "attn_in": 512, "attn_out": 512, "down": 512, "widen": 512, "up": 512, "narrow": 256}
PARTS = {("narrow", 0): 2, ("narrow", 1): 4}
LAG_Z = (2.5, 2.5, 2.5)
LAG_LINE = (8.0, 3.5, 5.5)
LAG_CORE = 2.75
PACE = 0.5
SETTLE = 0.8
HEADS = 16
LEN = 128
MICRO = 2
ROWS = 256
NORM_EPS = 1e-05
NEGATIVE = -1000000000.0
BRANCH_SCALE = 4.0


def hops_of(order, sizes):
    return [(axis, hop) for axis in order for hop in range(1, sizes[axis])]


def plan_units(shapes, names, sizes):
    devices = sizes["z"] * sizes["y"] * sizes["x"] * sizes["c"]
    units, clock = [], 0.0
    load = {"x": 0.85, "y": 0.0, "z": 0.0}
    for name, layer in SEQUENCE:
        if name not in names:
            continue
        rows, columns = shapes[name]
        step = min(COLUMNS[name], columns)
        parts = PARTS.get((name, layer), 1)
        if rows % (16 * parts):
            parts = 1
        height = rows // parts
        for left in range(0, columns, step):
            for top in range(0, rows, height):
                size = height * devices * step / 2**19
                best = None
                for order in ORDERS:
                    after, held = dict(load), 1
                    for axis in order:
                        after[axis] += size * held * (sizes[axis] - 1) * sizes["c"] / devices
                        held *= sizes[axis]
                    score = sum(value**4 for value in after.values())
                    if best is None or score < best[0]:
                        best = (score, order, after)
                load = best[2]
                units.append((name, layer, left, step, top, height, clock, best[1]))
                clock += size
    return units


def stage_clocks(unit, sizes):
    order = unit[7]
    found = [0.0]
    for axis, _ in hops_of(order, sizes):
        found.append(found[-1] + (LAG_Z if axis == "z" else LAG_LINE)[order.index(axis)])
    found.append(found[-1] + LAG_CORE)
    scale = min(1.0, 0.8 + unit[6] / 20.0)
    return [unit[6] + scale * value for value in found]


def dot(left, right):
    return jnp.dot(left, right, preferred_element_type=jnp.float32)


def dot_rows(left, right):
    return lax.dot_general(left, right, (((1,), (1,)), ((), ())), preferred_element_type=jnp.float32)


def dot_columns(left, right):
    return lax.dot_general(left, right, (((0,), (0,)), ((), ())), preferred_element_type=jnp.float32)


def low(value):
    return value.astype(jnp.bfloat16)


def wide(value):
    return value.astype(jnp.float32)


def norm_rows(value, gain, bias):
    centred = value - jnp.mean(value, -1, keepdims=True)
    inv_std = lax.rsqrt(jnp.mean(centred * centred, -1, keepdims=True) + NORM_EPS)
    normed = centred * inv_std
    return normed * gain + bias, normed, inv_std


def gelu_pair(value):
    half = 0.5 * (1.0 + lax.erf(value * 0.7071067811865476))
    return value * half, half + value * jnp.exp(-0.5 * value * value) * 0.3989422804014327


def lane_masks():
    lanes = lax.broadcasted_iota(jnp.int32, (LEN, 128), 1)
    first = (lanes < 64).astype(jnp.float32).astype(jnp.bfloat16)
    return first, (lanes >= 64).astype(jnp.float32).astype(jnp.bfloat16)


def stack_heads(value, masks):
    return jnp.concatenate([value * masks[0], value * masks[1]], 0)


def attend_pair(qkv, probs, attended, seq, pair, keep):
    masks = lane_masks()
    rows = pl.ds(pl.multiple_of(seq * LEN, LEN), LEN)

    def columns(part):
        return pl.ds(pl.multiple_of(part * 1024 + pair * 128, 128), 128)

    queries, keys, values = (qkv[rows, columns(part)] for part in range(3))
    scores = dot_rows(stack_heads(queries, masks), keys) * 0.125
    scores = jnp.where(keep(seq), scores, NEGATIVE)
    spread = jnp.exp(scores - jnp.max(scores, -1, keepdims=True))
    chance = low(spread / jnp.sum(spread, -1, keepdims=True))
    probs[seq, pair] = chance
    side = jnp.concatenate([chance[:LEN], chance[LEN:]], 1)
    attended[rows, columns(0)] = low(dot(side, stack_heads(values, masks)))


def forward_kernel(sizes, units, names, *refs):
    refs = list(refs)

    def take(count):
        found = refs[:count]
        del refs[:count]
        return found

    count = len(names)
    ins = dict(zip(names, take(count)))
    picked, places, key_keep = take(3)
    extra_up = None if "up" in names else take(1)[0]
    outs = dict(zip(names, take(count)))
    saved_out = take(8)
    send_sem, recv_sem, local_sem, sib_send, sib_recv = take(5)
    saved = take(8)
    qkv_all, probs_all, normed_all, inv_all, feed_in, slopes, bottles, decoded = saved
    embed_sem, embed_here, embed_core, embed_line = take(4)
    norm_tile, norms = take(2)
    stream, stream_low, memory, attended, branch, hidden = take(6)
    tiles, tall_tiles, tile_sem, tall_sem, save_sem = take(5)
    here = position(sizes)

    def at_device(**moved):
        return device_at(here, sizes, **moved)

    barrier = pltpu.get_barrier_semaphore()
    pl.semaphore_signal(barrier, inc=1, device_id=at_device(c=1 - here["c"]), device_id_type=MESH_ID)
    peers = jnp.int32(1)
    for step in range(1, sizes["x"]):
        other = (here["x"] + step) % sizes["x"]
        pl.semaphore_signal(barrier, inc=1, device_id=at_device(x=other), device_id_type=MESH_ID)
        peers = peers + 1
    for axis in "zy":
        for step in (-1, 1):
            ok = (here[axis] + step >= 0) & (here[axis] + step < sizes[axis])
            peers = peers + ok.astype(jnp.int32)

            @pl.when(ok)
            def _(axis=axis, step=step):
                pl.semaphore_signal(
                    barrier, inc=1, device_id=at_device(**{axis: here[axis] + step}), device_id_type=MESH_ID
                )

    pl.semaphore_wait(barrier, peers)

    everything = slice(None)

    def own_source(unit):
        name, layer, left, width, top, height = unit[:6]
        return ins[name].at[layer, pl.ds(top, height), pl.ds(left, width)]

    def piece(unit, index):
        name, layer, left, width, top, height = unit[:6]
        return outs[name].at[(layer,) + index + (pl.ds(top, height), pl.ds(left, width))]

    def view(unit, order, axis, coordinate):
        place = order.index(axis)
        at = {other: everything if order.index(other) < place else here[other] for other in "zyx"}
        at[axis] = coordinate
        return piece(unit, (at["z"], at["y"], at["x"], here["c"]))

    def sends(number, stage):
        unit, order = units[number], units[number][7]
        axis, hop = hops_of(order, sizes)[stage]
        size, mine = sizes[axis], here[axis]
        first = order.index(axis) == 0
        found = []
        for way, step in enumerate((1, -1)):
            origin = mine - step * (hop - 1)
            ok = (origin >= 0) & (origin < size) & (mine + step >= 0) & (mine + step < size)
            origin_r = mine - step * hop
            ok_r = (origin_r >= 0) & (origin_r < size)

            def build(receive, step=step, way=way, origin=origin, origin_r=origin_r):
                which = origin_r if receive else origin
                fresh = first and hop == 1 and not receive
                return pltpu.make_async_remote_copy(
                    src_ref=own_source(unit) if fresh else view(unit, order, axis, which),
                    dst_ref=view(unit, order, axis, which),
                    send_sem=send_sem.at[number, stage * 2 + way],
                    recv_sem=recv_sem.at[number, stage * 2 + way],
                    device_id=at_device(**{axis: mine + step}),
                    device_id_type=MESH_ID,
                )

            found.append((ok, ok_r, build))
        return found

    def local_copy(number):
        index = tuple(here[axis] for axis in "zyxc")
        return pltpu.make_async_copy(own_source(units[number]), piece(units[number], index), local_sem.at[number])

    def sibling(number):
        plane = piece(units[number], (everything, everything, everything, here["c"]))
        return pltpu.make_async_remote_copy(
            src_ref=plane,
            dst_ref=plane,
            send_sem=sib_send.at[number],
            recv_sem=sib_recv.at[number],
            device_id=at_device(c=1 - here["c"]),
            device_id_type=MESH_ID,
        )

    depth = sum(sizes[axis] - 1 for axis in "zyx")

    def comm_step(number, stage):
        if stage == 0:
            local_copy(number).start()
        if 1 <= stage <= depth:
            for _, ok_r, build in sends(number, stage - 1):

                @pl.when(ok_r)
                def _(build=build):
                    build(True).wait_recv()

        if stage == sizes[units[number][7][0]] - 1:
            local_copy(number).wait()
        if stage < depth:
            for ok, _, build in sends(number, stage):

                @pl.when(ok)
                def _(build=build):
                    build(False).start()

        if stage == depth:
            sibling(number).start()
        if stage == depth + 1:
            sibling(number).wait_recv()

    mine, column = here["c"], here["x"]

    def embed_first(group):
        return pltpu.make_async_remote_copy(
            src_ref=picked.at[:, 1 - mine, group],
            dst_ref=embed_core.at[group],
            send_sem=embed_sem.at[0, group],
            recv_sem=embed_sem.at[1, group],
            device_id=at_device(c=1 - mine),
            device_id_type=MESH_ID,
        )

    def embed_local(group):
        return pltpu.make_async_copy(picked.at[:, mine, group], embed_here.at[group], embed_sem.at[2, group])

    def embed_second(group, step):
        other = (column + step) % sizes["x"]
        return pltpu.make_async_remote_copy(
            src_ref=embed_here.at[group, other],
            dst_ref=embed_line.at[group, step - 1],
            send_sem=embed_sem.at[2 + step * 2 - 1, group],
            recv_sem=embed_sem.at[2 + step * 2, group],
            device_id=at_device(x=other),
            device_id_type=MESH_ID,
        )

    def embed_pass(group):
        embed_first(group).wait_recv()
        embed_local(group).wait()
        embed_here[group] = embed_here[group] + embed_core[group]
        for step in range(1, sizes["x"]):
            embed_second(group, step).start()

    def embed_rows(group):
        rows = wide(embed_here[group, column])
        for step in range(1, sizes["x"]):
            embed_second(group, step).wait_recv()
            rows = rows + wide(embed_line[group, step - 1])
        place = wide(places[group])
        return rows + jnp.concatenate([place] * MICRO, 0)

    saves = []

    def save(place, index):
        def build(number=len(saves)):
            return pltpu.make_async_copy(
                saved[place].at[index] if index else saved[place],
                saved_out[place].at[index] if index else saved_out[place],
                save_sem.at[number],
            )

        saves.append(build)
        build().start()

    def norm_step(value, which, side):
        result, normed, inv_std = norm_rows(value, norms[which : which + 1, :], norms[which + 7 : which + 8, :])
        normed_all[which] = normed
        inv_all[which] = jnp.broadcast_to(inv_std, (ROWS, 128))
        save(2, (which,))
        save(3, (which,))
        stream[side] = result
        stream_low[side] = low(result)

    def begin(side):
        def run():
            if side == 0:
                copy = pltpu.make_async_copy(outs["norms"].at[0], norm_tile, tile_sem.at[len(tiles_used)])
                copy.start()
                copy.wait()
                columns = norm_tile[...].reshape(-1, 128)
                norms[...] = columns.T[:16]
            norm_step(embed_rows(side), 3 * side, side)

        return run

    tiles_used = [None] * tiles.shape[0]

    def project(which, left, side, from_memory):
        def run(tile):
            source = memory[...] if from_memory else stream_low[side]
            qkv_all[which, :, pl.ds(left, 512)] = low(dot(source, tile()))

        return run

    def attention(which, start, keep):
        def run():
            def body(number, _):
                seq, pair = number // 8, number % 8
                attend_pair(qkv_all.at[which], probs_all.at[which], attended, seq, pair, keep)
                return 0

            lax.fori_loop(start, start + 4, body, 0)

        return run

    def project_out(left):
        def run(tile):
            branch[:, pl.ds(left, 512)] = dot(attended[...], tile())

        return run

    def finish_attention(which, norm, side):
        def run():
            save(0, (which,))
            save(1, (which,))
            norm_step(stream[side] + branch[...], norm, side)

        return run

    def narrow_down(side):
        def run(tile):
            feed_in[side] = stream_low[side]
            value, slope = gelu_pair(dot(stream_low[side], tile()))
            bottles[side, 0] = low(value)
            bottles[side, 1] = low(slope)
            save(4, (side,))
            save(6, (side,))

        return run

    def widen(left, side):
        def run(tile):
            value, slope = gelu_pair(dot(stream_low[side], tile()))
            hidden[:, pl.ds(left, 512)] = low(value)
            slopes[side, :, pl.ds(left, 512)] = low(slope)

        return run

    def raise_up(left, side):
        def run(tile):
            branch[:, pl.ds(left, 512)] = BRANCH_SCALE * dot(bottles[side, 0], tile())

        return run

    def narrow(left, side):
        def run(tile):
            branch[:, pl.ds(left, 256)] += dot(hidden[...], tile())

        return run

    def finish_feed(norm, side):
        def run():
            save(5, (side,))
            norm_step(stream[side] + branch[...], norm, side)
            if side == 0:
                memory[...] = stream_low[0]
            else:
                decoded[...] = stream_low[1]
                save(7, ())

        return run

    def source_keep(seq):
        return jnp.broadcast_to(key_keep[seq, 0:1, :] > 0.0, (2 * LEN, LEN))

    def causal_keep(seq):
        query = lax.broadcasted_iota(jnp.int32, (2 * LEN, LEN), 0) % LEN
        return lax.broadcasted_iota(jnp.int32, (2 * LEN, LEN), 1) <= query

    steps = []
    members = {}
    for number, unit in enumerate(units):
        members.setdefault(unit[:3], []).append(number)

    def add(run, cost, unit=None, clock=0.0):
        steps.append((unit, cost, clock, run))

    def attention_steps(which, norm, side, keep):
        for left in range(0, 3072, 512):
            from_memory = which == 2 and left >= 1024
            add(project(which, left, side, from_memory), 0.6, ("attn_in", which, left))
        for start in range(0, 16, 4):
            add(attention(which, start, keep), 2.0)
        for left in range(0, 1024, 512):
            add(project_out(left), 0.6, ("attn_out", which, left))
        add(finish_attention(which, norm, side), 1.0)

    def feed_steps(norm, side):
        add(narrow_down(side), 1.3, ("down", side, 0))
        for left in range(0, 4096, 512):
            add(widen(left, side), 1.3, ("widen", side, left))
        for left in range(0, 1024, 512):
            if "up" in names:
                add(raise_up(left, side), 0.4, ("up", side, left))
            else:
                part = functools.partial(lambda left, side: extra_up[side, :, pl.ds(left, 512)], left, side)
                add(functools.partial(raise_up(left, side), part), 0.4)
        for left in range(0, 1024, 256):
            add(narrow(left, side), 1.0, ("narrow", side, left))
        add(finish_feed(norm, side), 1.0)

    add(begin(0), 2.0, ("norms", 0, 0), 8.0)
    attention_steps(0, 1, 0, source_keep)
    feed_steps(2, 0)
    add(begin(1), 1.5, None, 20.0)
    attention_steps(1, 4, 1, causal_keep)
    attention_steps(2, 5, 1, source_keep)
    feed_steps(6, 1)

    loads = [step[0] for step in steps if step[0] is not None and step[0][0] != "norms"]
    slot_of, rings = {}, {"tall": [], "flat": []}
    for unit in loads:
        kind = "tall" if unit[0] == "narrow" else "flat"
        ring = rings[kind]
        size = (tall_tiles if kind == "tall" else tiles).shape[0]
        slot_of[unit] = (kind, len(ring) % size, ring[len(ring) - size] if len(ring) >= size else None)
        ring.append(unit)

    def tile_parts(unit):
        kind, slot, _ = slot_of[unit]
        name, layer, left = unit
        width = units[members[unit][0]][3]
        source = outs[name].at[layer, :, :, :, :, :, pl.ds(left, width)]
        buffer = (tall_tiles if kind == "tall" else tiles).at[slot]
        sem = (tall_sem if kind == "tall" else tile_sem).at[slot]
        rows = ins[name].shape[1] * sizes["z"] * sizes["y"] * sizes["x"] * sizes["c"]
        target = buffer.at[pl.ds(0, rows)]
        shape = tuple(sizes[axis] for axis in "zyxc") + (ins[name].shape[1], width)
        return pltpu.make_async_copy(source, target.reshape(shape), sem), target

    complete, loaded, done, moment = set(), {}, set(), [0.0]
    waiting = list(loads)

    def try_loads():
        while waiting:
            unit = waiting[0]
            before = slot_of[unit][2]
            if unit not in complete or (before is not None and before not in done):
                return
            tile_parts(unit)[0].start()
            loaded[unit] = moment[0]
            waiting.pop(0)

    queue = list(steps)

    def run_step():
        unit, cost, _, run = queue.pop(0)
        if unit is None or unit[0] == "norms":
            run()
        else:
            copy, target = tile_parts(unit)
            copy.wait()
            run(lambda: target[...])
            done.add(unit)
        try_loads()
        return cost

    def ready(clock):
        if not queue:
            return False
        unit, _, earliest, _ = queue[0]
        if earliest > clock:
            return False
        if unit is None:
            return True
        if unit[0] == "norms":
            return unit in complete
        return unit in loaded and clock - loaded[unit] >= SETTLE

    for group in range(2):
        embed_first(group).start()
        embed_local(group).start()
    events = sorted(
        (clock, -stage, number)
        for number, unit in enumerate(units)
        for stage, clock in enumerate(stage_clocks(unit, sizes))
    )
    embed_done, credit, last, arrived = [], 0.0, 0.0, set()
    for clock, minus, number in events:
        stage, moment[0] = -minus, clock
        comm_step(number, stage)
        for group in range(2):
            if group not in embed_done and clock >= 1.5 + 1.5 * group:
                embed_done.append(group)
                embed_pass(group)
        if stage == depth + 1:
            arrived.add(number)
            block = units[number][:3]
            if all(part in arrived for part in members[block]):
                complete.add(block)
                try_loads()
        credit = min(credit + 3.7 * PACE * (clock - last), 4.0)
        last = clock
        while ready(clock) and credit > 0.0:
            credit -= run_step()
    while queue:
        run_step()
    for build in saves:
        build().wait()
    for group in range(2):
        embed_first(group).wait_send()
        for step in range(1, sizes["x"]):
            embed_second(group, step).wait_send()
    for number in range(len(units)):
        sibling(number).wait_send()
        for stage in range(depth):
            for ok, _, build in sends(number, stage):

                @pl.when(ok)
                def _(build=build):
                    build(False).wait_send()


def run_forward(arrays, picked, places, key_keep, dp, vocab):
    sizes = grid_of(dp, vocab)
    grid = tuple(sizes[axis] for axis in "zyxc")
    extra = []
    arrays = dict(arrays)
    if arrays["up"].shape[1] % 8:
        extra = [lax.all_gather(arrays.pop("up"), ("dp", "vocab"), axis=1, tiled=True)]
    names = list(arrays)
    shapes = {name: arrays[name].shape[1:] for name in names}
    units = plan_units(shapes, names, sizes)
    depth = sum(sizes[axis] - 1 for axis in "zyx")
    anywhere, vmem = pl.BlockSpec(memory_space=pl.ANY), pl.BlockSpec(memory_space=pltpu.VMEM)
    f32, b16 = jnp.float32, jnp.bfloat16
    saved = [
        ((3, ROWS, 3072), b16),
        ((3, MICRO, 8, 2 * LEN, LEN), b16),
        ((7, ROWS, 1024), f32),
        ((7, ROWS, 128), f32),
        ((2, ROWS, 1024), b16),
        ((2, ROWS, 4096), b16),
        ((2, 2, ROWS, 512), b16),
        ((ROWS, 1024), b16),
    ]
    out_shape = [
        jax.ShapeDtypeStruct((arrays[name].shape[0],) + grid + arrays[name].shape[1:], arrays[name].dtype)
        for name in names
    ] + [jax.ShapeDtypeStruct(shape, kind) for shape, kind in saved]
    x, n = sizes["x"], len(units)
    dma = pltpu.SemaphoreType.DMA
    out = pl.pallas_call(
        functools.partial(forward_kernel, sizes, units, names),
        out_shape=out_shape,
        in_specs=[anywhere] * (len(names) + 1) + [vmem] * (2 + len(extra)),
        out_specs=[anywhere] * len(out_shape),
        scratch_shapes=[dma((n, 2 * depth)), dma((n, 2 * depth)), dma((n,)), dma((n,)), dma((n,))]
        + [pltpu.VMEM(shape, kind) for shape, kind in saved]
        + [
            dma((3 + 2 * x, 2)),
            pltpu.VMEM((2, x, ROWS, 1024), b16),
            pltpu.VMEM((2, x, ROWS, 1024), b16),
            pltpu.VMEM((2, x - 1, ROWS, 1024), b16),
            pltpu.VMEM(grid + arrays["norms"].shape[1:], f32),
            pltpu.VMEM((16, 1024), f32),
            pltpu.VMEM((2, ROWS, 1024), f32),
            pltpu.VMEM((2, ROWS, 1024), b16),
            pltpu.VMEM((ROWS, 1024), b16),
            pltpu.VMEM((ROWS, 1024), b16),
            pltpu.VMEM((ROWS, 1024), f32),
            pltpu.VMEM((ROWS, 4096), b16),
            pltpu.VMEM((6, 1024, 512), b16),
            pltpu.VMEM((3, 4096, 256), b16),
            dma((7,)),
            dma((3,)),
            dma((32,)),
        ],
        compiler_params=pltpu.CompilerParams(
            collective_id=0, has_side_effects=True, vmem_limit_bytes=61 * 2**20
        ),
    )(*[arrays[name] for name in names], picked, places, key_keep, *extra)
    held = dict(zip(names, out[: len(names)]))
    if extra:
        held["up"] = extra[0]
    return held, out[len(names) :]


TILE = 1280


def head_kernel(sizes, *refs):
    decoded, targets, weight, table_hbm, grad_out, loss_out = refs[:6]
    rows, table, logits, partial, core_send, core_part, line_send, line_part, stats = refs[6:15]
    table_sem, row_sem, stat_sem, core_sem, line_sem, send_sem = refs[15:]
    here = position(sizes)
    mine, column, cores, across = here["c"], here["x"], sizes["c"], sizes["x"]
    owners = across * cores
    me, twin = column * cores + mine, column * cores + 1 - mine
    count = table.shape[0]
    steps = count // TILE

    def table_copy(number):
        part = pl.ds(number * TILE, TILE)
        return pltpu.make_async_copy(table_hbm.at[part], table.at[part], table_sem.at[number])

    for number in range(steps):
        table_copy(number).start()
    barrier = pltpu.get_barrier_semaphore()
    for step in range(1, owners):
        other = (me + step) % owners
        pl.semaphore_signal(
            barrier,
            inc=1,
            device_id=device_at(here, sizes, x=other // cores, c=other % cores),
            device_id_type=MESH_ID,
        )
    pl.semaphore_wait(barrier, owners - 1)
    started = []

    def remote(src, dst, arrival, **moved):
        copy = pltpu.make_async_remote_copy(
            src_ref=src,
            dst_ref=dst,
            send_sem=send_sem.at[len(started)],
            recv_sem=arrival,
            device_id=device_at(here, sizes, **moved),
            device_id_type=MESH_ID,
        )
        copy.start()
        started.append(copy)

    def arrived(ref, arrival):
        pltpu.make_async_remote_copy(
            src_ref=ref,
            dst_ref=ref,
            send_sem=send_sem.at[0],
            recv_sem=arrival,
            device_id=device_at(here, sizes, c=1 - mine),
            device_id_type=MESH_ID,
        ).wait_recv()

    def far(step, core):
        return (column + step) % across * cores + core

    rows[me] = decoded[...]
    for step in range(1, across):
        remote(rows.at[me], rows.at[me], row_sem.at[me], x=(column + step) % across)
    remote(rows.at[me], rows.at[me], row_sem.at[me], c=1 - mine)
    lane = lax.broadcasted_iota(jnp.int32, (ROWS, 128), 1)

    def first_pass(block, fresh=False):
        wanted = targets[block] - me * count

        def body(number, carry):
            top, spread, hit = carry
            start = pl.multiple_of(number * TILE, TILE)
            if fresh:
                part = pl.ds(start, TILE)
                pltpu.make_async_copy(table_hbm.at[part], table.at[part], table_sem.at[number]).wait()
            values = dot_rows(rows[block], table[pl.ds(start, TILE), :])
            logits[block, :, pl.ds(start, TILE)] = values
            parts = [values[:, at : at + 128] for at in range(0, TILE, 128)]
            new_top = top
            for part in parts:
                new_top = jnp.maximum(new_top, part)
            spread = spread * jnp.exp(top - new_top)
            near = wanted - start - lane
            for place, part in enumerate(parts):
                spread = spread + jnp.exp(part - new_top)
                hit = hit + jnp.where(near == place * 128, part, 0.0)
            return new_top, spread, hit

        zero = jnp.zeros((ROWS, 128), jnp.float32)
        low_start = jnp.full((ROWS, 128), -3e38, jnp.float32)
        top, spread, hit = lax.fori_loop(0, steps, body, (low_start, zero, zero))
        whole = jnp.max(top, -1, keepdims=True)
        spread = jnp.sum(spread * jnp.exp(top - whole), -1, keepdims=True)
        hit = jnp.sum(hit, -1, keepdims=True)
        stats[block, me] = jnp.where(lane == 0, whole, jnp.where(lane == 1, spread, hit)).T[:8]
        for step in range(1, owners):
            other = (me + step) % owners
            remote(
                stats.at[block, me],
                stats.at[block, me],
                stat_sem.at[block, me],
                x=other // cores,
                c=other % cores,
            )

    def second_pass(block, place):
        for step in range(1, owners):
            other = (me + step) % owners
            arrived(stats.at[block, other], stat_sem.at[block, other])
        found = [stats[block, index] for index in range(owners)]
        top = found[0][0:1]
        for value in found[1:]:
            top = jnp.maximum(top, value[0:1])
        spread, hit = jnp.zeros_like(top), jnp.zeros_like(top)
        for value in found:
            spread = spread + value[1:2] * jnp.exp(value[0:1] - top)
            hit = hit + value[2:3]
        log_total = top + jnp.log(spread)
        level = jnp.broadcast_to(log_total, (128, ROWS)).T
        wanted = targets[block] - me * count
        partial[place] = jnp.zeros((ROWS, 1024), jnp.float32)

        def body(number, _):
            start = pl.multiple_of(number * TILE, TILE)
            near = wanted - start - lane
            values = logits[block, :, pl.ds(start, TILE)]
            parts = []
            for index in range(TILE // 128):
                value = jnp.exp(values[:, index * 128 : (index + 1) * 128] - level)
                parts.append(low(jnp.where(near == index * 128, value - 1.0, value)))
            partial[place] += dot(jnp.concatenate(parts, 1), table[pl.ds(start, TILE), :])
            return 0

        lax.fori_loop(0, steps, body, 0)
        return log_total - hit

    first_pass(me, True)
    arrived(rows.at[twin], row_sem.at[twin])
    first_pass(twin)
    for step in range(1, across):
        block = far(step, mine)
        arrived(rows.at[block], row_sem.at[block])
        remote(rows.at[block], rows.at[block], row_sem.at[block], c=1 - mine)
        first_pass(block)
    for step in range(1, across):
        block = far(step, 1 - mine)
        arrived(rows.at[block], row_sem.at[block])
        first_pass(block)
    for step in range(1, across):
        for core in range(cores):
            second_pass(far(step, core), core)

            @pl.when(mine != core)
            def _(core=core, step=step):
                core_send[step - 1] = low(partial[core])
                pltpu.make_async_remote_copy(
                    src_ref=core_send.at[step - 1],
                    dst_ref=core_part.at[step - 1],
                    send_sem=core_sem.at[0, step - 1],
                    recv_sem=core_sem.at[1, step - 1],
                    device_id=device_at(here, sizes, c=1 - mine),
                    device_id_type=MESH_ID,
                ).start()

        arrived(core_part.at[step - 1], core_sem.at[1, step - 1])
        line_send[step - 1] = low(partial[mine] + wide(core_part[step - 1]))
        remote(
            line_send.at[step - 1],
            line_part.at[step - 1],
            line_sem.at[step - 1],
            x=(column + step) % across,
        )
    second_pass(twin, 0)
    last = across - 1
    core_send[last] = low(partial[0])
    remote(core_send.at[last], core_part.at[last], core_sem.at[1, last], c=1 - mine)
    loss = second_pass(me, 1)
    loss_out[...] = jnp.broadcast_to(loss, (8, ROWS))
    arrived(core_part.at[last], core_sem.at[1, last])
    value = partial[1] + wide(core_part[last])
    for step in range(1, across):
        arrived(line_part.at[step - 1], line_sem.at[step - 1])
        value = value + wide(line_part[step - 1])
    grad_out[...] = value * weight[:, :1]
    for copy in started:
        copy.wait_send()
    for step in range(1, across):
        pltpu.make_async_remote_copy(
            src_ref=core_send.at[step - 1],
            dst_ref=core_part.at[step - 1],
            send_sem=core_sem.at[0, step - 1],
            recv_sem=core_sem.at[1, step - 1],
            device_id=device_at(here, sizes, c=1 - mine),
            device_id_type=MESH_ID,
        ).wait_send()


def run_head(decoded, targets, weight, table, dp, vocab):
    sizes = grid_of(dp, vocab)
    across, owners = sizes["x"], vocab
    f32, b16 = jnp.float32, jnp.bfloat16
    anywhere, vmem = pl.BlockSpec(memory_space=pl.ANY), pl.BlockSpec(memory_space=pltpu.VMEM)
    dma = pltpu.SemaphoreType.DMA
    return pl.pallas_call(
        functools.partial(head_kernel, sizes),
        out_shape=[jax.ShapeDtypeStruct((ROWS, 1024), f32), jax.ShapeDtypeStruct((8, ROWS), f32)],
        in_specs=[vmem] * 3 + [anywhere],
        out_specs=[vmem] * 2,
        scratch_shapes=[
            pltpu.VMEM((owners, ROWS, 1024), b16),
            pltpu.VMEM(table.shape, b16),
            pltpu.VMEM((owners, ROWS, table.shape[0]), f32),
            pltpu.VMEM((2, ROWS, 1024), f32),
            pltpu.VMEM((across, ROWS, 1024), b16),
            pltpu.VMEM((across, ROWS, 1024), b16),
            pltpu.VMEM((across - 1, ROWS, 1024), b16),
            pltpu.VMEM((across - 1, ROWS, 1024), b16),
            pltpu.VMEM((owners, owners, 8, ROWS), f32),
            dma((table.shape[0] // TILE,)),
            dma((owners,)),
            dma((owners, owners)),
            dma((2, across)),
            dma((across,)),
            dma((8 * owners,)),
        ],
        compiler_params=pltpu.CompilerParams(
            collective_id=3, has_side_effects=True, vmem_limit_bytes=62 * 2**20
        ),
    )(
        decoded,
        jnp.broadcast_to(targets.reshape(owners, ROWS, 1), (owners, ROWS, 128)),
        jnp.broadcast_to(weight.reshape(ROWS, 1), (ROWS, 128)),
        table,
    )


def backward_kernel(sizes, *refs):
    refs = list(refs)

    def take(count):
        found = refs[:count]
        del refs[:count]
        return found

    grad_in, norms, extra = take(3)
    names = ("attn_in", "attn_out", "widen", "narrow", "down", "up")
    held = dict(zip(names, take(6)))
    saved_in = take(7)
    shards = take(4)
    small_out, square_out = take(2)
    saved = take(7)
    qkv_all, probs_all, normed_ring, inv_all, feed_in, slopes, bottles = saved
    saved_sem, normed_sem, tiles, tile_sem, down_tile, down_sem = take(6)
    grads = take(4)
    sums, core_send, core_recv = take(4), take(4), take(4)
    wide_send, wide_recv, mid_send, mid_recv, last_send, last_recv = (take(4) for _ in range(6))
    small, small_slots, (late, owner_slots, group_slots) = take(1)[0], take(4), take(3)
    grad_low, grad_sum, grad_memory, grad_hidden, grad_att, packed = take(6)
    send_sem, recv_sem = take(2)
    here = position(sizes)
    mine = here["c"]

    loads = {}

    def fetch(place, index):
        if (place, index) not in loads:
            copy = pltpu.make_async_copy(
                saved_in[place].at[index], saved[place].at[index], saved_sem.at[len(loads)]
            )
            loads[place, index] = copy
            copy.start()
        return loads[place, index]

    order = (6, 5, 4, 3, 2, 1, 0)

    def normed_copy(number):
        slot = number % normed_ring.shape[0]
        return pltpu.make_async_copy(saved_in[2].at[order[number]], normed_ring.at[slot], normed_sem.at[slot])

    plan = []
    block = 1024
    for kind, which in (("feed", 1), ("attend", 2), ("attend", 1), ("feed", 0), ("attend", 0)):
        if kind == "feed":
            for left in range(0, 4096, block):
                plan += [("narrow", which, left), ("widen", which, left)]
            plan.append(("up", which, 0))
        else:
            plan.append(("attn_out", which, 0))
            plan += [("attn_in", which, left) for left in range(0, 3072, block)]
    grid = tuple(sizes[axis] for axis in "zyxc")
    depth = tiles.shape[0]

    def tile_copy(number):
        name, layer, left = plan[number]
        rows, columns = held[name].shape[5:]
        buffer = tiles.at[number % depth]
        if name == "narrow":
            planes = left // block
            source, shape = held[name].at[layer, planes], grid[1:] + (rows, columns)
        else:
            columns = min(columns, block)
            source = held[name].at[layer, :, :, :, :, :, pl.ds(left, columns)]
            shape = grid + (rows, columns)
        count = 1
        for size in shape[:-1]:
            count *= size
        target = buffer.at[pl.ds(0, count), pl.ds(0, columns)]
        return pltpu.make_async_copy(source, target.reshape(shape), tile_sem.at[number % depth]), target

    def down_copy(side):
        target = down_tile.reshape(grid + held["down"].shape[5:])
        return pltpu.make_async_copy(held["down"].at[side], target, down_sem.at[0])

    turn = [0]

    def with_tile(use):
        number = turn[0]
        turn[0] += 1
        copy, target = tile_copy(number)
        copy.wait()
        result = use(target[...])
        if number + depth < len(plan):
            tile_copy(number + depth)[0].start()
        return result

    for number in range(2):
        normed_copy(number).start()
    fetch(3, slice(None))
    fetch(5, 1)
    for number in range(depth):
        tile_copy(number)[0].start()
    down_copy(1).start()
    for place, index in ((6, 1), (4, 1), (0, 2), (1, 2), (0, 1), (1, 1), (5, 0), (6, 0), (4, 0), (0, 0), (1, 0)):
        fetch(place, index)
    barrier = pltpu.get_barrier_semaphore()
    owners, groups = sizes["x"] * sizes["c"], sizes["z"] * sizes["y"]
    owner, group = here["x"] * sizes["c"] + here["c"], here["z"] * sizes["y"] + here["y"]

    def owner_at(step):
        other = (owner + step) % owners
        return {"x": other // sizes["c"], "c": other % sizes["c"]}

    def group_at(step):
        other = (group + step) % groups
        return {"z": other // sizes["y"], "y": other % sizes["y"]}

    peers = [owner_at(step) for step in range(1, owners)] + [group_at(step) for step in range(1, groups)]
    for peer in peers:
        pl.semaphore_signal(barrier, inc=1, device_id=device_at(here, sizes, **peer), device_id_type=MESH_ID)
    pl.semaphore_wait(barrier, len(peers))

    used, started = [0], []

    def copy_to(src, dst, **moved):
        number = used[0]
        used[0] += 1
        copy = pltpu.make_async_remote_copy(
            src_ref=src,
            dst_ref=dst,
            send_sem=send_sem.at[number],
            recv_sem=recv_sem.at[number],
            device_id=device_at(here, sizes, **moved),
            device_id_type=MESH_ID,
        )
        copy.start()
        started.append(copy)
        return copy

    def share(slots, value, axis):
        slots[here[axis]] = value
        return [
            copy_to(slots.at[here[axis]], slots.at[here[axis]], **{axis: (here[axis] + step) % sizes[axis]})
            for step in range(1, sizes[axis])
        ]

    def total(slots, axis, copies):
        for copy in copies:
            copy.wait_recv()
        value = slots[0]
        for index in range(1, sizes[axis]):
            value = value + slots[index]
        return value

    plans = (("x", "y"), ("y", "x"), ("x", "y"), ("y", "x"))
    pending = [None] * 4

    def phase_core(parts):
        for part in parts:
            core_send[part][...] = low(grads[part][:, :, :, 1 - mine])
            pending[part] = copy_to(core_send[part], core_recv[part], c=1 - mine)

    def phase_wide(parts):
        for part in parts:
            pending[part].wait_recv()
            sums[part][...] = grads[part][:, :, :, mine] + wide(core_recv[part][...])
            axis = plans[part][0]
            found = []
            for step in range(1, sizes[axis]):
                other = (here[axis] + step) % sizes[axis]
                value = sums[part][:, :, other] if axis == "x" else sums[part][:, other]
                wide_send[part][step - 1] = low(value)
                found.append(copy_to(wide_send[part].at[step - 1], wide_recv[part].at[step - 1], **{axis: other}))
            pending[part] = found

    def phase_mid(parts):
        for part in parts:
            axis, later = plans[part]
            kept = sums[part].at[:, :, here["x"]] if axis == "x" else sums[part].at[:, here["y"]]
            value = kept[...]
            for step, copy in enumerate(pending[part]):
                copy.wait_recv()
                value = value + wide(wide_recv[part][step])
            kept[...] = value
            found = []
            for step in range(1, sizes[later]):
                other = (here[later] + step) % sizes[later]
                mid_send[part][step - 1] = low(kept[:, other])
                found.append(copy_to(mid_send[part].at[step - 1], mid_recv[part].at[step - 1], **{later: other}))
            pending[part] = found

    def phase_last(parts):
        for part in parts:
            kept = sums[part].at[:, here["y"], here["x"]]
            value = kept[...]
            for step, copy in enumerate(pending[part]):
                copy.wait_recv()
                value = value + wide(mid_recv[part][step])
            kept[...] = value
            found = []
            for step in range(1, sizes["z"]):
                other = (here["z"] + step) % sizes["z"]
                last_send[part][step - 1] = low(kept[other])
                found.append(copy_to(last_send[part].at[step - 1], last_recv[part].at[step - 1], z=other))
            pending[part] = found

    def phase_end(parts):
        square = jnp.zeros((1, 1), jnp.float32)
        for part in parts:
            value = sums[part][here["z"], here["y"], here["x"]]
            for step, copy in enumerate(pending[part]):
                copy.wait_recv()
                value = value + wide(last_recv[part][step])
            shards[part][...] = value
            square = square + jnp.sum(value * value, keepdims=True)
        return square

    norm_turn = [0]

    def norm_back(grad_out, which):
        number = norm_turn[0]
        norm_turn[0] += 1
        if number + 2 < len(order):
            normed_copy(number + 2).start()
        normed_copy(number).wait()
        normed = normed_ring[number % normed_ring.shape[0]]
        inv_std = inv_all[which][:, :1]
        scaled = grad_out * norms[which : which + 1, :]
        small[which : which + 1, :] = jnp.sum(grad_out * normed, 0, keepdims=True)
        small[which + 7 : which + 8, :] = jnp.sum(grad_out, 0, keepdims=True)
        grad = inv_std * (
            scaled - jnp.mean(scaled, -1, keepdims=True) - normed * jnp.mean(scaled * normed, -1, keepdims=True)
        )
        grad_sum[...] = grad
        grad_low[...] = low(grad)

    def feed_back(side):
        fetch(5, side).wait()
        for left in range(0, 4096, block):

            def first(tile, left=left):
                slope = wide(slopes[side, :, pl.ds(left, block)])
                grad_hidden[...] = low(dot_rows(grad_low[...], tile) * slope)

            def second(tile):
                grad_sum[...] += dot_rows(grad_hidden[...], tile)

            with_tile(first)
            with_tile(second)
        fetch(6, side).wait()
        fetch(4, side).wait()

        def up(tile):
            bottle = low(BRANCH_SCALE * dot_rows(grad_low[...], tile) * wide(bottles[side, 1]))
            grad_hidden[:, pl.ds(0, 512)] = bottle

        with_tile(up)
        down_copy(side).wait()
        grad_sum[...] += dot_rows(grad_hidden[:, pl.ds(0, 512)], down_tile[...])
        if side:
            down_copy(0).start()
        part = 2 * side
        grads[part + 1][...] = (BRANCH_SCALE * dot_columns(bottles[side, 0], grad_low[...])).reshape(
            grads[part + 1].shape
        )
        grads[part][...] = dot_columns(feed_in[side], grad_hidden[:, pl.ds(0, 512)]).reshape(grads[part].shape)

    def attend_back(layer, between=None):
        def first(tile):
            grad_att[...] = low(dot_rows(grad_low[...], tile))

        with_tile(first)
        fetch(0, layer).wait()
        fetch(1, layer).wait()

        def body(number, _):
            seq, pair = number // 8, number % 8
            masks = lane_masks()
            rows = pl.ds(pl.multiple_of(seq * LEN, LEN), LEN)

            def columns(part):
                return pl.ds(pl.multiple_of(part * 1024 + pair * 128, 128), 128)

            queries, keys, values = (qkv_all[layer, rows, columns(part)] for part in range(3))
            grad_out = stack_heads(grad_att[rows, columns(0)], masks)
            chance_low = probs_all[layer, seq, pair]
            chance = wide(chance_low)
            weighed = chance * dot_rows(grad_out, values)
            grad_scores = low(weighed - chance * jnp.sum(weighed, -1, keepdims=True))
            side = jnp.concatenate([grad_scores[:LEN], grad_scores[LEN:]], 1)
            packed[rows, columns(0)] = low(dot(side, stack_heads(keys, masks)) * 0.125)
            packed[rows, columns(1)] = low(dot_columns(grad_scores, stack_heads(queries, masks)) * 0.125)
            packed[rows, columns(2)] = low(dot_columns(chance_low, grad_out))
            return 0

        if between is None:
            lax.fori_loop(0, 8 * MICRO, body, 0, unroll=4)
        else:
            for seq, extra_work in enumerate(between):
                lax.fori_loop(8 * seq, 8 * seq + 8, body, 0, unroll=4)
                extra_work()
        for left in range(0, 3072, block):

            def second(tile, left=left):
                value = dot_rows(packed[:, pl.ds(left, block)], tile)
                if layer == 2 and left == block:
                    grad_memory[...] = value
                elif layer == 2 and left > block:
                    grad_memory[...] += value
                else:
                    grad_sum[...] += value

            with_tile(second)

    small[...] = extra[...]
    fetch(3, slice(None)).wait()
    norm_back(grad_in[...], 6)
    feed_back(1)
    phase_core((2, 3))
    norm_back(grad_sum[...], 5)
    attend_back(2)
    phase_wide((2, 3))
    norm_back(grad_sum[...], 4)
    attend_back(1)
    phase_mid((2, 3))
    norm_back(grad_sum[...], 3)
    norm_back(grad_memory[...], 2)
    feed_back(0)
    phase_core((0, 1))
    phase_last((2, 3))
    norm_back(grad_sum[...], 1)
    chain = [share(small_slots[0], small[...], "c")]

    def halfway():
        phase_wide((0, 1))
        chain.append(share(small_slots[1], total(small_slots[0], "c", chain[0]), "x"))

    def after():
        chain.append(share(small_slots[2], total(small_slots[1], "x", chain[1]), "y"))

    attend_back(0, (halfway, after))
    chain.append(share(small_slots[3], total(small_slots[2], "y", chain[2]), "z"))
    phase_mid((0, 1))
    square = phase_end((2, 3))
    norm_back(grad_sum[...], 0)
    phase_last((0, 1))
    for row in range(2):
        for place in range(8):
            late[8 * row + place : 8 * row + place + 1, :] = small[
                7 * row : 7 * row + 1, 128 * place : 128 * place + 128
            ]
    whole = total(small_slots[3], "z", chain[3])
    small_out[...] = whole
    norm_square = jnp.sum(whole[:14] * whole[:14], keepdims=True)
    square = square + phase_end((0, 1))
    late[16:24, :] = jnp.broadcast_to(square, (8, 128))

    def gather_late(slots, mine_at, count, at, value):
        slots[mine_at] = value
        copies = [copy_to(slots.at[mine_at], slots.at[mine_at], **at(step)) for step in range(1, count)]
        for copy in copies:
            copy.wait_recv()
        value = slots[0]
        for index in range(1, count):
            value = value + slots[index]
        return value

    value = gather_late(owner_slots, owner, owners, owner_at, late[...])
    value = gather_late(group_slots, group, groups, group_at, value)
    for row in range(2):
        for place in range(8):
            small_out[7 * row : 7 * row + 1, 128 * place : 128 * place + 128] = value[
                8 * row + place : 8 * row + place + 1, :
            ]
    norm_square = norm_square + jnp.sum(value[:16] * value[:16], keepdims=True)
    square_out[...] = value[16:24] + norm_square
    for copy in started:
        copy.wait_send()


def run_backward(grad_decoded, norms, extra, held, saved, dp, vocab):
    sizes = grid_of(dp, vocab)
    z, y, x, c = (sizes[axis] for axis in "zyxc")
    names = ("attn_in", "attn_out", "widen", "narrow", "down", "up")
    down, up = held["down"].shape[5:], held["up"].shape[5:]
    tails = (down, up, down, up)
    f32, b16 = jnp.float32, jnp.bfloat16
    anywhere, vmem = pl.BlockSpec(memory_space=pl.ANY), pl.BlockSpec(memory_space=pltpu.VMEM)
    dma = pltpu.SemaphoreType.DMA
    scratch = [pltpu.VMEM(value.shape, value.dtype) for value in saved]
    scratch[2] = pltpu.VMEM((3, ROWS, 1024), f32)
    scratch += [dma((16,)), dma((3,)), pltpu.VMEM((5, 1024, 1024), b16), dma((5,))]
    scratch += [pltpu.VMEM((1024, 512), b16), dma((1,))]
    scratch += [pltpu.VMEM((z, y, x, c) + tail, f32) for tail in tails]
    scratch += [pltpu.VMEM((z, y, x) + tail, f32) for tail in tails]
    for _ in range(2):
        scratch += [pltpu.VMEM((z, y, x) + tail, b16) for tail in tails]
    for lead in (((x - 1, z, y), (y - 1, z, x)), ((y - 1, z), (x - 1, z)), ((z - 1,), (z - 1,))):
        for _ in range(2):
            scratch += [pltpu.VMEM(lead[place % 2] + tail, b16) for place, tail in enumerate(tails)]
    scratch.append(pltpu.VMEM((16, 1024), f32))
    scratch += [pltpu.VMEM((sizes[axis], 16, 1024), f32) for axis in "cxyz"]
    scratch += [pltpu.VMEM(shape, f32) for shape in ((24, 128), (vocab, 24, 128), (dp, 24, 128))]
    scratch += [
        pltpu.VMEM((ROWS, 1024), b16),
        pltpu.VMEM((ROWS, 1024), f32),
        pltpu.VMEM((ROWS, 1024), f32),
        pltpu.VMEM((ROWS, 1024), b16),
        pltpu.VMEM((ROWS, 1024), b16),
        pltpu.VMEM((ROWS, 3072), b16),
    ]
    links = 6 * (x + y + z + c) + dp + vocab
    scratch += [dma((links,)), dma((links,))]
    return pl.pallas_call(
        functools.partial(backward_kernel, sizes),
        out_shape=[jax.ShapeDtypeStruct(tail, f32) for tail in tails]
        + [jax.ShapeDtypeStruct((16, 1024), f32), jax.ShapeDtypeStruct((8, 128), f32)],
        in_specs=[vmem] * 3 + [anywhere] * 13,
        out_specs=[vmem] * 6,
        scratch_shapes=scratch,
        compiler_params=pltpu.CompilerParams(
            collective_id=2, has_side_effects=True, vmem_limit_bytes=62 * 2**20
        ),
    )(grad_decoded, norms, extra, *[held[name] for name in names], *saved)


def attend_back(grad_low, queries, key_rows, values, probs, scale):
    grad_heads = split_heads(grad_low)
    grad_probs = jnp.einsum(
        "bqhd,bkhd->bhqk", grad_heads, split_heads(values), preferred_element_type=jnp.float32
    )
    grad_values = jnp.einsum("bhqk,bqhd->bkhd", probs, grad_heads, preferred_element_type=jnp.float32)
    probs = wide(probs)
    grad_scores = low(probs * (grad_probs - jnp.sum(probs * grad_probs, -1, keepdims=True)))
    grad_queries = (
        jnp.einsum("bhqk,bkhd->bqhd", grad_scores, split_heads(key_rows), preferred_element_type=jnp.float32)
        * scale
    )
    grad_keys = (
        jnp.einsum("bhqk,bqhd->bkhd", grad_scores, split_heads(queries), preferred_element_type=jnp.float32)
        * scale
    )
    return tuple(value.reshape(ROWS, -1) for value in (grad_queries, grad_keys, grad_values))


def split_heads(value):
    return value.reshape(MICRO, LEN, HEADS, value.shape[1] // HEADS)


def norm_back(grad_out, normed, inv_std, norm_gain):
    scaled = grad_out * norm_gain
    grad_in = inv_std * (
        scaled
        - jnp.mean(scaled, -1, keepdims=True)
        - normed * jnp.mean(scaled * normed, -1, keepdims=True)
    )
    return grad_in, jnp.sum(grad_out * normed, 0), jnp.sum(grad_out, 0)


def backward(grad_decoded, held, norms, saved):
    qkv_all, probs_all, normed_all, inv_all, feed_in, slopes, bottles = saved
    gains, biases = [None] * 7, [None] * 7

    def norm(grad, which):
        grad, gains[which], biases[which] = norm_back(grad, normed_all[which], inv_all[which, :, :1], norms[which])
        return grad

    def feed(grad, side, which):
        grad_sum = norm(grad, which)
        low_grad = low(grad_sum)
        grad_hidden = low(dot_rows(low_grad, held["narrow"][side]) * wide(slopes[side]))
        grad_bottle = low(BRANCH_SCALE * dot_rows(low_grad, held["up"][side]) * wide(bottles[side, 1]))
        grad_in = grad_sum + dot_rows(grad_hidden, held["widen"][side]) + dot_rows(grad_bottle, held["down"][side])
        grad_up = BRANCH_SCALE * dot_columns(bottles[side, 0], low_grad)
        return grad_in, dot_columns(feed_in[side], grad_bottle), grad_up

    def attend(grad, layer, which):
        grad_sum = norm(grad, which)
        grad_att = low(dot_rows(low(grad_sum), held["attn_out"][layer]))
        qkv = qkv_all[layer]
        probs = probs_all[layer].reshape(MICRO, HEADS, LEN, LEN)
        parts = attend_back(grad_att, qkv[:, :1024], qkv[:, 1024:2048], qkv[:, 2048:], probs, 0.125)
        packed = low(jnp.concatenate(parts, 1))
        w_in = held["attn_in"][layer]
        if layer == 2:
            return grad_sum + dot_rows(packed[:, :1024], w_in[:, :1024]), dot_rows(packed[:, 1024:], w_in[:, 1024:])
        return grad_sum + dot_rows(packed, w_in), None

    grad, down_dec, up_dec = feed(grad_decoded, 1, 6)
    grad, grad_memory = attend(grad, 2, 5)
    grad, _ = attend(grad, 1, 4)
    norm(grad, 3)
    grad, down_enc, up_enc = feed(grad_memory, 0, 2)
    grad, _ = attend(grad, 0, 1)
    norm(grad, 0)
    return down_enc, up_enc, down_dec, up_dec, jnp.stack(gains + biases)


def adam_step(weight, first, second, grad, rate):
    first = BETA_FIRST * first + (1.0 - BETA_FIRST) * grad
    second = BETA_SECOND * second + (1.0 - BETA_SECOND) * grad * grad
    first_hat = first / (1.0 - BETA_FIRST**STEP)
    second_hat = second / (1.0 - BETA_SECOND**STEP)
    weight = weight - rate * (
        first_hat / (jnp.sqrt(second_hat) + ADAM_EPSILON) + WEIGHT_DECAY * weight
    )
    return (first, second, weight)


def head(decoded, vocab_table, target_ids, target_length, seq_scale, groups, vocab_rank):
    rows_local = vocab_table.shape[0]
    key_index = jnp.arange(LEN)
    head_rows = lax.all_gather(decoded, "vocab", axis=0, tiled=True)
    logits = dot_rows(head_rows, vocab_table)
    local_target = target_ids.reshape(-1) - vocab_rank * rows_local
    target_hot = lax.broadcasted_iota(jnp.int32, logits.shape, 1) == local_target[:, None]
    target_logit = jnp.sum(jnp.where(target_hot, logits, 0.0), 1)
    local_max = jnp.max(logits, 1)
    row_max = lax.pmax(local_max, "vocab")
    row_total, row_target = lax.psum(
        (jnp.sum(jnp.exp(logits - row_max[:, None]), 1), target_logit), "vocab"
    )
    log_total = row_max + jnp.log(row_total)
    row_mask = (key_index[None, :] < target_length[:, None]).astype(jnp.float32)
    row_weight = (row_mask * seq_scale[:, None]).reshape(-1)
    row_loss = (log_total - row_target).reshape(-1, LEN) * row_mask
    own_loss = lax.dynamic_slice_in_dim(row_loss, vocab_rank * MICRO, MICRO)
    grad_logits = low(
        row_weight[:, None] * (jnp.exp(logits - log_total[:, None]) - target_hot.astype(jnp.float32))
    )
    grad_decoded = lax.psum_scatter(
        dot(grad_logits, vocab_table).astype(jnp.bfloat16), "vocab", scatter_dimension=0, tiled=True
    ).astype(jnp.float32)
    return grad_decoded, jnp.sum(own_loss, 1)


def local(
    source_ids,
    target_in,
    target_ids,
    source_length,
    target_length,
    task_ids,
    vocab_table,
    positions,
    attention_in,
    attention_out,
    widen_weight,
    narrow_weight,
    adapt_down,
    adapt_up,
    norm_params,
    down_first,
    down_second,
    up_first,
    up_second,
    norm_first,
    norm_second,
):
    dp, groups = lax.axis_size("dp"), lax.axis_size("vocab")
    vocab_rank = lax.axis_index("vocab")
    rows_local, width = vocab_table.shape
    joined_ids = (
        jnp.stack([source_ids.reshape(groups, -1), target_in.reshape(groups, -1)], 1).reshape(-1)
        - vocab_rank * rows_local
    )
    inside = (joined_ids >= 0) & (joined_ids < rows_local)
    picked = jnp.where(
        inside[:, None],
        jnp.take(vocab_table, jnp.clip(joined_ids, 0, rows_local - 1), axis=0),
        jnp.zeros((), jnp.bfloat16),
    ).reshape(groups // 2, 2, 2, ROWS, width)
    task_hot = (task_ids[:, None] == jnp.arange(TASKS)[None, :]).astype(jnp.float32)
    group_counts = jnp.sum(task_hot * target_length[:, None].astype(jnp.float32), 0)
    own = vocab_rank * MICRO
    source_count = lax.dynamic_slice_in_dim(source_length, own, MICRO)
    key_keep = jnp.broadcast_to(
        (jnp.arange(LEN)[None, None, :] < source_count[:, None, None]).astype(jnp.float32), (MICRO, 8, LEN)
    )
    parts = {
        "norms": jnp.concatenate(
            [
                norm_params.T,
                jnp.pad(group_counts, (0, norm_params.shape[1] - TASKS))[:, None],
                jnp.zeros((norm_params.shape[1], 113), jnp.float32),
            ],
            1,
        )[None],
        "attn_in": attention_in,
        "attn_out": attention_out,
        "widen": widen_weight,
        "narrow": narrow_weight,
        "down": low(adapt_down),
        "up": low(adapt_up),
    }
    held, saved = run_forward(parts, picked, positions, key_keep, dp, groups)
    slab = held.pop("norms").reshape(dp, groups, -1, 128)
    task_counts = jnp.sum(slab[:, 0, :TASKS, 14], 0)
    seq_scale = jnp.sum(task_hot * (1.0 / (TASKS * task_counts))[None, :], 1)
    norms = slab.reshape(width, 128)[:, :16].T
    if groups <= 4 and rows_local % TILE == 0:
        own_length = lax.dynamic_slice_in_dim(target_length, own, MICRO)
        own_mask = (jnp.arange(LEN)[None, :] < own_length[:, None]).astype(jnp.float32)
        own_weight = own_mask * lax.dynamic_slice_in_dim(seq_scale, own, MICRO)[:, None]
        grad_decoded, row_loss = run_head(saved[7], target_ids, own_weight, vocab_table, dp, groups)
        own_loss = jnp.sum(row_loss[0].reshape(MICRO, LEN) * own_mask, 1)
    else:
        grad_decoded, own_loss = head(
            saved[7], vocab_table, target_ids, target_length, seq_scale, groups, vocab_rank
        )
    task_local = jnp.sum(lax.dynamic_slice_in_dim(task_hot, own, MICRO) * own_loss[:, None], 0)
    task_row = jnp.pad(task_local[None], ((0, 1), (0, width - TASKS)))
    if groups <= 4:
        extra = jnp.pad(task_row, ((14, 0), (0, 0)))
        down_enc, up_enc, down_dec, up_dec, small, square = run_backward(
            grad_decoded, norms, extra, held, saved[:7], dp, groups
        )
    else:
        held = {name: value.reshape(value.shape[0], -1, value.shape[-1]) for name, value in held.items()}
        down_enc, up_enc, down_dec, up_dec, norm_grads = backward(grad_decoded, held, norms, saved[:7])
        small = jnp.concatenate([norm_grads, task_row], 0)
        down_enc, up_enc, down_dec, up_dec, small, square = reduce_gradients(
            down_enc, up_enc, down_dec, up_dec, small, dp, groups
        )
    shard_down = jnp.stack([down_enc, down_dec])
    shard_up = jnp.stack([up_enc, up_dec])
    full_norm, task_sums = small[:14], small[14, :TASKS]
    cut = norm_params.shape[1]
    shard_norm = lax.dynamic_slice_in_dim(full_norm, lax.axis_index(("dp", "vocab")) * cut, cut, 1)
    grad_norm = jnp.sqrt(square[0, 0])
    factor = CLIP_LIMIT / jnp.maximum(grad_norm, CLIP_LIMIT)
    down_new = adam_step(adapt_down, down_first, down_second, shard_down * factor, RATE_ADAPTER)
    up_new = adam_step(adapt_up, up_first, up_second, shard_up * factor, RATE_ADAPTER)
    norm_new = adam_step(norm_params, norm_first, norm_second, shard_norm * factor, RATE_NORMS)
    return (*down_new, *up_new, *norm_new, grad_norm, task_sums, task_counts)


def solution(mesh):
    return jax.shard_map(
        local,
        mesh=mesh,
        in_specs=(
            P("dp", None),
            P("dp", None),
            P("dp", None),
            P("dp"),
            P("dp"),
            P("dp"),
            P("vocab", None),
            P(),
            P(None, ("dp", "vocab"), None),
            P(None, ("dp", "vocab"), None),
            P(None, ("dp", "vocab"), None),
            P(None, ("dp", "vocab"), None),
            P(None, ("dp", "vocab"), None),
            P(None, ("dp", "vocab"), None),
            P(None, ("dp", "vocab")),
            P(None, ("dp", "vocab"), None),
            P(None, ("dp", "vocab"), None),
            P(None, ("dp", "vocab"), None),
            P(None, ("dp", "vocab"), None),
            P(None, ("dp", "vocab")),
            P(None, ("dp", "vocab")),
        ),
        out_specs=(
            P(None, ("dp", "vocab"), None),
            P(None, ("dp", "vocab"), None),
            P(None, ("dp", "vocab"), None),
            P(None, ("dp", "vocab"), None),
            P(None, ("dp", "vocab"), None),
            P(None, ("dp", "vocab"), None),
            P(None, ("dp", "vocab")),
            P(None, ("dp", "vocab")),
            P(None, ("dp", "vocab")),
            P(),
            P(),
            P(),
        ),
        check_vma=False,
    )
```

```python
import functools

import jax
import jax.numpy as jnp
from jax import lax
from jax.experimental import pallas as pl
from jax.experimental.pallas import tpu as pltpu
from jax.sharding import PartitionSpec as P

MESH_ID = pl.DeviceIdType.MESH
TASKS = 4
STEP = 10
CLIP_LIMIT = 0.002
BETA_FIRST = 0.9
BETA_SECOND = 0.999
ADAM_EPSILON = 1e-08
WEIGHT_DECAY = 0.01
RATE_ADAPTER = 0.02
RATE_NORMS = 0.2


def grid_of(dp, vocab):
    cores = 2
    across = vocab // cores
    return {"z": dp // across, "y": across, "x": across, "c": cores}


def position(sizes):
    dp, vocab = lax.axis_index("dp"), lax.axis_index("vocab")
    return {
        "z": dp // sizes["y"],
        "y": dp % sizes["y"],
        "x": vocab // sizes["c"],
        "c": vocab % sizes["c"],
    }


def device_at(here, sizes, **moved):
    at = dict(here)
    at.update(moved)
    return (at["z"] * sizes["y"] + at["y"], at["x"] * sizes["c"] + at["c"])


def lines_barrier(here, sizes):
    barrier = pltpu.get_barrier_semaphore()
    peers = 0
    for axis in "zyxc":
        for step in range(1, sizes[axis]):
            other = (here[axis] + step) % sizes[axis]
            pl.semaphore_signal(
                barrier, inc=1, device_id=device_at(here, sizes, **{axis: other}), device_id_type=MESH_ID
            )
            peers += 1
    pl.semaphore_wait(barrier, peers)


def reduce_kernel(sizes, *refs):
    grads = refs[0:4]
    small = refs[4]
    shards = refs[5:9]
    small_out, square_out = refs[9:11]
    sums, core_send, core_recv = refs[11:15], refs[15:19], refs[19:23]
    wide_send, wide_recv, mid_send, mid_recv, last_send, last_recv = (
        refs[23:27], refs[27:31], refs[31:35], refs[35:39], refs[39:43], refs[43:47]
    )
    small_slots, square_slots = refs[47:51], refs[51:55]
    send_sem, recv_sem = refs[55:57]
    here = position(sizes)
    lines_barrier(here, sizes)
    used = [0]
    started = []

    def copy_to(src, dst, **moved):
        number = used[0]
        used[0] += 1
        copy = pltpu.make_async_remote_copy(
            src_ref=src,
            dst_ref=dst,
            send_sem=send_sem.at[number],
            recv_sem=recv_sem.at[number],
            device_id=device_at(here, sizes, **moved),
            device_id_type=MESH_ID,
        )
        copy.start()
        started.append(copy)
        return copy

    def low(value):
        return value.astype(jnp.bfloat16)

    mine = here["c"]

    def share(slots, value, axis):
        slots[here[axis]] = value
        return [
            copy_to(slots.at[here[axis]], slots.at[here[axis]], **{axis: (here[axis] + step) % sizes[axis]})
            for step in range(1, sizes[axis])
        ]

    def total(slots, axis, copies):
        for copy in copies:
            copy.wait_recv()
        value = slots[0]
        for index in range(1, sizes[axis]):
            value = value + slots[index]
        return value

    first = []
    for part in range(4):
        core_send[part][...] = low(grads[part][:, :, :, 1 - mine])
        first.append(copy_to(core_send[part], core_recv[part], c=1 - mine))
    copies = share(small_slots[0], small[...], "c")
    plans = (("x", "y"), ("x", "y"), ("y", "x"), ("y", "x"))

    second = []
    for part in range(4):
        first[part].wait_recv()
        sums[part][...] = grads[part][:, :, :, mine] + core_recv[part][...].astype(jnp.float32)
        axis = plans[part][0]
        found = []
        for step in range(1, sizes[axis]):
            other = (here[axis] + step) % sizes[axis]
            piece = sums[part][:, :, other] if axis == "x" else sums[part][:, other]
            wide_send[part][step - 1] = low(piece)
            found.append(copy_to(wide_send[part].at[step - 1], wide_recv[part].at[step - 1], **{axis: other}))
        second.append(found)
    copies = share(small_slots[1], total(small_slots[0], "c", copies), "x")
    third = []
    for part in range(4):
        axis, later = plans[part]
        held = sums[part].at[:, :, here["x"]] if axis == "x" else sums[part].at[:, here["y"]]
        value = held[...]
        for step, copy in enumerate(second[part]):
            copy.wait_recv()
            value = value + wide_recv[part][step].astype(jnp.float32)
        held[...] = value
        found = []
        for step in range(1, sizes[later]):
            other = (here[later] + step) % sizes[later]
            mid_send[part][step - 1] = low(held[:, other])
            found.append(copy_to(mid_send[part].at[step - 1], mid_recv[part].at[step - 1], **{later: other}))
        third.append(found)
    copies = share(small_slots[2], total(small_slots[1], "x", copies), "y")
    fourth = []
    for part in range(4):
        axis, later = plans[part]
        held = sums[part].at[:, here["y"], here["x"]]
        value = held[...]
        for step, copy in enumerate(third[part]):
            copy.wait_recv()
            value = value + mid_recv[part][step].astype(jnp.float32)
        held[...] = value
        found = []
        for step in range(1, sizes["z"]):
            other = (here["z"] + step) % sizes["z"]
            last_send[part][step - 1] = low(held[other])
            found.append(copy_to(last_send[part].at[step - 1], last_recv[part].at[step - 1], z=other))
        fourth.append(found)
    copies = share(small_slots[3], total(small_slots[2], "y", copies), "z")
    square = jnp.zeros((1, 1), jnp.float32)
    for part in range(4):
        value = sums[part][here["z"], here["y"], here["x"]]
        for step, copy in enumerate(fourth[part]):
            copy.wait_recv()
            value = value + last_recv[part][step].astype(jnp.float32)
        shards[part][...] = value
        square = square + jnp.sum(value * value, keepdims=True)
    square = jnp.broadcast_to(square, (8, 128))
    for place, axis in enumerate("cxyz"):
        parts = share(square_slots[place], square, axis)
        if place == 0:
            whole = total(small_slots[3], "z", copies)
            small_out[...] = whole
            norm_square = jnp.sum(whole[:14] * whole[:14], keepdims=True)
        square = total(square_slots[place], axis, parts)
    square_out[...] = square + norm_square
    for copy in started:
        copy.wait_send()


def reduce_gradients(down_enc, up_enc, down_dec, up_dec, small, dp, vocab):
    sizes = grid_of(dp, vocab)
    grid = tuple(sizes[axis] for axis in "zyxc")
    whole = dp * vocab
    grads = [
        value.reshape(grid + (value.shape[0] // whole, value.shape[1]))
        for value in (down_enc, up_enc, down_dec, up_dec)
    ]
    z, y, x, c = grid
    tails = [value.shape[4:] for value in grads]
    vmem = pl.BlockSpec(memory_space=pltpu.VMEM)
    scratch = [pltpu.VMEM((z, y, x) + tail, jnp.float32) for tail in tails]
    for _ in range(2):
        scratch += [pltpu.VMEM((z, y, x) + tail, jnp.bfloat16) for tail in tails]
    for _ in range(2):
        scratch += [
            pltpu.VMEM(((x - 1, z, y) if place < 2 else (y - 1, z, x)) + tail, jnp.bfloat16)
            for place, tail in enumerate(tails)
        ]
    for _ in range(2):
        scratch += [
            pltpu.VMEM(((y - 1, z) if place < 2 else (x - 1, z)) + tail, jnp.bfloat16)
            for place, tail in enumerate(tails)
        ]
    for _ in range(2):
        scratch += [pltpu.VMEM((z - 1,) + tail, jnp.bfloat16) for tail in tails]
    scratch += [pltpu.VMEM((sizes[axis],) + small.shape, jnp.float32) for axis in "cxyz"]
    scratch += [pltpu.VMEM((sizes[axis], 8, 128), jnp.float32) for axis in "cxyz"]
    links = 6 * (x + y + z + c)
    scratch += [pltpu.SemaphoreType.DMA((links,)), pltpu.SemaphoreType.DMA((links,))]
    return pl.pallas_call(
        functools.partial(reduce_kernel, sizes),
        out_shape=[jax.ShapeDtypeStruct(tail, jnp.float32) for tail in tails]
        + [jax.ShapeDtypeStruct(small.shape, jnp.float32), jax.ShapeDtypeStruct((8, 128), jnp.float32)],
        in_specs=[vmem] * 5,
        out_specs=[vmem] * 6,
        scratch_shapes=scratch,
        compiler_params=pltpu.CompilerParams(
            collective_id=1, has_side_effects=True, vmem_limit_bytes=48 * 2**20
        ),
    )(*grads, small)


ORDERS = ("xzy", "yzx", "zyx", "zxy")
SEQUENCE = (
    ("norms", 0), ("attn_in", 0), ("attn_out", 0), ("down", 0), ("widen", 0), ("up", 0), ("narrow", 0),
    ("attn_in", 1), ("attn_out", 1), ("attn_in", 2), ("attn_out", 2), ("down", 1), ("widen", 1), ("up", 1),
    ("narrow", 1),
)
COLUMNS = {"norms": 128, "attn_in": 512, "attn_out": 512, "down": 512, "widen": 512, "up": 512, "narrow": 256}
PARTS = {("narrow", 1): 2}
LAG_Z = (3.0, 3.0, 3.0)
LAG_LINE = (8.0, 5.0, 5.5)
LAG_CORE = 3.0
PACE = 0.7
SETTLE = 0.8
HEADS = 16
LEN = 128
MICRO = 2
ROWS = 256
NORM_EPS = 1e-05
NEGATIVE = -1000000000.0
BRANCH_SCALE = 4.0


def hops_of(order, sizes):
    return [(axis, hop) for axis in order for hop in range(1, sizes[axis])]


def plan_units(shapes, names, sizes):
    devices = sizes["z"] * sizes["y"] * sizes["x"] * sizes["c"]
    units, clock = [], 0.0
    load = {"x": 0.85, "y": 0.0, "z": 0.0}
    for name, layer in SEQUENCE:
        if name not in names:
            continue
        rows, columns = shapes[name]
        step = min(COLUMNS[name], columns)
        parts = PARTS.get((name, layer), 1)
        if rows % (16 * parts):
            parts = 1
        height = rows // parts
        for left in range(0, columns, step):
            for top in range(0, rows, height):
                size = height * devices * step / 2**19
                best = None
                for order in ORDERS:
                    after, held = dict(load), 1
                    for axis in order:
                        after[axis] += size * held * (sizes[axis] - 1) * sizes["c"] / devices
                        held *= sizes[axis]
                    score = sum(value**4 for value in after.values())
                    if best is None or score < best[0]:
                        best = (score, order, after)
                load = best[2]
                units.append((name, layer, left, step, top, height, clock, best[1]))
                clock += size
    return units


def stage_clocks(unit, sizes):
    order = unit[7]
    found = [0.0]
    for axis, _ in hops_of(order, sizes):
        found.append(found[-1] + (LAG_Z if axis == "z" else LAG_LINE)[order.index(axis)])
    found.append(found[-1] + LAG_CORE)
    scale = min(1.0, 0.6 + unit[6] / 20.0)
    return [unit[6] + scale * value for value in found]


def dot(left, right):
    return jnp.dot(left, right, preferred_element_type=jnp.float32)


def dot_rows(left, right):
    return lax.dot_general(left, right, (((1,), (1,)), ((), ())), preferred_element_type=jnp.float32)


def dot_columns(left, right):
    return lax.dot_general(left, right, (((0,), (0,)), ((), ())), preferred_element_type=jnp.float32)


def low(value):
    return value.astype(jnp.bfloat16)


def wide(value):
    return value.astype(jnp.float32)


def norm_rows(value, gain, bias):
    centred = value - jnp.mean(value, -1, keepdims=True)
    inv_std = lax.rsqrt(jnp.mean(centred * centred, -1, keepdims=True) + NORM_EPS)
    normed = centred * inv_std
    return normed * gain + bias, normed, inv_std


def gelu_pair(value):
    half = 0.5 * (1.0 + lax.erf(value * 0.7071067811865476))
    return value * half, half + value * jnp.exp(-0.5 * value * value) * 0.3989422804014327


def lane_masks():
    lanes = lax.broadcasted_iota(jnp.int32, (LEN, 128), 1)
    first = (lanes < 64).astype(jnp.float32).astype(jnp.bfloat16)
    return first, (lanes >= 64).astype(jnp.float32).astype(jnp.bfloat16)


def stack_heads(value, masks):
    return jnp.concatenate([value * masks[0], value * masks[1]], 0)


def attend_pair(qkv, probs, attended, seq, pair, keep):
    masks = lane_masks()
    rows = pl.ds(pl.multiple_of(seq * LEN, LEN), LEN)

    def columns(part):
        return pl.ds(pl.multiple_of(part * 1024 + pair * 128, 128), 128)

    queries, keys, values = (qkv[rows, columns(part)] for part in range(3))
    scores = dot_rows(stack_heads(queries, masks), keys) * 0.125
    scores = jnp.where(keep(seq), scores, NEGATIVE)
    spread = jnp.exp(scores - jnp.max(scores, -1, keepdims=True))
    chance = low(spread / jnp.sum(spread, -1, keepdims=True))
    probs[seq, pair] = chance
    side = jnp.concatenate([chance[:LEN], chance[LEN:]], 1)
    attended[rows, columns(0)] = low(dot(side, stack_heads(values, masks)))


def forward_kernel(sizes, units, names, *refs):
    refs = list(refs)

    def take(count):
        found = refs[:count]
        del refs[:count]
        return found

    count = len(names)
    ins = dict(zip(names, take(count)))
    picked, places, key_keep, owned = take(4)
    extra_up = None if "up" in names else take(1)[0]
    outs = dict(zip(names, take(count)))
    saved_out = take(8)
    send_sem, recv_sem, local_sem, sib_send, sib_recv = take(5)
    saved = take(8)
    qkv_all, probs_all, normed_all, inv_all, feed_in, slopes, bottles, decoded = saved
    embed_sem, embed_here, embed_core, embed_line = take(4)
    norm_tile, norms = take(2)
    stream, stream_low, memory, attended, branch, hidden = take(6)
    tiles, tall_tiles, tile_sem, tall_sem, save_sem = take(5)
    here = position(sizes)

    def at_device(**moved):
        return device_at(here, sizes, **moved)

    barrier = pltpu.get_barrier_semaphore()
    pl.semaphore_signal(barrier, inc=1, device_id=at_device(c=1 - here["c"]), device_id_type=MESH_ID)
    peers = jnp.int32(1)
    for step in range(1, sizes["x"]):
        other = (here["x"] + step) % sizes["x"]
        pl.semaphore_signal(barrier, inc=1, device_id=at_device(x=other), device_id_type=MESH_ID)
        peers = peers + 1
    for axis in "zy":
        for step in (-1, 1):
            ok = (here[axis] + step >= 0) & (here[axis] + step < sizes[axis])
            peers = peers + ok.astype(jnp.int32)

            @pl.when(ok)
            def _(axis=axis, step=step):
                pl.semaphore_signal(
                    barrier, inc=1, device_id=at_device(**{axis: here[axis] + step}), device_id_type=MESH_ID
                )

    pl.semaphore_wait(barrier, peers)

    everything = slice(None)

    def own_source(unit):
        name, layer, left, width, top, height = unit[:6]
        return ins[name].at[layer, pl.ds(top, height), pl.ds(left, width)]

    def piece(unit, index):
        name, layer, left, width, top, height = unit[:6]
        return outs[name].at[(layer,) + index + (pl.ds(top, height), pl.ds(left, width))]

    def view(unit, order, axis, coordinate):
        place = order.index(axis)
        at = {other: everything if order.index(other) < place else here[other] for other in "zyx"}
        at[axis] = coordinate
        return piece(unit, (at["z"], at["y"], at["x"], here["c"]))

    def sends(number, stage):
        unit, order = units[number], units[number][7]
        axis, hop = hops_of(order, sizes)[stage]
        size, mine = sizes[axis], here[axis]
        first = order.index(axis) == 0
        found = []
        for way, step in enumerate((1, -1)):
            origin = mine - step * (hop - 1)
            ok = (origin >= 0) & (origin < size) & (mine + step >= 0) & (mine + step < size)
            origin_r = mine - step * hop
            ok_r = (origin_r >= 0) & (origin_r < size)

            def build(receive, step=step, way=way, origin=origin, origin_r=origin_r):
                which = origin_r if receive else origin
                fresh = first and hop == 1 and not receive
                return pltpu.make_async_remote_copy(
                    src_ref=own_source(unit) if fresh else view(unit, order, axis, which),
                    dst_ref=view(unit, order, axis, which),
                    send_sem=send_sem.at[number, stage * 2 + way],
                    recv_sem=recv_sem.at[number, stage * 2 + way],
                    device_id=at_device(**{axis: mine + step}),
                    device_id_type=MESH_ID,
                )

            found.append((ok, ok_r, build))
        return found

    def local_copy(number):
        index = tuple(here[axis] for axis in "zyxc")
        return pltpu.make_async_copy(own_source(units[number]), piece(units[number], index), local_sem.at[number])

    def sibling(number):
        plane = piece(units[number], (everything, everything, everything, here["c"]))
        return pltpu.make_async_remote_copy(
            src_ref=plane,
            dst_ref=plane,
            send_sem=sib_send.at[number],
            recv_sem=sib_recv.at[number],
            device_id=at_device(c=1 - here["c"]),
            device_id_type=MESH_ID,
        )

    depth = sum(sizes[axis] - 1 for axis in "zyx")

    def comm_step(number, stage):
        if stage == 0:
            local_copy(number).start()
        if 1 <= stage <= depth:
            for _, ok_r, build in sends(number, stage - 1):

                @pl.when(ok_r)
                def _(build=build):
                    build(True).wait_recv()

        if stage == sizes[units[number][7][0]] - 1:
            local_copy(number).wait()
        if stage < depth:
            for ok, _, build in sends(number, stage):

                @pl.when(ok)
                def _(build=build):
                    build(False).start()

        if stage == depth:
            sibling(number).start()
        if stage == depth + 1:
            sibling(number).wait_recv()

    mine, column = here["c"], here["x"]

    def embed_first(group):
        return pltpu.make_async_remote_copy(
            src_ref=picked.at[:, 1 - mine, group],
            dst_ref=embed_core.at[group],
            send_sem=embed_sem.at[0, group],
            recv_sem=embed_sem.at[1, group],
            device_id=at_device(c=1 - mine),
            device_id_type=MESH_ID,
        )

    def embed_local(group):
        return pltpu.make_async_copy(picked.at[:, mine, group], embed_here.at[group], embed_sem.at[2, group])

    def embed_second(group, step):
        other = (column + step) % sizes["x"]
        return pltpu.make_async_remote_copy(
            src_ref=embed_here.at[group, other],
            dst_ref=embed_line.at[group, step - 1],
            send_sem=embed_sem.at[2 + step * 2 - 1, group],
            recv_sem=embed_sem.at[2 + step * 2, group],
            device_id=at_device(x=other),
            device_id_type=MESH_ID,
        )

    def embed_pass(group):
        embed_first(group).wait_recv()
        embed_local(group).wait()
        here_keep, core_keep = (jnp.concatenate([owned[core, group]] * 8, -1) for core in range(2))
        embed_here[group] = embed_here[group] * here_keep + embed_core[group] * core_keep
        for step in range(1, sizes["x"]):
            embed_second(group, step).start()

    def embed_rows(group):
        rows = wide(embed_here[group, column])
        for step in range(1, sizes["x"]):
            embed_second(group, step).wait_recv()
            rows = rows + wide(embed_line[group, step - 1])
        place = wide(places[group])
        return rows + jnp.concatenate([place] * MICRO, 0)

    saves = []

    def save(place, index):
        def build(number=len(saves)):
            return pltpu.make_async_copy(
                saved[place].at[index] if index else saved[place],
                saved_out[place].at[index] if index else saved_out[place],
                save_sem.at[number],
            )

        saves.append(build)
        build().start()

    def norm_step(value, which, side):
        result, normed, inv_std = norm_rows(value, norms[which : which + 1, :], norms[which + 7 : which + 8, :])
        normed_all[which] = normed
        inv_all[which] = jnp.broadcast_to(inv_std, (ROWS, 128))
        save(2, (which,))
        save(3, (which,))
        stream[side] = result
        stream_low[side] = low(result)

    def begin(side):
        def run():
            if side == 0:
                copy = pltpu.make_async_copy(outs["norms"].at[0], norm_tile, tile_sem.at[len(tiles_used)])
                copy.start()
                copy.wait()
                columns = norm_tile[...].reshape(-1, 128)
                norms[...] = columns.T[:16]
            norm_step(embed_rows(side), 3 * side, side)

        return run

    tiles_used = [None] * tiles.shape[0]

    def project(which, left, side, from_memory):
        def run(tile):
            source = memory[...] if from_memory else stream_low[side]
            qkv_all[which, :, pl.ds(left, 512)] = low(dot(source, tile()))

        return run

    def attention(which, start, keep):
        def run():
            def body(number, _):
                seq, pair = number // 8, number % 8
                attend_pair(qkv_all.at[which], probs_all.at[which], attended, seq, pair, keep)
                return 0

            lax.fori_loop(start, start + 4, body, 0)

        return run

    def project_out(left):
        def run(tile):
            branch[:, pl.ds(left, 512)] = dot(attended[...], tile())

        return run

    def finish_attention(which, norm, side):
        def run():
            save(0, (which,))
            save(1, (which,))
            norm_step(stream[side] + branch[...], norm, side)

        return run

    def narrow_down(side):
        def run(tile):
            feed_in[side] = stream_low[side]
            value, slope = gelu_pair(dot(stream_low[side], tile()))
            bottles[side, 0] = low(value)
            bottles[side, 1] = low(slope)
            save(4, (side,))
            save(6, (side,))

        return run

    def widen(left, side):
        def run(tile):
            value, slope = gelu_pair(dot(stream_low[side], tile()))
            hidden[:, pl.ds(left, 512)] = low(value)
            slopes[side, :, pl.ds(left, 512)] = low(slope)

        return run

    def raise_up(left, side):
        def run(tile):
            branch[:, pl.ds(left, 512)] = BRANCH_SCALE * dot(bottles[side, 0], tile())

        return run

    def narrow(left, side):
        def run(tile):
            branch[:, pl.ds(left, 256)] += dot(hidden[...], tile())

        return run

    def finish_feed(norm, side):
        def run():
            save(5, (side,))
            norm_step(stream[side] + branch[...], norm, side)
            if side == 0:
                memory[...] = stream_low[0]
            else:
                decoded[...] = stream_low[1]
                save(7, ())

        return run

    def source_keep(seq):
        return jnp.broadcast_to(key_keep[seq, 0:1, :] > 0.0, (2 * LEN, LEN))

    def causal_keep(seq):
        query = lax.broadcasted_iota(jnp.int32, (2 * LEN, LEN), 0) % LEN
        return lax.broadcasted_iota(jnp.int32, (2 * LEN, LEN), 1) <= query

    steps = []
    members = {}
    for number, unit in enumerate(units):
        members.setdefault(unit[:3], []).append(number)

    def add(run, cost, unit=None, clock=0.0):
        steps.append((unit, cost, clock, run))

    def attention_steps(which, norm, side, keep):
        for left in range(0, 3072, 512):
            from_memory = which == 2 and left >= 1024
            add(project(which, left, side, from_memory), 0.6, ("attn_in", which, left))
        for start in range(0, 16, 4):
            add(attention(which, start, keep), 2.0)
        for left in range(0, 1024, 512):
            add(project_out(left), 0.6, ("attn_out", which, left))
        add(finish_attention(which, norm, side), 1.0)

    def feed_steps(norm, side):
        add(narrow_down(side), 1.3, ("down", side, 0))
        for left in range(0, 4096, 512):
            add(widen(left, side), 1.3, ("widen", side, left))
        for left in range(0, 1024, 512):
            if "up" in names:
                add(raise_up(left, side), 0.4, ("up", side, left))
            else:
                part = functools.partial(lambda left, side: extra_up[side, :, pl.ds(left, 512)], left, side)
                add(functools.partial(raise_up(left, side), part), 0.4)
        for left in range(0, 1024, 256):
            add(narrow(left, side), 1.0, ("narrow", side, left))
        add(finish_feed(norm, side), 1.0)

    add(begin(0), 2.0, ("norms", 0, 0), 8.0)
    attention_steps(0, 1, 0, source_keep)
    feed_steps(2, 0)
    add(begin(1), 1.5, None, 20.0)
    attention_steps(1, 4, 1, causal_keep)
    attention_steps(2, 5, 1, source_keep)
    feed_steps(6, 1)

    loads = [step[0] for step in steps if step[0] is not None and step[0][0] != "norms"]
    slot_of, rings = {}, {"tall": [], "flat": []}
    for unit in loads:
        kind = "tall" if unit[0] == "narrow" else "flat"
        ring = rings[kind]
        size = (tall_tiles if kind == "tall" else tiles).shape[0]
        slot_of[unit] = (kind, len(ring) % size, ring[len(ring) - size] if len(ring) >= size else None)
        ring.append(unit)

    def tile_parts(unit):
        kind, slot, _ = slot_of[unit]
        name, layer, left = unit
        width = units[members[unit][0]][3]
        source = outs[name].at[layer, :, :, :, :, :, pl.ds(left, width)]
        buffer = (tall_tiles if kind == "tall" else tiles).at[slot]
        sem = (tall_sem if kind == "tall" else tile_sem).at[slot]
        rows = ins[name].shape[1] * sizes["z"] * sizes["y"] * sizes["x"] * sizes["c"]
        target = buffer.at[pl.ds(0, rows)]
        shape = tuple(sizes[axis] for axis in "zyxc") + (ins[name].shape[1], width)
        return pltpu.make_async_copy(source, target.reshape(shape), sem), target

    complete, loaded, done, moment = set(), {}, set(), [0.0]
    waiting = list(loads)

    def try_loads():
        while waiting:
            unit = waiting[0]
            before = slot_of[unit][2]
            if unit not in complete or (before is not None and before not in done):
                return
            tile_parts(unit)[0].start()
            loaded[unit] = moment[0]
            waiting.pop(0)

    queue = list(steps)

    def run_step():
        unit, cost, _, run = queue.pop(0)
        if unit is None or unit[0] == "norms":
            run()
        else:
            copy, target = tile_parts(unit)
            copy.wait()
            run(lambda: target[...])
            done.add(unit)
        try_loads()
        return cost

    def ready(clock):
        if not queue:
            return False
        unit, _, earliest, _ = queue[0]
        if earliest > clock:
            return False
        if unit is None:
            return True
        if unit[0] == "norms":
            return unit in complete
        return unit in loaded and clock - loaded[unit] >= SETTLE

    for group in range(2):
        embed_first(group).start()
        embed_local(group).start()
    events = sorted(
        (clock, -stage, number)
        for number, unit in enumerate(units)
        for stage, clock in enumerate(stage_clocks(unit, sizes))
    )
    embed_done, credit, last, arrived = [], 0.0, 0.0, set()
    for clock, minus, number in events:
        stage, moment[0] = -minus, clock
        comm_step(number, stage)
        for group in range(2):
            if group not in embed_done and clock >= 1.5 + 1.5 * group:
                embed_done.append(group)
                embed_pass(group)
        if stage == depth + 1:
            arrived.add(number)
            block = units[number][:3]
            if all(part in arrived for part in members[block]):
                complete.add(block)
                try_loads()
        credit = min(credit + 3.7 * PACE * (clock - last), 4.0)
        last = clock
        while ready(clock) and credit > 0.0:
            credit -= run_step()
    while queue:
        run_step()
    for build in saves:
        build().wait()
    for group in range(2):
        embed_first(group).wait_send()
        for step in range(1, sizes["x"]):
            embed_second(group, step).wait_send()
    for number in range(len(units)):
        sibling(number).wait_send()
        for stage in range(depth):
            for ok, _, build in sends(number, stage):

                @pl.when(ok)
                def _(build=build):
                    build(False).wait_send()


def run_forward(arrays, picked, places, key_keep, owned, dp, vocab):
    sizes = grid_of(dp, vocab)
    grid = tuple(sizes[axis] for axis in "zyxc")
    extra = []
    arrays = dict(arrays)
    if arrays["up"].shape[1] % 8:
        extra = [lax.all_gather(arrays.pop("up"), ("dp", "vocab"), axis=1, tiled=True)]
    names = list(arrays)
    shapes = {name: arrays[name].shape[1:] for name in names}
    units = plan_units(shapes, names, sizes)
    depth = sum(sizes[axis] - 1 for axis in "zyx")
    anywhere, vmem = pl.BlockSpec(memory_space=pl.ANY), pl.BlockSpec(memory_space=pltpu.VMEM)
    f32, b16 = jnp.float32, jnp.bfloat16
    saved = [
        ((3, ROWS, 3072), b16),
        ((3, MICRO, 8, 2 * LEN, LEN), b16),
        ((7, ROWS, 1024), f32),
        ((7, ROWS, 128), f32),
        ((2, ROWS, 1024), b16),
        ((2, ROWS, 4096), b16),
        ((2, 2, ROWS, 512), b16),
        ((ROWS, 1024), b16),
    ]
    out_shape = [
        jax.ShapeDtypeStruct((arrays[name].shape[0],) + grid + arrays[name].shape[1:], arrays[name].dtype)
        for name in names
    ] + [jax.ShapeDtypeStruct(shape, kind) for shape, kind in saved]
    x, n = sizes["x"], len(units)
    dma = pltpu.SemaphoreType.DMA
    out = pl.pallas_call(
        functools.partial(forward_kernel, sizes, units, names),
        out_shape=out_shape,
        in_specs=[anywhere] * (len(names) + 1) + [vmem] * (3 + len(extra)),
        out_specs=[anywhere] * len(out_shape),
        scratch_shapes=[dma((n, 2 * depth)), dma((n, 2 * depth)), dma((n,)), dma((n,)), dma((n,))]
        + [pltpu.VMEM(shape, kind) for shape, kind in saved]
        + [
            dma((3 + 2 * x, 2)),
            pltpu.VMEM((2, x, ROWS, 1024), b16),
            pltpu.VMEM((2, x, ROWS, 1024), b16),
            pltpu.VMEM((2, x - 1, ROWS, 1024), b16),
            pltpu.VMEM(grid + arrays["norms"].shape[1:], f32),
            pltpu.VMEM((16, 1024), f32),
            pltpu.VMEM((2, ROWS, 1024), f32),
            pltpu.VMEM((2, ROWS, 1024), b16),
            pltpu.VMEM((ROWS, 1024), b16),
            pltpu.VMEM((ROWS, 1024), b16),
            pltpu.VMEM((ROWS, 1024), f32),
            pltpu.VMEM((ROWS, 4096), b16),
            pltpu.VMEM((6, 1024, 512), b16),
            pltpu.VMEM((3, 4096, 256), b16),
            dma((7,)),
            dma((3,)),
            dma((32,)),
        ],
        compiler_params=pltpu.CompilerParams(
            collective_id=0, has_side_effects=True, vmem_limit_bytes=61 * 2**20
        ),
    )(*[arrays[name] for name in names], picked, places, key_keep, owned, *extra)
    held = dict(zip(names, out[: len(names)]))
    if extra:
        held["up"] = extra[0]
    return held, out[len(names) :]


TILE = 1280


def head_kernel(sizes, *refs):
    decoded, targets, weight, table_hbm, grad_out, loss_out = refs[:6]
    rows, table, logits, partial, core_send, core_part, line_send, line_part, stats = refs[6:15]
    table_sem, row_sem, stat_sem, core_sem, line_sem, send_sem = refs[15:]
    here = position(sizes)
    mine, column, cores, across = here["c"], here["x"], sizes["c"], sizes["x"]
    owners = across * cores
    me, twin = column * cores + mine, column * cores + 1 - mine
    count = table.shape[0]
    steps = count // TILE

    def table_copy(number):
        part = pl.ds(number * TILE, TILE)
        return pltpu.make_async_copy(table_hbm.at[part], table.at[part], table_sem.at[number])

    for number in range(steps):
        table_copy(number).start()
    barrier = pltpu.get_barrier_semaphore()
    for step in range(1, owners):
        other = (me + step) % owners
        pl.semaphore_signal(
            barrier,
            inc=1,
            device_id=device_at(here, sizes, x=other // cores, c=other % cores),
            device_id_type=MESH_ID,
        )
    pl.semaphore_wait(barrier, owners - 1)
    started = []

    def remote(src, dst, arrival, **moved):
        copy = pltpu.make_async_remote_copy(
            src_ref=src,
            dst_ref=dst,
            send_sem=send_sem.at[len(started)],
            recv_sem=arrival,
            device_id=device_at(here, sizes, **moved),
            device_id_type=MESH_ID,
        )
        copy.start()
        started.append(copy)

    def arrived(ref, arrival):
        pltpu.make_async_remote_copy(
            src_ref=ref,
            dst_ref=ref,
            send_sem=send_sem.at[0],
            recv_sem=arrival,
            device_id=device_at(here, sizes, c=1 - mine),
            device_id_type=MESH_ID,
        ).wait_recv()

    def far(step, core):
        return (column + step) % across * cores + core

    rows[me] = decoded[...]
    for step in range(1, across):
        remote(rows.at[me], rows.at[me], row_sem.at[me], x=(column + step) % across)
    remote(rows.at[me], rows.at[me], row_sem.at[me], c=1 - mine)
    lane = lax.broadcasted_iota(jnp.int32, (ROWS, 128), 1)

    def first_pass(block, fresh=False):
        wanted = targets[block] - me * count

        def body(number, carry):
            top, spread, hit = carry
            start = pl.multiple_of(number * TILE, TILE)
            if fresh:
                part = pl.ds(start, TILE)
                pltpu.make_async_copy(table_hbm.at[part], table.at[part], table_sem.at[number]).wait()
            values = dot_rows(rows[block], table[pl.ds(start, TILE), :])
            logits[block, :, pl.ds(start, TILE)] = values
            parts = [values[:, at : at + 128] for at in range(0, TILE, 128)]
            new_top = top
            for part in parts:
                new_top = jnp.maximum(new_top, part)
            spread = spread * jnp.exp(top - new_top)
            near = wanted - start - lane
            for place, part in enumerate(parts):
                spread = spread + jnp.exp(part - new_top)
                hit = hit + jnp.where(near == place * 128, part, 0.0)
            return new_top, spread, hit

        zero = jnp.zeros((ROWS, 128), jnp.float32)
        low_start = jnp.full((ROWS, 128), -3e38, jnp.float32)
        top, spread, hit = lax.fori_loop(0, steps, body, (low_start, zero, zero))
        whole = jnp.max(top, -1, keepdims=True)
        spread = jnp.sum(spread * jnp.exp(top - whole), -1, keepdims=True)
        hit = jnp.sum(hit, -1, keepdims=True)
        stats[block, me] = jnp.where(lane == 0, whole, jnp.where(lane == 1, spread, hit)).T[:8]
        for step in range(1, owners):
            other = (me + step) % owners
            remote(
                stats.at[block, me],
                stats.at[block, me],
                stat_sem.at[block, me],
                x=other // cores,
                c=other % cores,
            )

    def second_pass(block, place):
        for step in range(1, owners):
            other = (me + step) % owners
            arrived(stats.at[block, other], stat_sem.at[block, other])
        found = [stats[block, index] for index in range(owners)]
        top = found[0][0:1]
        for value in found[1:]:
            top = jnp.maximum(top, value[0:1])
        spread, hit = jnp.zeros_like(top), jnp.zeros_like(top)
        for value in found:
            spread = spread + value[1:2] * jnp.exp(value[0:1] - top)
            hit = hit + value[2:3]
        log_total = top + jnp.log(spread)
        level = jnp.broadcast_to(log_total, (128, ROWS)).T
        wanted = targets[block] - me * count
        partial[place] = jnp.zeros((ROWS, 1024), jnp.float32)

        def body(number, _):
            start = pl.multiple_of(number * TILE, TILE)
            near = wanted - start - lane
            values = logits[block, :, pl.ds(start, TILE)]
            parts = []
            for index in range(TILE // 128):
                value = jnp.exp(values[:, index * 128 : (index + 1) * 128] - level)
                parts.append(low(jnp.where(near == index * 128, value - 1.0, value)))
            partial[place] += dot(jnp.concatenate(parts, 1), table[pl.ds(start, TILE), :])
            return 0

        lax.fori_loop(0, steps, body, 0)
        return log_total - hit

    first_pass(me, True)
    arrived(rows.at[twin], row_sem.at[twin])
    first_pass(twin)
    for step in range(1, across):
        block = far(step, mine)
        arrived(rows.at[block], row_sem.at[block])
        remote(rows.at[block], rows.at[block], row_sem.at[block], c=1 - mine)
        first_pass(block)
    for step in range(1, across):
        block = far(step, 1 - mine)
        arrived(rows.at[block], row_sem.at[block])
        first_pass(block)
    for step in range(1, across):
        for core in range(cores):
            second_pass(far(step, core), core)

            @pl.when(mine != core)
            def _(core=core, step=step):
                core_send[step - 1] = low(partial[core])
                pltpu.make_async_remote_copy(
                    src_ref=core_send.at[step - 1],
                    dst_ref=core_part.at[step - 1],
                    send_sem=core_sem.at[0, step - 1],
                    recv_sem=core_sem.at[1, step - 1],
                    device_id=device_at(here, sizes, c=1 - mine),
                    device_id_type=MESH_ID,
                ).start()

        arrived(core_part.at[step - 1], core_sem.at[1, step - 1])
        line_send[step - 1] = low(partial[mine] + wide(core_part[step - 1]))
        remote(
            line_send.at[step - 1],
            line_part.at[step - 1],
            line_sem.at[step - 1],
            x=(column + step) % across,
        )
    second_pass(twin, 0)
    last = across - 1
    core_send[last] = low(partial[0])
    remote(core_send.at[last], core_part.at[last], core_sem.at[1, last], c=1 - mine)
    loss = second_pass(me, 1)
    loss_out[...] = jnp.broadcast_to(loss, (8, ROWS))
    arrived(core_part.at[last], core_sem.at[1, last])
    value = partial[1] + wide(core_part[last])
    for step in range(1, across):
        arrived(line_part.at[step - 1], line_sem.at[step - 1])
        value = value + wide(line_part[step - 1])
    grad_out[...] = value * weight[:, :1]
    for copy in started:
        copy.wait_send()
    for step in range(1, across):
        pltpu.make_async_remote_copy(
            src_ref=core_send.at[step - 1],
            dst_ref=core_part.at[step - 1],
            send_sem=core_sem.at[0, step - 1],
            recv_sem=core_sem.at[1, step - 1],
            device_id=device_at(here, sizes, c=1 - mine),
            device_id_type=MESH_ID,
        ).wait_send()


def run_head(decoded, targets, weight, table, dp, vocab):
    sizes = grid_of(dp, vocab)
    across, owners = sizes["x"], vocab
    f32, b16 = jnp.float32, jnp.bfloat16
    anywhere, vmem = pl.BlockSpec(memory_space=pl.ANY), pl.BlockSpec(memory_space=pltpu.VMEM)
    dma = pltpu.SemaphoreType.DMA
    return pl.pallas_call(
        functools.partial(head_kernel, sizes),
        out_shape=[jax.ShapeDtypeStruct((ROWS, 1024), f32), jax.ShapeDtypeStruct((8, ROWS), f32)],
        in_specs=[vmem] * 3 + [anywhere],
        out_specs=[vmem] * 2,
        scratch_shapes=[
            pltpu.VMEM((owners, ROWS, 1024), b16),
            pltpu.VMEM(table.shape, b16),
            pltpu.VMEM((owners, ROWS, table.shape[0]), f32),
            pltpu.VMEM((2, ROWS, 1024), f32),
            pltpu.VMEM((across, ROWS, 1024), b16),
            pltpu.VMEM((across, ROWS, 1024), b16),
            pltpu.VMEM((across - 1, ROWS, 1024), b16),
            pltpu.VMEM((across - 1, ROWS, 1024), b16),
            pltpu.VMEM((owners, owners, 8, ROWS), f32),
            dma((table.shape[0] // TILE,)),
            dma((owners,)),
            dma((owners, owners)),
            dma((2, across)),
            dma((across,)),
            dma((8 * owners,)),
        ],
        compiler_params=pltpu.CompilerParams(
            collective_id=3, has_side_effects=True, vmem_limit_bytes=62 * 2**20
        ),
    )(
        decoded,
        jnp.broadcast_to(targets.reshape(owners, ROWS, 1), (owners, ROWS, 128)),
        jnp.broadcast_to(weight.reshape(ROWS, 1), (ROWS, 128)),
        table,
    )


def backward_kernel(sizes, *refs):
    refs = list(refs)

    def take(count):
        found = refs[:count]
        del refs[:count]
        return found

    grad_in, norms, extra = take(3)
    names = ("attn_in", "attn_out", "widen", "narrow", "down", "up")
    held = dict(zip(names, take(6)))
    saved_in = take(7)
    shards = take(4)
    small_out, square_out = take(2)
    saved = take(7)
    qkv_all, probs_all, normed_ring, inv_all, feed_in, slopes, bottles = saved
    saved_sem, normed_sem, tiles, tile_sem, down_tile, down_sem = take(6)
    grads = take(4)
    sums, core_send, core_recv = take(4), take(4), take(4)
    wide_send, wide_recv, mid_send, mid_recv, last_send, last_recv = (take(4) for _ in range(6))
    small, small_slots, (late, owner_slots, group_slots) = take(1)[0], take(4), take(3)
    grad_low, grad_sum, grad_memory, grad_hidden, grad_att, packed = take(6)
    send_sem, recv_sem = take(2)
    here = position(sizes)
    mine = here["c"]

    loads = {}

    def fetch(place, index):
        if (place, index) not in loads:
            copy = pltpu.make_async_copy(
                saved_in[place].at[index], saved[place].at[index], saved_sem.at[len(loads)]
            )
            loads[place, index] = copy
            copy.start()
        return loads[place, index]

    order = (6, 5, 4, 3, 2, 1, 0)

    def normed_copy(number):
        slot = number % normed_ring.shape[0]
        return pltpu.make_async_copy(saved_in[2].at[order[number]], normed_ring.at[slot], normed_sem.at[slot])

    plan = []
    block = 1024
    for kind, which in (("feed", 1), ("attend", 2), ("attend", 1), ("feed", 0), ("attend", 0)):
        if kind == "feed":
            for left in range(0, 4096, block):
                plan += [("narrow", which, left), ("widen", which, left)]
            plan.append(("up", which, 0))
        else:
            plan.append(("attn_out", which, 0))
            plan += [("attn_in", which, left) for left in range(0, 3072, block)]
    grid = tuple(sizes[axis] for axis in "zyxc")
    depth = tiles.shape[0]

    def tile_copy(number):
        name, layer, left = plan[number]
        rows, columns = held[name].shape[5:]
        buffer = tiles.at[number % depth]
        if name == "narrow":
            planes = left // block
            source, shape = held[name].at[layer, planes], grid[1:] + (rows, columns)
        else:
            columns = min(columns, block)
            source = held[name].at[layer, :, :, :, :, :, pl.ds(left, columns)]
            shape = grid + (rows, columns)
        count = 1
        for size in shape[:-1]:
            count *= size
        target = buffer.at[pl.ds(0, count), pl.ds(0, columns)]
        return pltpu.make_async_copy(source, target.reshape(shape), tile_sem.at[number % depth]), target

    def down_copy(side):
        target = down_tile.reshape(grid + held["down"].shape[5:])
        return pltpu.make_async_copy(held["down"].at[side], target, down_sem.at[0])

    turn = [0]

    def with_tile(use):
        number = turn[0]
        turn[0] += 1
        copy, target = tile_copy(number)
        copy.wait()
        result = use(target[...])
        if number + depth < len(plan):
            tile_copy(number + depth)[0].start()
        return result

    for number in range(2):
        normed_copy(number).start()
    fetch(3, slice(None))
    fetch(5, 1)
    for number in range(depth):
        tile_copy(number)[0].start()
    down_copy(1).start()
    for place, index in ((6, 1), (4, 1), (0, 2), (1, 2), (0, 1), (1, 1), (5, 0), (6, 0), (4, 0), (0, 0), (1, 0)):
        fetch(place, index)
    barrier = pltpu.get_barrier_semaphore()
    owners, groups = sizes["x"] * sizes["c"], sizes["z"] * sizes["y"]
    owner, group = here["x"] * sizes["c"] + here["c"], here["z"] * sizes["y"] + here["y"]

    def owner_at(step):
        other = (owner + step) % owners
        return {"x": other // sizes["c"], "c": other % sizes["c"]}

    def group_at(step):
        other = (group + step) % groups
        return {"z": other // sizes["y"], "y": other % sizes["y"]}

    peers = [owner_at(step) for step in range(1, owners)] + [group_at(step) for step in range(1, groups)]
    for peer in peers:
        pl.semaphore_signal(barrier, inc=1, device_id=device_at(here, sizes, **peer), device_id_type=MESH_ID)
    pl.semaphore_wait(barrier, len(peers))

    used, started = [0], []

    def copy_to(src, dst, **moved):
        number = used[0]
        used[0] += 1
        copy = pltpu.make_async_remote_copy(
            src_ref=src,
            dst_ref=dst,
            send_sem=send_sem.at[number],
            recv_sem=recv_sem.at[number],
            device_id=device_at(here, sizes, **moved),
            device_id_type=MESH_ID,
        )
        copy.start()
        started.append(copy)
        return copy

    def share(slots, value, axis):
        slots[here[axis]] = value
        return [
            copy_to(slots.at[here[axis]], slots.at[here[axis]], **{axis: (here[axis] + step) % sizes[axis]})
            for step in range(1, sizes[axis])
        ]

    def total(slots, axis, copies):
        for copy in copies:
            copy.wait_recv()
        value = slots[0]
        for index in range(1, sizes[axis]):
            value = value + slots[index]
        return value

    plans = (("x", "y"), ("y", "x"), ("x", "y"), ("y", "x"))
    pending = [None] * 4

    def phase_core(parts):
        for part in parts:
            core_send[part][...] = low(grads[part][:, :, :, 1 - mine])
            pending[part] = copy_to(core_send[part], core_recv[part], c=1 - mine)

    def phase_wide(parts):
        for part in parts:
            pending[part].wait_recv()
            sums[part][...] = grads[part][:, :, :, mine] + wide(core_recv[part][...])
            axis = plans[part][0]
            found = []
            for step in range(1, sizes[axis]):
                other = (here[axis] + step) % sizes[axis]
                value = sums[part][:, :, other] if axis == "x" else sums[part][:, other]
                wide_send[part][step - 1] = low(value)
                found.append(copy_to(wide_send[part].at[step - 1], wide_recv[part].at[step - 1], **{axis: other}))
            pending[part] = found

    def phase_mid(parts):
        for part in parts:
            axis, later = plans[part]
            kept = sums[part].at[:, :, here["x"]] if axis == "x" else sums[part].at[:, here["y"]]
            value = kept[...]
            for step, copy in enumerate(pending[part]):
                copy.wait_recv()
                value = value + wide(wide_recv[part][step])
            kept[...] = value
            found = []
            for step in range(1, sizes[later]):
                other = (here[later] + step) % sizes[later]
                mid_send[part][step - 1] = low(kept[:, other])
                found.append(copy_to(mid_send[part].at[step - 1], mid_recv[part].at[step - 1], **{later: other}))
            pending[part] = found

    def phase_last(parts):
        for part in parts:
            kept = sums[part].at[:, here["y"], here["x"]]
            value = kept[...]
            for step, copy in enumerate(pending[part]):
                copy.wait_recv()
                value = value + wide(mid_recv[part][step])
            kept[...] = value
            found = []
            for step in range(1, sizes["z"]):
                other = (here["z"] + step) % sizes["z"]
                last_send[part][step - 1] = low(kept[other])
                found.append(copy_to(last_send[part].at[step - 1], last_recv[part].at[step - 1], z=other))
            pending[part] = found

    def phase_end(parts):
        square = jnp.zeros((1, 1), jnp.float32)
        for part in parts:
            value = sums[part][here["z"], here["y"], here["x"]]
            for step, copy in enumerate(pending[part]):
                copy.wait_recv()
                value = value + wide(last_recv[part][step])
            shards[part][...] = value
            square = square + jnp.sum(value * value, keepdims=True)
        return square

    norm_turn = [0]

    def norm_back(grad_out, which):
        number = norm_turn[0]
        norm_turn[0] += 1
        if number + 2 < len(order):
            normed_copy(number + 2).start()
        normed_copy(number).wait()
        normed = normed_ring[number % normed_ring.shape[0]]
        inv_std = inv_all[which][:, :1]
        scaled = grad_out * norms[which : which + 1, :]
        small[which : which + 1, :] = jnp.sum(grad_out * normed, 0, keepdims=True)
        small[which + 7 : which + 8, :] = jnp.sum(grad_out, 0, keepdims=True)
        grad = inv_std * (
            scaled - jnp.mean(scaled, -1, keepdims=True) - normed * jnp.mean(scaled * normed, -1, keepdims=True)
        )
        grad_sum[...] = grad
        grad_low[...] = low(grad)

    def feed_back(side):
        fetch(5, side).wait()
        for left in range(0, 4096, block):

            def first(tile, left=left):
                slope = wide(slopes[side, :, pl.ds(left, block)])
                grad_hidden[...] = low(dot_rows(grad_low[...], tile) * slope)

            def second(tile):
                grad_sum[...] += dot_rows(grad_hidden[...], tile)

            with_tile(first)
            with_tile(second)
        fetch(6, side).wait()
        fetch(4, side).wait()

        def up(tile):
            bottle = low(BRANCH_SCALE * dot_rows(grad_low[...], tile) * wide(bottles[side, 1]))
            grad_hidden[:, pl.ds(0, 512)] = bottle

        with_tile(up)
        down_copy(side).wait()
        grad_sum[...] += dot_rows(grad_hidden[:, pl.ds(0, 512)], down_tile[...])
        if side:
            down_copy(0).start()
        part = 2 * side
        grads[part + 1][...] = (BRANCH_SCALE * dot_columns(bottles[side, 0], grad_low[...])).reshape(
            grads[part + 1].shape
        )
        grads[part][...] = dot_columns(feed_in[side], grad_hidden[:, pl.ds(0, 512)]).reshape(grads[part].shape)

    def attend_back(layer, between=None):
        def first(tile):
            grad_att[...] = low(dot_rows(grad_low[...], tile))

        with_tile(first)
        fetch(0, layer).wait()
        fetch(1, layer).wait()

        def body(number, _):
            seq, pair = number // 8, number % 8
            masks = lane_masks()
            rows = pl.ds(pl.multiple_of(seq * LEN, LEN), LEN)

            def columns(part):
                return pl.ds(pl.multiple_of(part * 1024 + pair * 128, 128), 128)

            queries, keys, values = (qkv_all[layer, rows, columns(part)] for part in range(3))
            grad_out = stack_heads(grad_att[rows, columns(0)], masks)
            chance_low = probs_all[layer, seq, pair]
            chance = wide(chance_low)
            weighed = chance * dot_rows(grad_out, values)
            grad_scores = low(weighed - chance * jnp.sum(weighed, -1, keepdims=True))
            side = jnp.concatenate([grad_scores[:LEN], grad_scores[LEN:]], 1)
            packed[rows, columns(0)] = low(dot(side, stack_heads(keys, masks)) * 0.125)
            packed[rows, columns(1)] = low(dot_columns(grad_scores, stack_heads(queries, masks)) * 0.125)
            packed[rows, columns(2)] = low(dot_columns(chance_low, grad_out))
            return 0

        if between is None:
            lax.fori_loop(0, 8 * MICRO, body, 0, unroll=4)
        else:
            for seq, extra_work in enumerate(between):
                lax.fori_loop(8 * seq, 8 * seq + 8, body, 0, unroll=4)
                extra_work()
        for left in range(0, 3072, block):

            def second(tile, left=left):
                value = dot_rows(packed[:, pl.ds(left, block)], tile)
                if layer == 2 and left == block:
                    grad_memory[...] = value
                elif layer == 2 and left > block:
                    grad_memory[...] += value
                else:
                    grad_sum[...] += value

            with_tile(second)

    small[...] = extra[...]
    fetch(3, slice(None)).wait()
    norm_back(grad_in[...], 6)
    feed_back(1)
    phase_core((2, 3))
    norm_back(grad_sum[...], 5)
    attend_back(2)
    phase_wide((2, 3))
    norm_back(grad_sum[...], 4)
    attend_back(1)
    phase_mid((2, 3))
    norm_back(grad_sum[...], 3)
    norm_back(grad_memory[...], 2)
    feed_back(0)
    phase_core((0, 1))
    phase_last((2, 3))
    norm_back(grad_sum[...], 1)
    chain = [share(small_slots[0], small[...], "c")]

    def halfway():
        phase_wide((0, 1))
        chain.append(share(small_slots[1], total(small_slots[0], "c", chain[0]), "x"))

    def after():
        chain.append(share(small_slots[2], total(small_slots[1], "x", chain[1]), "y"))

    attend_back(0, (halfway, after))
    chain.append(share(small_slots[3], total(small_slots[2], "y", chain[2]), "z"))
    phase_mid((0, 1))
    square = phase_end((2, 3))
    norm_back(grad_sum[...], 0)
    phase_last((0, 1))
    for row in range(2):
        for place in range(8):
            late[8 * row + place : 8 * row + place + 1, :] = small[
                7 * row : 7 * row + 1, 128 * place : 128 * place + 128
            ]
    whole = total(small_slots[3], "z", chain[3])
    small_out[...] = whole
    norm_square = jnp.sum(whole[:14] * whole[:14], keepdims=True)
    square = square + phase_end((0, 1))
    late[16:24, :] = jnp.broadcast_to(square, (8, 128))

    def gather_late(slots, mine_at, count, at, value):
        slots[mine_at] = value
        copies = [copy_to(slots.at[mine_at], slots.at[mine_at], **at(step)) for step in range(1, count)]
        for copy in copies:
            copy.wait_recv()
        value = slots[0]
        for index in range(1, count):
            value = value + slots[index]
        return value

    value = gather_late(owner_slots, owner, owners, owner_at, late[...])
    value = gather_late(group_slots, group, groups, group_at, value)
    for row in range(2):
        for place in range(8):
            small_out[7 * row : 7 * row + 1, 128 * place : 128 * place + 128] = value[
                8 * row + place : 8 * row + place + 1, :
            ]
    norm_square = norm_square + jnp.sum(value[:16] * value[:16], keepdims=True)
    square_out[...] = value[16:24] + norm_square
    for copy in started:
        copy.wait_send()


def run_backward(grad_decoded, norms, extra, held, saved, dp, vocab):
    sizes = grid_of(dp, vocab)
    z, y, x, c = (sizes[axis] for axis in "zyxc")
    names = ("attn_in", "attn_out", "widen", "narrow", "down", "up")
    down, up = held["down"].shape[5:], held["up"].shape[5:]
    tails = (down, up, down, up)
    f32, b16 = jnp.float32, jnp.bfloat16
    anywhere, vmem = pl.BlockSpec(memory_space=pl.ANY), pl.BlockSpec(memory_space=pltpu.VMEM)
    dma = pltpu.SemaphoreType.DMA
    scratch = [pltpu.VMEM(value.shape, value.dtype) for value in saved]
    scratch[2] = pltpu.VMEM((3, ROWS, 1024), f32)
    scratch += [dma((16,)), dma((3,)), pltpu.VMEM((5, 1024, 1024), b16), dma((5,))]
    scratch += [pltpu.VMEM((1024, 512), b16), dma((1,))]
    scratch += [pltpu.VMEM((z, y, x, c) + tail, f32) for tail in tails]
    scratch += [pltpu.VMEM((z, y, x) + tail, f32) for tail in tails]
    for _ in range(2):
        scratch += [pltpu.VMEM((z, y, x) + tail, b16) for tail in tails]
    for lead in (((x - 1, z, y), (y - 1, z, x)), ((y - 1, z), (x - 1, z)), ((z - 1,), (z - 1,))):
        for _ in range(2):
            scratch += [pltpu.VMEM(lead[place % 2] + tail, b16) for place, tail in enumerate(tails)]
    scratch.append(pltpu.VMEM((16, 1024), f32))
    scratch += [pltpu.VMEM((sizes[axis], 16, 1024), f32) for axis in "cxyz"]
    scratch += [pltpu.VMEM(shape, f32) for shape in ((24, 128), (vocab, 24, 128), (dp, 24, 128))]
    scratch += [
        pltpu.VMEM((ROWS, 1024), b16),
        pltpu.VMEM((ROWS, 1024), f32),
        pltpu.VMEM((ROWS, 1024), f32),
        pltpu.VMEM((ROWS, 1024), b16),
        pltpu.VMEM((ROWS, 1024), b16),
        pltpu.VMEM((ROWS, 3072), b16),
    ]
    links = 6 * (x + y + z + c) + dp + vocab
    scratch += [dma((links,)), dma((links,))]
    return pl.pallas_call(
        functools.partial(backward_kernel, sizes),
        out_shape=[jax.ShapeDtypeStruct(tail, f32) for tail in tails]
        + [jax.ShapeDtypeStruct((16, 1024), f32), jax.ShapeDtypeStruct((8, 128), f32)],
        in_specs=[vmem] * 3 + [anywhere] * 13,
        out_specs=[vmem] * 6,
        scratch_shapes=scratch,
        compiler_params=pltpu.CompilerParams(
            collective_id=2, has_side_effects=True, vmem_limit_bytes=62 * 2**20
        ),
    )(grad_decoded, norms, extra, *[held[name] for name in names], *saved)


def attend_back(grad_low, queries, key_rows, values, probs, scale):
    grad_heads = split_heads(grad_low)
    grad_probs = jnp.einsum(
        "bqhd,bkhd->bhqk", grad_heads, split_heads(values), preferred_element_type=jnp.float32
    )
    grad_values = jnp.einsum("bhqk,bqhd->bkhd", probs, grad_heads, preferred_element_type=jnp.float32)
    probs = wide(probs)
    grad_scores = low(probs * (grad_probs - jnp.sum(probs * grad_probs, -1, keepdims=True)))
    grad_queries = (
        jnp.einsum("bhqk,bkhd->bqhd", grad_scores, split_heads(key_rows), preferred_element_type=jnp.float32)
        * scale
    )
    grad_keys = (
        jnp.einsum("bhqk,bqhd->bkhd", grad_scores, split_heads(queries), preferred_element_type=jnp.float32)
        * scale
    )
    return tuple(value.reshape(ROWS, -1) for value in (grad_queries, grad_keys, grad_values))


def split_heads(value):
    return value.reshape(MICRO, LEN, HEADS, value.shape[1] // HEADS)


def norm_back(grad_out, normed, inv_std, norm_gain):
    scaled = grad_out * norm_gain
    grad_in = inv_std * (
        scaled
        - jnp.mean(scaled, -1, keepdims=True)
        - normed * jnp.mean(scaled * normed, -1, keepdims=True)
    )
    return grad_in, jnp.sum(grad_out * normed, 0), jnp.sum(grad_out, 0)


def backward(grad_decoded, held, norms, saved):
    qkv_all, probs_all, normed_all, inv_all, feed_in, slopes, bottles = saved
    gains, biases = [None] * 7, [None] * 7

    def norm(grad, which):
        grad, gains[which], biases[which] = norm_back(grad, normed_all[which], inv_all[which, :, :1], norms[which])
        return grad

    def feed(grad, side, which):
        grad_sum = norm(grad, which)
        low_grad = low(grad_sum)
        grad_hidden = low(dot_rows(low_grad, held["narrow"][side]) * wide(slopes[side]))
        grad_bottle = low(BRANCH_SCALE * dot_rows(low_grad, held["up"][side]) * wide(bottles[side, 1]))
        grad_in = grad_sum + dot_rows(grad_hidden, held["widen"][side]) + dot_rows(grad_bottle, held["down"][side])
        grad_up = BRANCH_SCALE * dot_columns(bottles[side, 0], low_grad)
        return grad_in, dot_columns(feed_in[side], grad_bottle), grad_up

    def attend(grad, layer, which):
        grad_sum = norm(grad, which)
        grad_att = low(dot_rows(low(grad_sum), held["attn_out"][layer]))
        qkv = qkv_all[layer]
        probs = probs_all[layer].reshape(MICRO, HEADS, LEN, LEN)
        parts = attend_back(grad_att, qkv[:, :1024], qkv[:, 1024:2048], qkv[:, 2048:], probs, 0.125)
        packed = low(jnp.concatenate(parts, 1))
        w_in = held["attn_in"][layer]
        if layer == 2:
            return grad_sum + dot_rows(packed[:, :1024], w_in[:, :1024]), dot_rows(packed[:, 1024:], w_in[:, 1024:])
        return grad_sum + dot_rows(packed, w_in), None

    grad, down_dec, up_dec = feed(grad_decoded, 1, 6)
    grad, grad_memory = attend(grad, 2, 5)
    grad, _ = attend(grad, 1, 4)
    norm(grad, 3)
    grad, down_enc, up_enc = feed(grad_memory, 0, 2)
    grad, _ = attend(grad, 0, 1)
    norm(grad, 0)
    return down_enc, up_enc, down_dec, up_dec, jnp.stack(gains + biases)


def adam_step(weight, first, second, grad, rate):
    first = BETA_FIRST * first + (1.0 - BETA_FIRST) * grad
    second = BETA_SECOND * second + (1.0 - BETA_SECOND) * grad * grad
    first_hat = first / (1.0 - BETA_FIRST**STEP)
    second_hat = second / (1.0 - BETA_SECOND**STEP)
    weight = weight - rate * (
        first_hat / (jnp.sqrt(second_hat) + ADAM_EPSILON) + WEIGHT_DECAY * weight
    )
    return (first, second, weight)


def head(decoded, vocab_table, target_ids, target_length, seq_scale, groups, vocab_rank):
    rows_local = vocab_table.shape[0]
    key_index = jnp.arange(LEN)
    head_rows = lax.all_gather(decoded, "vocab", axis=0, tiled=True)
    logits = dot_rows(head_rows, vocab_table)
    local_target = target_ids.reshape(-1) - vocab_rank * rows_local
    target_hot = lax.broadcasted_iota(jnp.int32, logits.shape, 1) == local_target[:, None]
    target_logit = jnp.sum(jnp.where(target_hot, logits, 0.0), 1)
    local_max = jnp.max(logits, 1)
    row_max = lax.pmax(local_max, "vocab")
    row_total, row_target = lax.psum(
        (jnp.sum(jnp.exp(logits - row_max[:, None]), 1), target_logit), "vocab"
    )
    log_total = row_max + jnp.log(row_total)
    row_mask = (key_index[None, :] < target_length[:, None]).astype(jnp.float32)
    row_weight = (row_mask * seq_scale[:, None]).reshape(-1)
    row_loss = (log_total - row_target).reshape(-1, LEN) * row_mask
    own_loss = lax.dynamic_slice_in_dim(row_loss, vocab_rank * MICRO, MICRO)
    grad_logits = low(
        row_weight[:, None] * (jnp.exp(logits - log_total[:, None]) - target_hot.astype(jnp.float32))
    )
    grad_decoded = lax.psum_scatter(
        dot(grad_logits, vocab_table).astype(jnp.bfloat16), "vocab", scatter_dimension=0, tiled=True
    ).astype(jnp.float32)
    return grad_decoded, jnp.sum(own_loss, 1)


def local(
    source_ids,
    target_in,
    target_ids,
    source_length,
    target_length,
    task_ids,
    vocab_table,
    positions,
    attention_in,
    attention_out,
    widen_weight,
    narrow_weight,
    adapt_down,
    adapt_up,
    norm_params,
    down_first,
    down_second,
    up_first,
    up_second,
    norm_first,
    norm_second,
):
    dp, groups = lax.axis_size("dp"), lax.axis_size("vocab")
    vocab_rank = lax.axis_index("vocab")
    rows_local, width = vocab_table.shape
    joined_ids = jnp.stack([source_ids.reshape(groups, -1), target_in.reshape(groups, -1)], 1)
    local_ids = jnp.clip(joined_ids.reshape(-1) - vocab_rank * rows_local, 0, rows_local - 1)
    picked = jnp.take(vocab_table, local_ids, axis=0, mode="clip").reshape(groups // 2, 2, 2, ROWS, width)
    core = vocab_rank % 2
    owner = lax.dynamic_index_in_dim(
        joined_ids.reshape(groups // 2, 2, 2, ROWS) // rows_local, core, 1, keepdims=False
    ).transpose(1, 0, 2)
    twins = jnp.stack([vocab_rank, vocab_rank + 1 - 2 * core])
    owned = (owner[None] == twins[:, None, None, None]).astype(jnp.bfloat16)
    owned = jnp.broadcast_to(owned[..., None], owned.shape + (128,))
    task_hot = (task_ids[:, None] == jnp.arange(TASKS)[None, :]).astype(jnp.float32)
    group_counts = jnp.sum(task_hot * target_length[:, None].astype(jnp.float32), 0)
    own = vocab_rank * MICRO
    source_count = lax.dynamic_slice_in_dim(source_length, own, MICRO)
    key_keep = jnp.broadcast_to(
        (jnp.arange(LEN)[None, None, :] < source_count[:, None, None]).astype(jnp.float32), (MICRO, 8, LEN)
    )
    parts = {
        "norms": jnp.concatenate(
            [
                norm_params.T,
                jnp.pad(group_counts, (0, norm_params.shape[1] - TASKS))[:, None],
                jnp.zeros((norm_params.shape[1], 113), jnp.float32),
            ],
            1,
        )[None],
        "attn_in": attention_in,
        "attn_out": attention_out,
        "widen": widen_weight,
        "narrow": narrow_weight,
        "down": low(adapt_down),
        "up": low(adapt_up),
    }
    held, saved = run_forward(parts, picked, positions, key_keep, owned, dp, groups)
    slab = held.pop("norms").reshape(dp, groups, -1, 128)
    task_counts = jnp.sum(slab[:, 0, :TASKS, 14], 0)
    seq_scale = jnp.sum(task_hot * (1.0 / (TASKS * task_counts))[None, :], 1)
    norms = slab.reshape(width, 128)[:, :16].T
    if groups <= 4 and rows_local % TILE == 0:
        own_length = lax.dynamic_slice_in_dim(target_length, own, MICRO)
        own_mask = (jnp.arange(LEN)[None, :] < own_length[:, None]).astype(jnp.float32)
        own_weight = own_mask * lax.dynamic_slice_in_dim(seq_scale, own, MICRO)[:, None]
        grad_decoded, row_loss = run_head(saved[7], target_ids, own_weight, vocab_table, dp, groups)
        own_loss = jnp.sum(row_loss[0].reshape(MICRO, LEN) * own_mask, 1)
    else:
        grad_decoded, own_loss = head(
            saved[7], vocab_table, target_ids, target_length, seq_scale, groups, vocab_rank
        )
    task_local = jnp.sum(lax.dynamic_slice_in_dim(task_hot, own, MICRO) * own_loss[:, None], 0)
    task_row = jnp.pad(task_local[None], ((0, 1), (0, width - TASKS)))
    if groups <= 4:
        extra = jnp.pad(task_row, ((14, 0), (0, 0)))
        down_enc, up_enc, down_dec, up_dec, small, square = run_backward(
            grad_decoded, norms, extra, held, saved[:7], dp, groups
        )
    else:
        held = {name: value.reshape(value.shape[0], -1, value.shape[-1]) for name, value in held.items()}
        down_enc, up_enc, down_dec, up_dec, norm_grads = backward(grad_decoded, held, norms, saved[:7])
        small = jnp.concatenate([norm_grads, task_row], 0)
        down_enc, up_enc, down_dec, up_dec, small, square = reduce_gradients(
            down_enc, up_enc, down_dec, up_dec, small, dp, groups
        )
    shard_down = jnp.stack([down_enc, down_dec])
    shard_up = jnp.stack([up_enc, up_dec])
    full_norm, task_sums = small[:14], small[14, :TASKS]
    cut = norm_params.shape[1]
    shard_norm = lax.dynamic_slice_in_dim(full_norm, lax.axis_index(("dp", "vocab")) * cut, cut, 1)
    grad_norm = jnp.sqrt(square[0, 0])
    factor = CLIP_LIMIT / jnp.maximum(grad_norm, CLIP_LIMIT)
    down_new = adam_step(adapt_down, down_first, down_second, shard_down * factor, RATE_ADAPTER)
    up_new = adam_step(adapt_up, up_first, up_second, shard_up * factor, RATE_ADAPTER)
    norm_new = adam_step(norm_params, norm_first, norm_second, shard_norm * factor, RATE_NORMS)
    return (*down_new, *up_new, *norm_new, grad_norm, task_sums, task_counts)


def solution(mesh):
    return jax.shard_map(
        local,
        mesh=mesh,
        in_specs=(
            P("dp", None),
            P("dp", None),
            P("dp", None),
            P("dp"),
            P("dp"),
            P("dp"),
            P("vocab", None),
            P(),
            P(None, ("dp", "vocab"), None),
            P(None, ("dp", "vocab"), None),
            P(None, ("dp", "vocab"), None),
            P(None, ("dp", "vocab"), None),
            P(None, ("dp", "vocab"), None),
            P(None, ("dp", "vocab"), None),
            P(None, ("dp", "vocab")),
            P(None, ("dp", "vocab"), None),
            P(None, ("dp", "vocab"), None),
            P(None, ("dp", "vocab"), None),
            P(None, ("dp", "vocab"), None),
            P(None, ("dp", "vocab")),
            P(None, ("dp", "vocab")),
        ),
        out_specs=(
            P(None, ("dp", "vocab"), None),
            P(None, ("dp", "vocab"), None),
            P(None, ("dp", "vocab"), None),
            P(None, ("dp", "vocab"), None),
            P(None, ("dp", "vocab"), None),
            P(None, ("dp", "vocab"), None),
            P(None, ("dp", "vocab")),
            P(None, ("dp", "vocab")),
            P(None, ("dp", "vocab")),
            P(),
            P(),
            P(),
        ),
        check_vma=False,
    )
```
